32 devices in a mesh: dp: 16 (over z, y, x), ctx: 2 (over core).
Axes of the slice: x: 2, y: 2, z: 4, core: 2. Of those that a mesh axis runs over, the one named last changes fastest.
Arguments:
- tokens: bfloat16 [32, 1024, 1472], P('dp', 'ctx'), may hold values from -6 to 6
- lengths: int32 [32], P('dp'), may hold values from 2 to 1024, as said below
- qkv_weight: bfloat16 [1472, 1152], P(None, ('dp', 'ctx')), may hold values from -0.078125 to 0.078125
- out_weight: bfloat16 [384, 1472], P(('dp', 'ctx')), may hold values from -2 to 2
- gate_weight: bfloat16 [1472, 3584], P(None, ('dp', 'ctx')), may hold values from -0.15625 to 0.15625
- up_weight: bfloat16 [1472, 3584], P(None, ('dp', 'ctx')), may hold values from -0.15625 to 0.15625
- down_weight: bfloat16 [3584, 1472], P(('dp', 'ctx')), may hold values from -0.09375 to 0.09375
- norm_gains: float32 [3, 1472], P(None, 'dp'), may hold values from 0.25 to 1.75
- delete_weight: bfloat16 [1472], P('dp'), may hold values from -0.15625 to 0.15625
- bias_table: float32 [32, 6], replicated, may hold values from -4 to 4
- out_grad: bfloat16 [32, 1024, 1472], P('dp', 'ctx'), may hold values from -6 to 6
- gate_grad: float32 [32, 1024], P('dp', 'ctx'), may hold values from -24 to 24
Outputs:
- block_out: float32 [32, 1024, 1472], P('dp', 'ctx')
- gate_values: float32 [32, 1024], P('dp', 'ctx')
- tokens_grad: float32 [32, 1024, 1472], P('dp', 'ctx')
- qkv_weight_grad: float32 [1472, 1152], P(None, ('dp', 'ctx'))
- out_weight_grad: float32 [384, 1472], P(('dp', 'ctx'))
- gate_weight_grad: float32 [1472, 3584], P(None, ('dp', 'ctx'))
- up_weight_grad: float32 [1472, 3584], P(None, ('dp', 'ctx'))
- down_weight_grad: float32 [3584, 1472], P(('dp', 'ctx'))
- norm_gains_grad: float32 [3, 1472], P(None, 'dp')
- delete_weight_grad: float32 [1472], P('dp')
- bias_table_grad: float32 [32, 6], replicated
The draws below stay inside these ranges and needn't reach their ends.
Inputs may be any that keep to these rules, and one draw needn't show every extreme that they name: `lengths`: in each index of dp one of its 2 sequences, drawn from the seed, has length 1024.
All inputs are finite; a program needn't handle non-finite values.
Results may differ from the reference program's by a relative error of at most 0.017.
The reference program's roundings to bfloat16 on the way count: a program that leaves them out, or rounds other values in their place, can miss the bound.
Values may be sent and summed in bfloat16 or wider, within the bound.
A program may use at most 384 MiB of HBM per device.

```python
import jax
import jax.numpy as jnp
from jax import lax

D = 1472
FF = 3584
HEADS = 6
HDIM = 64
BUCKETS = 32
LEN = 1024
SEQS_DEV = 2
SEQS = 32


def draw_lengths(key, part):
    key = jax.random.fold_in(key, 7)
    key_one, key_two, key_three = jax.random.split(key, 3)
    factor_one = jax.random.randint(key_one, (SEQS,), 0, LEN)
    factor_two = jax.random.randint(key_two, (SEQS,), 0, LEN)
    ragged = LEN - factor_one * factor_two // LEN
    chosen = jax.random.randint(key_three, (SEQS // SEQS_DEV, 1), 0, SEQS_DEV)
    longest = (jnp.arange(SEQS_DEV)[None, :] == chosen).reshape(SEQS)
    return jnp.where(longest, LEN, ragged).astype(jnp.int32)


def level_of(rng, dims, cuts, low, largest):
    def one(axis_at, parts):
        steps = jax.random.uniform(jax.random.fold_in(jax.random.fold_in(rng, 6), axis_at), (parts,), jnp.float32, low / len(cuts), largest / len(cuts))
        return jnp.repeat(jnp.exp(steps), dims[axis_at] // parts).reshape((-1,) + (1,) * (len(dims) - axis_at - 1))

    level = one(*cuts[0])
    for cut in cuts[1:]:
        level = level * one(*cut)
    return level


def gaussian(key, dims, deviation, limit, shards=(), kind=jnp.bfloat16):
    array = jax.random.normal(key, dims, jnp.float32) * deviation
    if len(shards) > 0:
        array = level_of(key, dims, shards, -0.22, 0.18) * array
    return jnp.clip(array, min=-limit, max=limit).astype(kind)


def setup_inputs(seed: int = 0) -> dict:
    arg_keys = jax.random.split(jax.random.key(seed), 13)
    return {
        "tokens": gaussian(arg_keys[0], (SEQS, LEN, D), 1.0, 6.0, ((0, 16), (1, 2))),
        "lengths": draw_lengths(jax.random.fold_in(arg_keys[12], 71), 0),
        "qkv_weight": gaussian(arg_keys[2], (D, 3 * HEADS * HDIM), (4 * D) ** -0.5, 0.078125, ((1, 32),)),
        "out_weight": gaussian(arg_keys[3], (HEADS * HDIM, D), 8 ** -0.5, 2.0, ((0, 32),)),
        "gate_weight": gaussian(arg_keys[4], (D, FF), D ** -0.5, 0.15625, ((1, 32),)),
        "up_weight": gaussian(arg_keys[5], (D, FF), D ** -0.5, 0.15625, ((1, 32),)),
        "down_weight": gaussian(arg_keys[6], (FF, D), FF ** -0.5, 0.09375, ((0, 32),)),
        "norm_gains": jnp.clip(1.0 + 0.15 * jax.random.normal(arg_keys[7], (3, D), jnp.float32), 0.25, 1.75),
        "delete_weight": gaussian(arg_keys[8], (D,), D ** -0.5, 0.15625, ((0, 16),)),
        "bias_table": gaussian(arg_keys[9], (BUCKETS, HEADS), 1.0, 4.0, (), jnp.float32),
        "out_grad": gaussian(arg_keys[10], (SEQS, LEN, D), 1.0, 6.0, ((0, 16), (1, 2))),
        "gate_grad": gaussian(arg_keys[11], (SEQS, LEN), 4.0, 24.0, ((0, 16), (1, 2)), jnp.float32),
    }


@jax.custom_vjp
def low(v):
    return lax.optimization_barrier(v.astype(jnp.bfloat16)).astype(jnp.float32)

@jax.custom_vjp
def low_back(v):
    return v

def low_keep(v):
    return (low(v), None)

def low_pass(kept, grad):
    return (grad,)

def back_keep(v):
    return (v, None)

def back_low(kept, grad):
    return (low(grad),)
low.defvjp(low_keep, low_pass)
low_back.defvjp(back_keep, back_low)
norm_eps = 1e-06
masked_score = -1e+30
delete_scale = -30.0
bucket_edges = (12, 16, 23, 32, 46, 64, 91)

def bucket_of(offset):
    distance = jnp.abs(offset)
    far_bucket = 8 + sum(((distance >= boundary).astype(jnp.int32) for boundary in bucket_edges))
    near_bucket = jnp.where(distance < 8, distance, jnp.minimum(far_bucket, 15))
    return (near_bucket + jnp.where(offset > 0, 16, 0)).astype(jnp.int32)

def matmul_high(left, right):
    return jnp.dot(left, right, precision=lax.Precision.HIGHEST)

def rms_norm(values, gain_row):
    return values * lax.rsqrt(lax.optimization_barrier(jnp.mean(values * values, axis=-1, keepdims=True)) + norm_eps) * gain_row

def layer_one(weights, inputs, length):
    qkv_w, out_w, gate_w, up_w, down_w, gain_rows, delete_w, table = weights
    key_count = inputs.shape[0]
    inner_width = out_w.shape[0]
    head_count = table.shape[1]
    head_dim = inner_width // head_count
    low1 = low(rms_norm(inputs, gain_rows[0]))
    projected = low(low_back(matmul_high(low1, qkv_w)))
    queries = projected[:, :inner_width].reshape(key_count, head_count, head_dim)
    key_rows = projected[:, inner_width:2 * inner_width].reshape(key_count, head_count, head_dim)
    values = projected[:, 2 * inner_width:].reshape(key_count, head_count, head_dim)
    positions = jnp.arange(key_count, dtype=jnp.int32)
    buckets = bucket_of(positions[None, :] - positions[:, None])
    bias = jnp.transpose(table[buckets], (2, 0, 1))
    scores = jnp.einsum('ihd,jhd->hij', queries, key_rows, precision=lax.Precision.HIGHEST) + bias
    scores = low_back(scores)
    scores = jnp.where((positions < length)[None, None, :], scores, masked_score)
    row_max = lax.optimization_barrier(jnp.max(scores, axis=-1, keepdims=True))
    exponent = jnp.exp(scores - row_max)
    attn_probs = exponent / lax.optimization_barrier(jnp.sum(exponent, axis=-1, keepdims=True))
    attended = jnp.einsum('hij,jhd->ihd', low(attn_probs), values, precision=lax.Precision.HIGHEST)
    attended = low(low_back(attended.reshape(key_count, inner_width)))
    after_attn = inputs + low_back(matmul_high(attended, out_w))
    low2 = low(rms_norm(after_attn, gain_rows[1]))
    gate_pre = low_back(matmul_high(low2, gate_w))
    up_pre = low_back(matmul_high(low2, up_w))
    hidden = low(jax.nn.gelu(gate_pre, approximate=True) * up_pre)
    block_out = after_attn + low_back(matmul_high(hidden, down_w))
    low3 = low(rms_norm(block_out, gain_rows[2]))
    delete_logit = low_back(matmul_high(low3, delete_w))
    return (block_out, delete_scale * jax.nn.sigmoid(delete_logit))

def reference(tokens, lengths, qkv_weight, out_weight, gate_weight, up_weight, down_weight, norm_gains, delete_weight, bias_table, out_grad, gate_grad):
    inputs = tokens.astype(jnp.float32)
    weights = (qkv_weight.astype(jnp.float32), out_weight.astype(jnp.float32), gate_weight.astype(jnp.float32), up_weight.astype(jnp.float32), down_weight.astype(jnp.float32), norm_gains.astype(jnp.float32), delete_weight.astype(jnp.float32), bias_table.astype(jnp.float32))

    def forward(all_inputs, all_weights):
        stepper = jax.checkpoint(layer_one)

        def one_item(items):
            return stepper(all_weights, items[0], items[1])
        return lax.map(one_item, (all_inputs, lengths))
    (block_out, gate_values), pull_back = jax.vjp(forward, inputs, weights)
    grad_inputs, grad_weights = pull_back((out_grad.astype(jnp.float32), gate_grad.astype(jnp.float32)))
    return (block_out, gate_values, grad_inputs, grad_weights[0], grad_weights[1], grad_weights[2], grad_weights[3], grad_weights[4], grad_weights[5], grad_weights[6], grad_weights[7])
```

```python
import functools

import jax
import jax.numpy as jnp
from jax import lax
from jax.experimental import pallas as pl
from jax.experimental.pallas import tpu as pltpu
from jax.sharding import PartitionSpec as P

norm_eps = 1e-06
masked_score = -1e30
delete_scale = -30.0
bucket_edges = (12, 16, 23, 32, 46, 64, 91)
f32 = jnp.float32
bf16 = jnp.bfloat16
strip_rows = 128


def bucket_of(offset):
    distance = jnp.abs(offset)
    far_bucket = 8 + sum(((distance >= boundary).astype(jnp.int32) for boundary in bucket_edges))
    near_bucket = jnp.where(distance < 8, distance, jnp.minimum(far_bucket, 15))
    return near_bucket + jnp.where(offset > 0, 16, 0)


def dot_nt(left, right):
    return lax.dot_general(left, right, (((1,), (1,)), ((), ())), preferred_element_type=f32)


def dot_nn(left, right):
    return lax.dot_general(left, right, (((1,), (0,)), ((), ())), preferred_element_type=f32)


def dot_tn(left, right):
    return lax.dot_general(left, right, (((0,), (0,)), ((), ())), preferred_element_type=f32)


def swap_ctx(block):
    return lax.ppermute(block, "ctx", [(0, 1), (1, 0)])


def head_lanes(block, head, width):
    lane = lax.broadcasted_iota(jnp.int32, block.shape, 1)
    return jnp.where(lane // width == head, block, jnp.zeros_like(block))


def fold_rows(block, op):
    return op(block.reshape(block.shape[0] // 8, 8, block.shape[1]), axis=0)


def score_block(valid_ref, seq, key_ref, query, strip_ref, head, half, at, rows):
    start = half * strip_ref.shape[2] // 2 + rows - strip_rows - at
    scores = dot_nt(key_ref[pl.ds(at, strip_rows), :], query) + strip_ref[head, :, pl.ds(start, rows)]
    place = at + lax.broadcasted_iota(jnp.int32, scores.shape, 0)
    return jnp.where(place < valid_ref[seq, half], scores, masked_score)


def attend_kernel(
    valid_ref, q_ref, k_own, v_own, k_far, v_far, strip_ref, mixed_ref, stat_ref, work, probs
):
    seq = pl.program_id(1)
    rows = q_ref.shape[0]
    width = q_ref.shape[1] // 2
    outs = []
    stat_ref[...] = jnp.zeros_like(stat_ref)
    for head in range(2):
        query = head_lanes(q_ref[...], head, width)
        top = jnp.full((8, rows), masked_score, f32)
        for half, key_ref in enumerate((k_own, k_far)):
            for at in range(0, rows, strip_rows):
                scores = score_block(valid_ref, seq, key_ref, query, strip_ref, head, half, at, rows)
                work[pl.ds(half * rows + at, strip_rows), :] = scores
                top = jnp.maximum(top, fold_rows(scores, jnp.max))
        row_max = jnp.max(top, axis=0, keepdims=True)
        total = jnp.zeros((8, rows), f32)
        for at in range(0, 2 * rows, strip_rows):
            exponent = jnp.exp(work[pl.ds(at, strip_rows), :] - row_max)
            work[pl.ds(at, strip_rows), :] = exponent
            total = total + fold_rows(exponent, jnp.sum)
        row_sum = jnp.sum(total, axis=0, keepdims=True)
        share = 1.0 / row_sum
        for at in range(0, 2 * rows, strip_rows):
            probs[pl.ds(at, strip_rows), :] = (work[pl.ds(at, strip_rows), :] * share).astype(bf16)
        stat_ref[0, 0, pl.ds(head, 1), :] = row_max + jnp.log(row_sum)
        mixed = dot_tn(v_own[...], probs[pl.ds(0, rows), :]) + dot_tn(
            v_far[...], probs[pl.ds(rows, rows), :]
        )
        outs.append(mixed[head * width : (head + 1) * width, :])
    mixed_ref[...] = jnp.concatenate(outs, axis=0).T.astype(bf16)


def attend_back_kernel(
    valid_ref,
    q_ref,
    k_own,
    v_own,
    k_far,
    v_far,
    strip_ref,
    stat_ref,
    g_ref,
    gq_ref,
    gkv_own,
    gkv_far,
    diag_ref,
    probs,
    slopes,
    low,
    strip_sum,
):
    seq = pl.program_id(1)
    rows = q_ref.shape[0]
    width = q_ref.shape[1] // 2

    @pl.when(seq == 0)
    def _():
        strip_sum[...] = jnp.zeros_like(strip_sum)

    outs = []
    for head in range(2):
        query = head_lanes(q_ref[...], head, width)
        grad = head_lanes(g_ref[...], head, width)
        log_total = stat_ref[0, 0, pl.ds(head, 1), :]
        drift = jnp.zeros((8, rows), f32)
        for half, (key_ref, value_ref) in enumerate(((k_own, v_own), (k_far, v_far))):
            for at in range(0, rows, strip_rows):
                place = pl.ds(half * rows + at, strip_rows)
                scores = score_block(valid_ref, seq, key_ref, query, strip_ref, head, half, at, rows)
                part = jnp.exp(scores - log_total)
                slope = dot_nt(value_ref[pl.ds(at, strip_rows), :], grad)
                probs[place, :] = part
                slopes[place, :] = slope
                drift = drift + fold_rows(part * slope, jnp.sum)
        drift = jnp.sum(drift, axis=0, keepdims=True)
        for half, out_ref in enumerate((gkv_own, gkv_far)):
            for at in range(0, rows, strip_rows):
                place = pl.ds(half * rows + at, strip_rows)
                part = probs[place, :]
                grad_scores = (part * (slopes[place, :] - drift)).astype(bf16)
                low[place, :] = grad_scores
                start = half * strip_ref.shape[2] // 2 + rows - strip_rows - at
                strip_sum[head, :, pl.ds(start, rows)] += grad_scores.astype(f32)
                to = pl.ds(at, strip_rows)
                grad_key = dot_nn(grad_scores, query)
                grad_value = dot_nn(part.astype(bf16), grad)
                if head == 0:
                    out_ref[0, to, :] = grad_key
                    out_ref[1, to, :] = grad_value
                else:
                    out_ref[0, to, :] += grad_key
                    out_ref[1, to, :] += grad_value
        grad_query = dot_tn(k_own[...], low[pl.ds(0, rows), :]) + dot_tn(
            k_far[...], low[pl.ds(rows, rows), :]
        )
        outs.append(grad_query[head * width : (head + 1) * width, :])
    gq_ref[...] = jnp.concatenate(outs, axis=0).T.astype(bf16)

    @pl.when(seq == pl.num_programs(1) - 1)
    def _():
        span = strip_ref.shape[2] // 2
        for head in range(2):
            for half in range(2):
                skew = strip_sum[head, :, pl.ds(half * span, span)]
                row = lax.broadcasted_iota(jnp.int32, skew.shape, 0)
                step = 1
                while step < strip_rows:
                    skew = jnp.where(row & step != 0, pltpu.roll(skew, span - step, 1), skew)
                    step = 2 * step
                diag_ref[head, :, pl.ds(half * span, span)] = fold_rows(skew, jnp.sum)


def cost(flops, moved, exps=0):
    return pl.CostEstimate(flops=flops, bytes_accessed=moved, transcendentals=exps)


def attend_specs(rows, width, heads):
    pairs = heads // 2
    at = lambda first: pl.BlockSpec((rows, 2 * width), lambda pair, seq: (seq, first + pair))
    strip = 2 * 2 * rows
    return pairs, [
        pl.BlockSpec(memory_space=pltpu.SMEM),
        at(0),
        at(pairs),
        at(2 * pairs),
        at(0),
        at(pairs),
        pl.BlockSpec((2, strip_rows, strip), lambda pair, seq: (pair, 0, 0)),
    ]


def attend(valid, projected, far_kv, strip, seqs, rows, width, heads):
    pairs, specs = attend_specs(rows, width, heads)
    return pl.pallas_call(
        attend_kernel,
        grid=(pairs, seqs),
        in_specs=specs,
        out_specs=[
            pl.BlockSpec((rows, 2 * width), lambda pair, seq: (seq, pair)),
            pl.BlockSpec((1, 1, 8, rows), lambda pair, seq: (pair, seq, 0, 0)),
        ],
        out_shape=[
            jax.ShapeDtypeStruct((seqs * rows, heads * width), bf16),
            jax.ShapeDtypeStruct((pairs, seqs, 8, rows), f32),
        ],
        scratch_shapes=[pltpu.VMEM((2 * rows, rows), f32), pltpu.VMEM((2 * rows, rows), bf16)],
        compiler_params=pltpu.CompilerParams(vmem_limit_bytes=48 * 2**20),
        cost_estimate=cost(16 * 2**30, 16 * 2**20, seqs * heads * 2 * rows * rows),
    )(valid, projected, projected, projected, far_kv, far_kv, strip)


def attend_back(valid, projected, far_kv, strip, stats, grad, seqs, rows, width, heads):
    pairs, specs = attend_specs(rows, width, heads)
    block = pl.BlockSpec((rows, 2 * width), lambda pair, seq: (seq, pair))
    pair_block = pl.BlockSpec((2, rows, 2 * width), lambda pair, seq: (0, seq, pair))
    return pl.pallas_call(
        attend_back_kernel,
        grid=(pairs, seqs),
        in_specs=specs + [pl.BlockSpec((1, 1, 8, rows), lambda pair, seq: (pair, seq, 0, 0)), block],
        out_specs=[
            block,
            pair_block,
            pair_block,
            pl.BlockSpec((2, 8, 4 * rows), lambda pair, seq: (pair, 0, 0)),
        ],
        out_shape=[
            jax.ShapeDtypeStruct((seqs * rows, heads * width), bf16),
            jax.ShapeDtypeStruct((2, seqs * rows, heads * width), f32),
            jax.ShapeDtypeStruct((2, seqs * rows, heads * width), f32),
            jax.ShapeDtypeStruct((heads, 8, 4 * rows), f32),
        ],
        scratch_shapes=[
            pltpu.VMEM((2 * rows, rows), f32),
            pltpu.VMEM((2 * rows, rows), f32),
            pltpu.VMEM((2 * rows, rows), bf16),
            pltpu.VMEM((2, strip_rows, 4 * rows), f32),
        ],
        compiler_params=pltpu.CompilerParams(vmem_limit_bytes=48 * 2**20),
        cost_estimate=cost(40 * 2**30, 32 * 2**20, seqs * heads * 2 * rows * rows),
    )(valid, projected, projected, projected, far_kv, far_kv, strip, stats, grad)


def flip(at, bits):
    bit = 1
    while bit <= bits:
        if bits & bit:
            at = at + bit - 2 * bit * (at // bit % 2)
        bit = 2 * bit
    return at


class Copies:
    def __init__(self, send, recv):
        self.send, self.recv, self.made, self.ctx = send, recv, [], lax.axis_index("ctx")
        self.dp = lax.axis_index("dp")

    def start(self, source, target, bits):
        where = {"dp": flip(self.dp, bits)} if bits else {"ctx": 1 - self.ctx}
        at = len(self.made)
        copy = pltpu.make_async_remote_copy(
            src_ref=source,
            dst_ref=target,
            send_sem=self.send.at[at],
            recv_sem=self.recv.at[at],
            device_id=where,
            device_id_type=pl.DeviceIdType.MESH,
        )
        copy.start()
        self.made.append(copy)
        return copy

    def finish(self):
        for copy in self.made:
            copy.wait_send()


def greet(count):
    barrier = pltpu.get_barrier_semaphore()
    dp, ctx = lax.axis_index("dp"), lax.axis_index("ctx")
    bits = [1, 2] + [4 * step for step in range(1, count // 4)]
    for at in bits:
        pl.semaphore_signal(
            barrier, inc=1, device_id={"dp": flip(dp, at)}, device_id_type=pl.DeviceIdType.MESH
        )
    pl.semaphore_signal(
        barrier, inc=1, device_id={"ctx": 1 - ctx}, device_id_type=pl.DeviceIdType.MESH
    )
    pl.semaphore_wait(barrier, len(bits) + 1)


def gather_kernel(
    count,
    small_in,
    mixed_in,
    gate_in,
    up_in,
    down_in,
    small_out,
    mixed_out,
    gate_out,
    up_out,
    down_out,
    send,
    recv,
    local,
):
    planes = count // 4
    part = planes // 2
    greet(count)
    copies = Copies(send, recv)
    dp, ctx = copies.dp, copies.ctx
    z, y, x = dp // 4, dp // 2 % 2, dp % 2
    near = pl.ds(z // part * part, part)
    away = pl.ds((1 - z // part) * part, part)
    here = [
        pltpu.make_async_copy(source, target, local.at[at])
        for at, (source, target) in enumerate(
            (
                (mixed_in, mixed_out.at[z, y, x, ctx]),
                (small_in, small_out.at[z, y, x]),
            )
            + tuple(
                (source, target.at[0, 0])
                for source, target in ((gate_in, gate_out), (up_in, up_out), (down_in, down_out))
            )
        )
    ]
    for copy in here:
        copy.start()

    small_waits = [
        copies.start(small_in, small_out.at[z, y, x], 4 * step) for step in range(1, planes)
    ]
    waits = [
        copies.start(mixed_in, mixed_out.at[z, y, x, ctx], 4 * step) for step in range(1, planes)
    ]

    def planes_of(source, target):
        found = []
        for step in range(1, planes):
            place = step if step < part else 4 * part + step - part
            found.append(copies.start(source, target.at[0, place], 4 * step))
        return found

    def first_turn(target):
        second = 4 * part
        return [
            copies.start(target.at[0, pl.ds(0, part)], target.at[0, pl.ds(part, part)], 2),
            copies.start(
                target.at[0, pl.ds(second, part)], target.at[0, pl.ds(second + part, part)], 1
            ),
        ]

    def second_turn(target):
        second = 4 * part
        return [
            copies.start(target.at[0, pl.ds(0, 2 * part)], target.at[0, pl.ds(2 * part, 2 * part)], 1),
            copies.start(
                target.at[0, pl.ds(second, 2 * part)],
                target.at[0, pl.ds(second + 2 * part, 2 * part)],
                2,
            ),
        ]

    def core_turn(target, late):
        return [
            copies.start(
                target.at[0, pl.ds(base + late, 2 * part)],
                target.at[1, pl.ds(base + late, 2 * part)],
                0,
            )
            for base in (0, 4 * part)
        ]

    def arrive(found):
        for copy in found:
            copy.wait_recv()

    matrices = ((gate_in, gate_out), (up_in, up_out), (down_in, down_out))
    plane_waits = [planes_of(*matrices[0])]
    for copy in here:
        copy.wait()
    arrive(small_waits)
    small_waits = [copies.start(small_out.at[:, y, x], small_out.at[:, y, x], 2)]
    arrive(waits)
    waits = [
        copies.start(mixed_out.at[near, y, x, ctx], mixed_out.at[near, y, x, ctx], 2),
        copies.start(mixed_out.at[away, y, x, ctx], mixed_out.at[away, y, x, ctx], 1),
    ]
    plane_waits.append(planes_of(*matrices[1]))
    arrive(small_waits)
    small_waits = [copies.start(small_out.at[:, :, x], small_out.at[:, :, x], 1)]
    arrive(waits)
    waits = [
        copies.start(mixed_out.at[near, :, x, ctx], mixed_out.at[near, :, x, ctx], 1),
        copies.start(mixed_out.at[away, y, :, ctx], mixed_out.at[away, y, :, ctx], 2),
    ]
    arrive(plane_waits[0])
    first = first_turn(matrices[0][1])
    plane_waits.append(planes_of(*matrices[2]))
    arrive(waits)
    waits = [copies.start(mixed_out.at[:, :, :, ctx], mixed_out.at[:, :, :, ctx], 0)]
    cores = []
    for at, (_, target) in enumerate(matrices):
        arrive(first)
        cores += core_turn(target, 0)
        second = second_turn(target)
        if at + 1 < len(matrices):
            arrive(plane_waits[at + 1])
            first = first_turn(matrices[at + 1][1])
        arrive(second)
        cores += core_turn(target, 2 * part)
    arrive(small_waits)
    arrive(waits)
    arrive(cores)
    copies.finish()


def gather(small_in, mixed_in, gate_t, up_t, down, count):
    planes = count // 4
    copies = 5 * (planes - 1) + 7 + 3 * 8
    any_space = pl.BlockSpec(memory_space=pl.ANY)
    wide = jax.ShapeDtypeStruct((2, count) + gate_t.shape, bf16)
    return pl.pallas_call(
        functools.partial(gather_kernel, count),
        in_specs=[any_space] * 5,
        out_specs=[any_space] * 5,
        out_shape=[
            jax.ShapeDtypeStruct((planes, 2, 2) + small_in.shape, f32),
            jax.ShapeDtypeStruct((planes, 2, 2, 2) + mixed_in.shape, bf16),
            wide,
            wide,
            wide,
        ],
        scratch_shapes=[
            pltpu.SemaphoreType.DMA((copies,)),
            pltpu.SemaphoreType.DMA((copies,)),
            pltpu.SemaphoreType.DMA((5,)),
        ],
        compiler_params=pltpu.CompilerParams(collective_id=0, has_side_effects=True),
    )(small_in, mixed_in, gate_t, up_t, down)


def butterfly(count):
    return [0] + [1 << at for at in range(count.bit_length() - 1)]


def reduce_kernel(
    count,
    mixed_in,
    small_in,
    gate_own,
    gate_far,
    up_own,
    up_far,
    down_own,
    down_far,
    mixed_out,
    small_out,
    gate_out,
    up_out,
    down_out,
    mixed_sum,
    gate_sum,
    up_sum,
    down_sum,
    mixed_one,
    gate_one,
    up_one,
    down_one,
    mixed_two,
    gate_two,
    up_two,
    down_two,
    mixed_last,
    gate_last,
    up_last,
    down_last,
    own,
    mixed_own,
    small,
    send,
    recv,
    local,
):
    planes = count // 4
    part = planes // 2
    greet(count)
    copies = Copies(send, recv)
    dp, ctx = copies.dp, copies.ctx
    turns = ((1, 2), (2, 1))

    def relative(half, at):
        far, near, plane = at // (2 * part), at // part % 2, at % part
        return turns[half][0] * far + turns[half][1] * near + 4 * (half * part + plane)

    matrices = (
        (down_own, down_far, down_sum, down_one, down_two, down_last, down_out),
        (gate_own, gate_far, gate_sum, gate_one, gate_two, gate_last, gate_out),
        (up_own, up_far, up_sum, up_one, up_two, up_last, up_out),
        (mixed_in, mixed_in, mixed_sum, mixed_one, mixed_two, mixed_last, mixed_out),
    )
    last = len(matrices) - 1
    arrivals = {}
    loads = {}

    def load(at, half):
        if at == last:
            loads[at, half] = []
            for piece in range(4 * part):
                copy = pltpu.make_async_copy(
                    mixed_in.at[flip(dp, relative(half, piece)), ctx],
                    mixed_own.at[half, piece],
                    local.at[2 + half * 4 * part + piece],
                )
                copy.start()
                loads[at, half].append(copy)
        else:
            copy = pltpu.make_async_copy(
                matrices[at][0].at[pl.ds(half * 4 * part, 4 * part)], own.at[half], local.at[half]
            )
            copy.start()
            loads[at, half] = [copy]

    for half in range(2):
        load(0, half)
    for at, matrix in enumerate(matrices):
        for half in range(2):
            if at == last:
                arrivals[at, half, 0] = [
                    copies.start(
                        mixed_in.at[flip(dp, relative(half, piece)), 1 - ctx],
                        mixed_sum.at[half, piece],
                        0,
                    )
                    for piece in range(4 * part)
                ]
            else:
                arrivals[at, half, 0] = [
                    copies.start(matrix[1].at[pl.ds(half * 4 * part, 4 * part)], matrix[2].at[half], 0)
                ]

    def add(target, half, size, other, place):
        @pl.loop(0, size)
        def _(piece):
            target[half, piece] = (
                target[half, piece].astype(f32) + other[place, piece].astype(f32)
            ).astype(bf16)

    rounds = butterfly(count)
    small_wait = None
    small[0] = small_in[...]
    for step in range(max(len(matrices) + 3, len(rounds) + 1)):
        for at in range(len(matrices)):
            own_ref, far_ref, total, one, two, final, out = matrices[at]
            stage = step - at
            for half in range(2):
                if stage == 0:
                    for copy in loads[at, half]:
                        copy.wait()
                    for copy in arrivals[at, half, 0]:
                        copy.wait_recv()
                    add(total, half, 4 * part, mixed_own if at == last else own, half)
                    if at < last:
                        load(at + 1, half)
                    arrivals[at, half, 1] = [
                        copies.start(
                            total.at[half, pl.ds(2 * part, 2 * part)], one.at[half], turns[half][0]
                        )
                    ]
                if stage == 1:
                    arrivals[at, half, 1][0].wait_recv()
                    add(total, half, 2 * part, one, half)
                    arrivals[at, half, 2] = [
                        copies.start(total.at[half, pl.ds(part, part)], two.at[half], turns[half][1])
                    ]
                if stage == 2:
                    arrivals[at, half, 2][0].wait_recv()
                    add(total, half, part, two, half)
                    arrivals[at, half, 3] = [
                        copies.start(
                            total.at[half, plane], final.at[half * part + plane - 1], 4 * (half * part + plane)
                        )
                        for plane in range(1 - half, part)
                    ]
                if stage == 3:
                    for copy in arrivals[at, half, 3]:
                        copy.wait_recv()
            if stage == 3:
                out[...] = total[0, 0].astype(f32)
                for plane in range(1, planes):
                    out[...] += final[plane - 1].astype(f32)
        if step > 0 and step <= len(rounds):
            small_wait.wait_recv()
            small[2 * step] = small[2 * step - 2] + small[2 * step - 1]
        if step < len(rounds):
            small_wait = copies.start(small.at[2 * step], small.at[2 * step + 1], rounds[step])
    small_out[...] = small[2 * len(rounds)]
    copies.finish()


def reduce(mixed, small, gate, up, down, count):
    planes = count // 4
    part = planes // 2
    rounds = len(butterfly(count))
    model = mixed.shape[-1]
    rows = (mixed.shape[-2],) + (gate[0].shape[-2],) * 3
    number = 6 + 4 * part * 2 + 4 * 4 + 4 * (planes - 1) + rounds
    any_space = pl.BlockSpec(memory_space=pl.ANY)
    vmem = pl.BlockSpec(memory_space=pltpu.VMEM)
    buffers = lambda size: [pltpu.VMEM((2, size, at, model), bf16) for at in rows]
    return pl.pallas_call(
        functools.partial(reduce_kernel, count),
        in_specs=[any_space, vmem] + [any_space] * 6,
        out_specs=[vmem] * 5,
        out_shape=[
            jax.ShapeDtypeStruct((rows[0], model), f32),
            jax.ShapeDtypeStruct(small.shape, f32),
        ]
        + [jax.ShapeDtypeStruct((rows[1], model), f32)] * 3,
        scratch_shapes=buffers(4 * part)
        + buffers(2 * part)
        + buffers(part)
        + [pltpu.VMEM((planes - 1, at, model), bf16) for at in rows]
        + [
            pltpu.VMEM((2, 4 * part, rows[1], model), bf16),
            pltpu.VMEM((2, 4 * part, rows[0], model), bf16),
            pltpu.VMEM((2 * rounds + 1,) + small.shape, f32),
            pltpu.SemaphoreType.DMA((number,)),
            pltpu.SemaphoreType.DMA((number,)),
            pltpu.SemaphoreType.DMA((2 + 8 * part,)),
        ],
        compiler_params=pltpu.CompilerParams(
            collective_id=1, has_side_effects=True, vmem_limit_bytes=60 * 2**20
        ),
    )(mixed, small, *gate, *up, *down)


def rms_norm(values, gain_row):
    inv_rms = lax.rsqrt(jnp.mean(values * values, axis=-1, keepdims=True) + norm_eps)
    return (values * inv_rms * gain_row, inv_rms)


def norm_back(values, inv_rms, gain_row, grad_out):
    scaled = grad_out * gain_row
    grad_in = inv_rms * scaled - values * inv_rms**3 * jnp.mean(
        values * scaled, axis=-1, keepdims=True
    )
    return (grad_in, jnp.sum(grad_out * values * inv_rms, axis=0))


def per_device(
    tokens,
    lengths,
    qkv_weight,
    out_weight,
    gate_weight,
    up_weight,
    down_weight,
    norm_gains,
    delete_weight,
    bias_table,
    out_grad,
    gate_grad,
):
    seqs, rows, model = tokens.shape
    total = seqs * rows
    ctx = lax.axis_index("ctx")
    dp_count = lax.axis_size("dp")
    heads = bias_table.shape[1]
    buckets = bias_table.shape[0]

    qkv_rows = qkv_weight.shape[1]
    shard = model // dp_count
    small = jnp.concatenate([norm_gains, delete_weight.astype(f32)[None]])
    small_all, attn_all, gate_all, up_all, down_all = gather(
        jnp.pad(small, ((0, 4), (0, -shard % 128))),
        jnp.concatenate([qkv_weight.T, out_weight]),
        gate_weight.T,
        up_weight.T,
        down_weight,
        dp_count,
    )
    small_all = small_all.reshape(dp_count, 8, -1)[:, :4, :shard]
    gains = small_all.transpose(1, 0, 2).reshape(4, model)
    delete_full = gains[3]
    delete_low = delete_full.astype(bf16)
    attn_all = attn_all.reshape(2 * dp_count, -1, model)
    qkv_t = attn_all[:, :qkv_rows].reshape(-1, model)
    out_full = attn_all[:, qkv_rows:].reshape(-1, model)
    inner = out_full.shape[0]
    width = inner // heads

    own, far = [
        [matrix[half].reshape(-1, model) for matrix in (gate_all, up_all, down_all)]
        for half in range(2)
    ]

    shift = rows * (1 - 2 * ctx)
    key_at = jnp.arange(strip_rows, dtype=jnp.int32)[:, None]
    lane_at = jnp.arange(2 * rows, dtype=jnp.int32)[None, :]
    offset = key_at - lane_at + (rows - strip_rows)
    offsets = jnp.concatenate([offset, offset + shift], axis=1)
    strip_bucket = bucket_of(offsets)
    strip = jnp.zeros((heads,) + strip_bucket.shape, f32)
    for bucket in range(buckets):
        strip = jnp.where(strip_bucket[None] == bucket, bias_table[bucket][:, None, None], strip)
    valid = jnp.stack([lengths - rows * ctx, lengths - rows * (1 - ctx)], axis=1)

    inputs = tokens.reshape(total, model).astype(f32)
    normed_in, scale_in = rms_norm(inputs, gains[0])
    low_in = normed_in.astype(bf16)
    projected = dot_nt(low_in, qkv_t).astype(bf16)
    far_kv = swap_ctx(projected[:, inner:])
    mixed, stats = attend(valid, projected, far_kv, strip, seqs, rows, width, heads)
    after_attn = inputs + dot_nn(mixed, out_full)
    normed_mid, scale_mid = rms_norm(after_attn, gains[1])
    low_mid = normed_mid.astype(bf16)
    block_out = after_attn
    kept = []
    for gate_t, up_t, down in (own, far):
        gate_pre = dot_nt(low_mid, gate_t)
        up_pre = dot_nt(low_mid, up_t)
        hidden = (jax.nn.gelu(gate_pre, approximate=True) * up_pre).astype(bf16)
        block_out = block_out + dot_nn(hidden, down)
        kept.append((gate_pre, up_pre, hidden))
    normed_out, scale_out = rms_norm(block_out, gains[2])
    low_out = normed_out.astype(bf16)
    delete_logit = jnp.dot(low_out, delete_low, preferred_element_type=f32)
    sigmoid_val = jax.nn.sigmoid(delete_logit)
    gate_values = delete_scale * sigmoid_val

    grad_logit = (
        gate_grad.reshape(total) * delete_scale * sigmoid_val * (1.0 - sigmoid_val)
    ).astype(bf16)
    grad_delete = jnp.dot(grad_logit, low_out, preferred_element_type=f32)
    grad_normed = grad_logit.astype(f32)[:, None] * delete_full[None, :]
    grad_from_out, grad_gain_out = norm_back(block_out, scale_out, gains[2], grad_normed)
    grad_block = out_grad.reshape(total, model).astype(f32) + grad_from_out
    grad_ff = grad_block.astype(bf16)

    grad_low_mid = 0.0
    terms = []
    for (gate_t, up_t, down), (gate_pre, up_pre, hidden) in zip((far, own), kept[::-1]):
        grad_hidden = dot_nt(grad_ff, down)
        _, pull = jax.vjp(
            lambda gate_in, up_in: jax.nn.gelu(gate_in, approximate=True) * up_in, gate_pre, up_pre
        )
        grad_gate, grad_up = pull(grad_hidden)
        grad_gate = grad_gate.astype(bf16)
        grad_up = grad_up.astype(bf16)
        terms.append(
            [
                dot_tn(grad_gate, low_mid).astype(bf16),
                dot_tn(grad_up, low_mid).astype(bf16),
                dot_tn(hidden, grad_ff).astype(bf16),
            ]
        )
        grad_low_mid = grad_low_mid + dot_nn(grad_gate, gate_t) + dot_nn(grad_up, up_t)
    grad_from_mid, grad_gain_mid = norm_back(after_attn, scale_mid, gains[1], grad_low_mid)
    grad_after = grad_block + grad_from_mid
    grad_attn = grad_after.astype(bf16)
    grad_mixed = dot_nt(grad_attn, out_full).astype(bf16)
    out_term = dot_tn(mixed, grad_attn).astype(bf16)
    grad_query, grad_own, grad_far, diagonals = attend_back(
        valid, projected, far_kv, strip, stats, grad_mixed, seqs, rows, width, heads
    )
    grad_kv = grad_own + swap_ctx(grad_far.astype(bf16)).astype(f32)
    grad_projected = jnp.concatenate(
        [grad_query, grad_kv[0].astype(bf16), grad_kv[1].astype(bf16)], axis=1
    )
    grad_low_in = dot_nn(grad_projected, qkv_t)
    grad_from_in, grad_gain_in = norm_back(inputs, scale_in, gains[0], grad_low_in)
    tokens_grad = grad_after + grad_from_in
    qkv_term = dot_tn(grad_projected, low_in).astype(bf16)

    span = 2 * rows
    place = jnp.arange(span, dtype=jnp.int32)
    diagonal = (rows - strip_rows) - jnp.where(place >= span - strip_rows, place - span, place)
    diagonal = jnp.concatenate([diagonal, diagonal + shift])
    one_hot = (bucket_of(diagonal)[:, None] == jnp.arange(buckets)[None, :]).astype(f32)
    grad_table = jnp.dot(
        one_hot.T, jnp.sum(diagonals, axis=1).T, precision=lax.Precision.HIGHEST
    )
    small_term = jnp.concatenate(
        [
            jnp.stack([grad_gain_in, grad_gain_mid, grad_gain_out, grad_delete]),
            jnp.pad(grad_table.reshape(1, -1), ((0, 3), (0, model - buckets * heads))),
        ]
    )
    mixed_term = jnp.concatenate(
        [
            qkv_term.reshape(dp_count, 2, qkv_rows, model),
            out_term.reshape(dp_count, 2, -1, model),
        ],
        axis=2,
    )
    pieces = [
        [term.reshape((dp_count,) + down_weight.shape) for term in (own_term, far_term)]
        for far_term, own_term in zip(*terms)
    ]
    mixed_sum, small_sum, gate_sum, up_sum, down_sum = reduce(
        mixed_term, small_term, *pieces, dp_count
    )
    anchor = lax.axis_index("dp") * shard
    return (
        block_out.reshape(seqs, rows, model),
        gate_values.reshape(seqs, rows),
        tokens_grad.reshape(seqs, rows, model),
        mixed_sum[:qkv_rows].T,
        mixed_sum[qkv_rows:],
        gate_sum.T,
        up_sum.T,
        down_sum,
        lax.dynamic_slice_in_dim(small_sum[:3], anchor, shard, 1),
        lax.dynamic_slice_in_dim(small_sum[3], anchor, shard, 0),
        small_sum[4, : buckets * heads].reshape(buckets, heads),
    )


def solution(mesh):
    wide = P("dp", "ctx", None)
    columns = P(None, ("dp", "ctx"))
    depth = P(("dp", "ctx"), None)
    return jax.shard_map(
        per_device,
        mesh=mesh,
        in_specs=(
            wide,
            P("dp"),
            columns,
            depth,
            columns,
            columns,
            depth,
            P(None, "dp"),
            P("dp"),
            P(),
            wide,
            P("dp", "ctx"),
        ),
        out_specs=(
            wide,
            P("dp", "ctx"),
            wide,
            columns,
            depth,
            columns,
            columns,
            depth,
            P(None, "dp"),
            P("dp"),
            P(),
        ),
        check_vma=False,
    )
```

```python
import functools

import jax
import jax.numpy as jnp
from jax import lax
from jax.experimental import pallas as pl
from jax.experimental.pallas import tpu as pltpu
from jax.sharding import PartitionSpec as P

norm_eps = 1e-06
masked_score = -1e30
delete_scale = -30.0
bucket_edges = (12, 16, 23, 32, 46, 64, 91)
f32 = jnp.float32
bf16 = jnp.bfloat16
strip_rows = 128


def bucket_of(offset):
    distance = jnp.abs(offset)
    far_bucket = 8 + sum(((distance >= boundary).astype(jnp.int32) for boundary in bucket_edges))
    near_bucket = jnp.where(distance < 8, distance, jnp.minimum(far_bucket, 15))
    return near_bucket + jnp.where(offset > 0, 16, 0)


def dot_nt(left, right):
    return lax.dot_general(left, right, (((1,), (1,)), ((), ())), preferred_element_type=f32)


def dot_nn(left, right):
    return lax.dot_general(left, right, (((1,), (0,)), ((), ())), preferred_element_type=f32)


def dot_tn(left, right):
    return lax.dot_general(left, right, (((0,), (0,)), ((), ())), preferred_element_type=f32)


def swap_ctx(block):
    return lax.ppermute(block, "ctx", [(0, 1), (1, 0)])


def head_lanes(block, head, width):
    lane = lax.broadcasted_iota(jnp.int32, block.shape, 1)
    return jnp.where(lane // width == head, block, jnp.zeros_like(block))


def fold_rows(block, op):
    return op(block.reshape(block.shape[0] // 8, 8, block.shape[1]), axis=0)


def flip(at, bits):
    bit = 1
    while bit <= bits:
        if bits & bit:
            at = at + bit - 2 * bit * (at // bit % 2)
        bit = 2 * bit
    return at


class Copies:
    def __init__(self, count, send, recv):
        self.send, self.recv, self.made, self.done = send, recv, [], set()
        self.dp, self.ctx = lax.axis_index("dp"), lax.axis_index("ctx")
        self.where = {0: {"ctx": 1 - self.ctx}}
        for bits in [1, 2] + [4 * step for step in range(1, count // 4)]:
            self.where[bits] = {"dp": flip(self.dp, bits)}

    def start(self, source, target, bits):
        at = len(self.made)
        copy = pltpu.make_async_remote_copy(
            src_ref=source,
            dst_ref=target,
            send_sem=self.send.at[at],
            recv_sem=self.recv.at[at],
            device_id=self.where[bits],
            device_id_type=pl.DeviceIdType.MESH,
        )
        copy.start()
        self.made.append(copy)
        return copy

    def sent(self, copy):
        if id(copy) not in self.done:
            copy.wait_send()
            self.done.add(id(copy))

    def finish(self):
        for copy in self.made:
            self.sent(copy)


def greet(count):
    barrier = pltpu.get_barrier_semaphore()
    dp, ctx = lax.axis_index("dp"), lax.axis_index("ctx")
    bits = [1, 2] + [4 * step for step in range(1, count // 4)]
    for at in bits:
        pl.semaphore_signal(
            barrier, inc=1, device_id={"dp": flip(dp, at)}, device_id_type=pl.DeviceIdType.MESH
        )
    pl.semaphore_signal(
        barrier, inc=1, device_id={"ctx": 1 - ctx}, device_id_type=pl.DeviceIdType.MESH
    )
    pl.semaphore_wait(barrier, len(bits) + 1)


def rows_of(total, size):
    return [pl.ds(at, size) for at in range(0, total, size)]


def strip_of(diagonal, span):
    wide = jnp.broadcast_to(diagonal, (strip_rows, span))
    return pltpu.roll(wide, 0, 1, stride=1, stride_axis=0)


def fill_strips(strips, diag_ref, pair, span):
    for head in range(2):
        for half in range(2):
            strips[head, :, pl.ds(half * span, span)] = strip_of(
                diag_ref[pl.ds(4 * pair + 2 * head + half, 1), :], span
            )


def score_block(valid_ref, seq, keys, query, strips, head, half, at, rows):
    start = half * strips.shape[2] // 2 + rows - strip_rows - at
    scores = dot_nt(keys, query) + strips[head, :, pl.ds(start, rows)]
    place = at + lax.broadcasted_iota(jnp.int32, scores.shape, 0)
    return jnp.where(place < valid_ref[seq, half], scores, masked_score)


def lanes(first):
    return pl.ds(first, strip_rows)


def attend_pair(valid_ref, seq, pair, projected, far, strips, mixed_ref, stat_ref, work, probs, rows, inner):
    width = strip_rows // 2
    seq_rows = pl.ds(pl.multiple_of(seq * rows, rows), rows)
    first = strip_rows * pair
    queries = projected[seq_rows, lanes(first)]
    outs = []
    for head in range(2):
        query = head_lanes(queries, head, width)
        top = jnp.full((8, rows), masked_score, f32)
        for half, (source, base) in enumerate(((projected, inner), (far, 0))):
            for at in range(0, rows, strip_rows):
                keys = source[pl.ds(pl.multiple_of(seq * rows + at, strip_rows), strip_rows), lanes(base + first)]
                scores = score_block(
                    valid_ref, seq, keys, query, strips, head, half, at, rows
                )
                work[pl.ds(half * rows + at, strip_rows), :] = scores
                top = jnp.maximum(top, fold_rows(scores, jnp.max))
        row_max = jnp.max(top, axis=0, keepdims=True)
        total = jnp.zeros((8, rows), f32)
        for at in range(0, 2 * rows, strip_rows):
            exponent = jnp.exp(work[pl.ds(at, strip_rows), :] - row_max)
            work[pl.ds(at, strip_rows), :] = exponent
            total = total + fold_rows(exponent, jnp.sum)
        row_sum = jnp.sum(total, axis=0, keepdims=True)
        share = 1.0 / row_sum
        for at in range(0, 2 * rows, strip_rows):
            probs[pl.ds(at, strip_rows), :] = (work[pl.ds(at, strip_rows), :] * share).astype(bf16)
        stat_ref[seq, pair, pl.ds(head, 1), :] = row_max + jnp.log(row_sum)
        mixed = dot_tn(
            projected[seq_rows, lanes(2 * inner + first)], probs[pl.ds(0, rows), :]
        ) + dot_tn(far[seq_rows, lanes(inner + first)], probs[pl.ds(rows, rows), :])
        outs.append(mixed[head * width : (head + 1) * width, :])
    mixed_ref[seq_rows, lanes(first)] = jnp.concatenate(outs, axis=0).T.astype(bf16)


def gelu_parts(value):
    inner = 0.7978845608028654 * (value + 0.044715 * value * value * value)
    slope = 0.7978845608028654 * (1.0 + 3.0 * 0.044715 * value * value)
    tanh = jnp.tanh(inner)
    half = 0.5 * (1.0 + tanh)
    return value * half, half + 0.5 * value * (1.0 - tanh * tanh) * slope


def front_kernel(
    count,
    qkv_rows,
    valid_ref,
    diag_ref,
    tokens_ref,
    small_in,
    mixed_in,
    gate_in,
    up_in,
    down_in,
    gate_all,
    up_all,
    down_all,
    low_in_out,
    projected_out,
    far_out,
    mixed_out,
    stat_out,
    after_out,
    low_mid_out,
    gains_out,
    qkv_out,
    proj_out,
    gate_pre_out,
    up_pre_out,
    hidden_out,
    block_out,
    small_all,
    mixed_all,
    low_in,
    projected,
    far,
    mixed,
    stat,
    total,
    low_mid,
    gains,
    qkv,
    proj,
    strips,
    probs,
    weights,
    gate_buf,
    up_buf,
    hidden,
    send,
    recv,
    local,
    flush,
    fetch,
    store,
):
    planes = count // 4
    part = planes // 2
    piece = gate_in.shape[0]
    model = tokens_ref.shape[1]
    row_total = tokens_ref.shape[0]
    seqs, pairs = stat.shape[:2]
    rows = row_total // seqs
    inner = proj.shape[0]
    group = gate_all.shape[2]
    shard = model // count
    greet(count)
    copies = Copies(count, send, recv)
    dp, ctx = copies.dp, copies.ctx
    z, y, x = dp // 4, dp // 2 % 2, dp % 2
    near = pl.ds(z // part * part, part)
    away = pl.ds((1 - z // part) * part, part)
    matrices = ((gate_in, gate_all), (up_in, up_all), (down_in, down_all))
    here = [
        pltpu.make_async_copy(source, target, local.at[at])
        for at, (source, target) in enumerate(
            (
                (mixed_in, mixed_all.at[z, y, x, ctx]),
                (small_in, small_all.at[z, y, x]),
            )
            + tuple((source, target.at[0, 0, pl.ds(0, piece)]) for source, target in matrices)
        )
    ]
    for copy in here:
        copy.start()
    flushed = []

    def put(source, target):
        copy = pltpu.make_async_copy(source, target, flush.at[len(flushed)])
        copy.start()
        flushed.append(copy)

    def arrive(found):
        for copy in found:
            copy.wait_recv()

    def planes_of(source, target):
        found = []
        for step in range(1, planes):
            place = pl.ds(step % part * piece, piece)
            found.append(copies.start(source, target.at[0, 2 * (step // part), place], 4 * step))
        return found

    def first_turn(target):
        low, high = pl.ds(0, part * piece), pl.ds(part * piece, part * piece)
        return [
            copies.start(target.at[0, at, low], target.at[0, at, high], bits)
            for at, bits in ((0, 2), (2, 1))
        ]

    def second_turn(target):
        return [
            copies.start(target.at[0, at], target.at[0, at + 1], bits)
            for at, bits in ((0, 1), (2, 2))
        ]

    def core_turn(target, late):
        return [
            copies.start(target.at[0, at + late], target.at[1, at + late], 0) for at in (0, 2)
        ]

    small_waits = [
        copies.start(small_in, small_all.at[z, y, x], 4 * step) for step in range(1, planes)
    ]
    waits = [
        copies.start(mixed_in, mixed_all.at[z, y, x, ctx], 4 * step) for step in range(1, planes)
    ]
    plane_waits = [planes_of(*matrix) for matrix in matrices]

    work = gate_buf.at[0, :, pl.ds(0, rows)]
    for copy in here:
        copy.wait()
    arrive(small_waits)
    small_turn = [copies.start(small_all.at[:, y, x], small_all.at[:, y, x], 2)]
    arrive(waits)
    turn = [
        copies.start(mixed_all.at[near, y, x, ctx], mixed_all.at[near, y, x, ctx], 2),
        copies.start(mixed_all.at[away, y, x, ctx], mixed_all.at[away, y, x, ctx], 1),
    ]
    arrive(small_turn)
    small_turn = [copies.start(small_all.at[:, :, x], small_all.at[:, :, x], 1)]
    arrive(turn)
    turn = [
        copies.start(mixed_all.at[near, :, x, ctx], mixed_all.at[near, :, x, ctx], 1),
        copies.start(mixed_all.at[away, y, :, ctx], mixed_all.at[away, y, :, ctx], 2),
    ]
    arrive(small_turn)
    padded = -(-model // 128) * 128
    lane = lax.broadcasted_iota(jnp.int32, (8, 128), 1)
    found = jnp.zeros((8, padded), f32)
    for at in range(count):
        block = jnp.where(lane < shard, small_all[at // 4, at // 2 % 2, at % 2], 0.0)
        block = jnp.concatenate([block, jnp.zeros((8, padded - 128), f32)], axis=1)
        found = found + (pltpu.roll(block, at * shard, 1) if at else block)
    gains[...] = found[:, :model]
    put(gains, gains_out)

    @pl.loop(0, row_total // strip_rows)
    def _(at):
        place = pl.ds(pl.multiple_of(at * strip_rows, strip_rows), strip_rows)
        value = tokens_ref[place, :].astype(f32)
        scale = lax.rsqrt(jnp.mean(value * value, axis=1, keepdims=True) + norm_eps)
        low_in[place, :] = (value * scale * gains[pl.ds(0, 1), :]).astype(bf16)

    put(low_in, low_in_out)
    arrive(turn)
    turn = [copies.start(mixed_all.at[:, :, :, ctx], mixed_all.at[:, :, :, ctx], 0)]
    arrive(plane_waits[0])
    first = first_turn(gate_all)
    arrive(turn)
    block_rows = mixed_in.shape[0]
    for target, begin, size in ((qkv, 0, qkv_rows), (proj, qkv_rows, inner // (2 * count))):
        batch = min(2 * count, row_total // size // 16 * 16)
        for base in range(0, 2 * count, batch):
            for at in range(base, min(base + batch, 2 * count)):
                block = mixed_all[at // 8, at // 4 % 2, at // 2 % 2, at % 2].astype(f32)
                total[pl.ds((at - base) * size, size), :] = block[begin : begin + size, :]
            number = min(batch, 2 * count - base) * size
            target[pl.ds(base * size, number), :] = total[pl.ds(0, number), :].astype(bf16)
    put(qkv, qkv_out)
    put(proj, proj_out)
    for place in rows_of(row_total, rows):
        for to in rows_of(3 * inner, inner):
            projected[place, to] = dot_nt(low_in[place, :], qkv[to, :]).astype(bf16)
    put(projected, projected_out)
    swap = [copies.start(projected.at[:, pl.ds(inner, 2 * inner)], far, 0)]
    arrive(first)
    cores = core_turn(gate_all, 0)
    second = second_turn(gate_all)
    arrive(swap)
    put(far, far_out)
    stat[...] = jnp.zeros_like(stat)
    for pair in range(pairs):
        fill_strips(strips, diag_ref, pair, 2 * rows)

        @pl.loop(0, seqs)
        def _(seq):
            attend_pair(
                valid_ref, seq, pair, projected, far, strips, mixed, stat, work, probs, rows, inner
            )

        if pair == 1:
            arrive(plane_waits[1])
            first = first_turn(up_all)
    put(mixed, mixed_out)
    put(stat, stat_out)

    for place in rows_of(row_total, rows // 2):
        value = tokens_ref[place, :].astype(f32) + dot_nn(mixed[place, :], proj[...])
        total[place, :] = value
        scale = lax.rsqrt(jnp.mean(value * value, axis=1, keepdims=True) + norm_eps)
        low_mid[place, :] = (value * scale * gains[pl.ds(1, 1), :]).astype(bf16)
    put(total, after_out)
    put(low_mid, low_mid_out)

    columns = pl.ds(0, group)

    def stream(order, target, body, extra=None):
        def get(at, slot):
            half, number = order[at]
            found = [
                pltpu.make_async_copy(target.at[half, number], weights.at[slot], fetch.at[0, slot])
            ]
            if extra is not None:
                found.append(
                    pltpu.make_async_copy(
                        extra.at[half, number], gate_buf.at[slot], fetch.at[1, slot]
                    )
                )
            for copy in found:
                copy.start()
            return found

        waiting = get(0, 0)
        for at, (half, number) in enumerate(order):
            following = get(at + 1, (at + 1) % 2) if at + 1 < len(order) else None
            for copy in waiting:
                copy.wait()
            body(at, half, number, at % 2)
            waiting = following

    pending = {}

    def settle(slot):
        for copy in pending.pop(slot, ()):
            copy.wait()

    def gate_body(at, half, number, slot):
        settle(slot)
        for place in rows_of(row_total, rows):
            gate_buf[slot, place, columns] = dot_nt(low_mid[place, :], weights[slot])
        copy = pltpu.make_async_copy(
            gate_buf.at[slot], gate_pre_out.at[half, number], store.at[slot]
        )
        copy.start()
        pending[slot] = [copy]

    def up_body(at, half, number, slot):
        settle(slot)
        for place in rows_of(row_total, rows // 2):
            value = dot_nt(low_mid[place, :], weights[slot])
            up_buf[slot, place, columns] = value
            hidden[half, number, place, columns] = (
                gelu_parts(gate_buf[slot, place, columns])[0] * value
            ).astype(bf16)
        copy = pltpu.make_async_copy(
            up_buf.at[slot], up_pre_out.at[half, number], store.at[slot]
        )
        copy.start()
        pending[slot] = [copy]

    def down_body(at, half, number, slot):
        for place in rows_of(row_total, rows // 2):
            total[place, :] += dot_nn(hidden[half, number, place, columns], weights[slot])

    every = [(half, number) for half in range(2) for number in range(4)]
    cores_held = cores
    arrive(second)
    cores_held = cores_held + core_turn(gate_all, 1)
    stream(every[:4], gate_all, gate_body)
    arrive(first)
    up_cores = core_turn(up_all, 0)
    up_second = second_turn(up_all)
    arrive(cores_held)
    stream(every[4:], gate_all, gate_body)
    arrive(plane_waits[2])
    down_first = first_turn(down_all)
    settle(0)
    settle(1)
    arrive(up_second)
    up_cores = up_cores + core_turn(up_all, 1)
    stream(every[:4], up_all, up_body, gate_pre_out)
    arrive(down_first)
    down_cores = core_turn(down_all, 0)
    down_second = second_turn(down_all)
    arrive(up_cores)
    stream(every[4:], up_all, up_body, gate_pre_out)
    settle(0)
    settle(1)
    put(hidden, hidden_out)
    for copy in flushed:
        if copy is not flushed[-1]:
            copy.wait()
    arrive(down_cores)
    stream([(0, 0), (0, 2), (1, 0), (1, 2)], down_all, down_body)
    arrive(down_second)
    down_cores = core_turn(down_all, 1)
    stream([(0, 1), (0, 3)], down_all, down_body)
    arrive(down_cores)
    stream([(1, 1), (1, 3)], down_all, down_body)
    flushed[-1].wait()

    put(total, block_out)
    flushed[-1].wait()
    copies.finish()


def front(valid, diagonal, tokens, small, mixed, gate_t, up_t, down, qkv_rows, sizes, count):
    seqs, rows, heads, inner = sizes
    total, model = tokens.shape
    planes = count // 4
    group = count // 4 * gate_t.shape[0]
    number = 5 * (planes - 1) + 8 + 3 * 8
    any_space = pl.BlockSpec(memory_space=pl.ANY)
    vmem = pl.BlockSpec(memory_space=pltpu.VMEM)
    shape = jax.ShapeDtypeStruct
    kept = [
        ((total, model), bf16),
        ((total, 3 * inner), bf16),
        ((total, 2 * inner), bf16),
        ((total, inner), bf16),
        ((seqs, heads // 2, 8, rows), f32),
        ((total, model), f32),
        ((total, model), bf16),
        ((8, model), f32),
        ((3 * inner, model), bf16),
        ((inner, model), bf16),
    ]
    return pl.pallas_call(
        functools.partial(front_kernel, count, qkv_rows),
        in_specs=[pl.BlockSpec(memory_space=pltpu.SMEM), vmem, vmem] + [any_space] * 5,
        out_specs=[any_space] * 17,
        out_shape=[shape((2, 4, group, model), bf16)] * 3
        + [shape(*at) for at in kept]
        + [shape((2, 4, total, max(rows, group)), f32)] * 2
        + [shape((2, 4, total, max(rows, group)), bf16), shape((total, model), f32)],
        scratch_shapes=[
            pltpu.VMEM((planes, 2, 2) + small.shape, f32),
            pltpu.VMEM((planes, 2, 2, 2) + mixed.shape, bf16),
        ]
        + [pltpu.VMEM(*at) for at in kept]
        + [
            pltpu.VMEM((2, strip_rows, 4 * rows), f32),
            pltpu.VMEM((2 * rows, rows), bf16),
            pltpu.VMEM((2, group, model), bf16),
            pltpu.VMEM((2, total, max(rows, group)), f32),
            pltpu.VMEM((2, total, max(rows, group)), f32),
            pltpu.VMEM((2, 4, total, max(rows, group)), bf16),
            pltpu.SemaphoreType.DMA((number,)),
            pltpu.SemaphoreType.DMA((number,)),
            pltpu.SemaphoreType.DMA((5,)),
            pltpu.SemaphoreType.DMA((16,)),
            pltpu.SemaphoreType.DMA((2, 2)),
            pltpu.SemaphoreType.DMA((2,)),
        ],
        compiler_params=pltpu.CompilerParams(
            collective_id=0, has_side_effects=True, vmem_limit_bytes=61 * 2**20
        ),
    )(valid, diagonal, tokens, small, mixed, gate_t, up_t, down)


def butterfly(count):
    return [0] + [1 << at for at in range(count.bit_length() - 1)]


def norm_slope(value, gain, grad):
    scale = lax.rsqrt(jnp.mean(value * value, axis=1, keepdims=True) + norm_eps)
    scaled = grad * gain
    drift = jnp.mean(value * scaled, axis=1, keepdims=True)
    return scale * scaled - value * (scale * scale * scale * drift), grad * value * scale


def attend_back_pair(
    valid_ref, seq, pair, projected, far, window, stat, grads, probs, slopes, low, strip_sum, halves,
    own_out, far_out, rows, inner,
):
    width = strip_rows // 2
    seq_rows = pl.ds(pl.multiple_of(seq * rows, rows), rows)
    first = strip_rows * pair
    queries = projected[seq_rows, lanes(first)]
    grad_rows = grads[seq_rows, lanes(first)]
    sources = ((projected, inner), (far, 0))
    outs = []
    for head in range(2):
        query = head_lanes(queries, head, width)
        grad = head_lanes(grad_rows, head, width)
        log_total = stat[seq, pair, pl.ds(head, 1), :]
        drift = jnp.zeros((8, rows), f32)
        for half, (source, base) in enumerate(sources):
            for at in range(0, rows, strip_rows):
                place = pl.ds(half * rows + at, strip_rows)
                to = pl.ds(pl.multiple_of(seq * rows + at, strip_rows), strip_rows)
                start = rows - strip_rows - at
                scores = dot_nt(source[to, lanes(base + first)], query) + window(head, half, start)
                row = at + lax.broadcasted_iota(jnp.int32, scores.shape, 0)
                scores = jnp.where(row < valid_ref[seq, half], scores, masked_score)
                part = jnp.exp(scores - log_total)
                slope = dot_nt(source[to, lanes(base + inner + first)], grad)
                probs[place, :] = part
                slopes[place, :] = slope
                drift = drift + fold_rows(part * slope, jnp.sum)
        drift = jnp.sum(drift, axis=0, keepdims=True)
        for half in range(2):
            for at in range(0, rows, strip_rows):
                place = pl.ds(half * rows + at, strip_rows)
                to = pl.ds(pl.multiple_of(seq * rows + at, strip_rows), strip_rows)
                part = probs[place, :]
                grad_scores = (part * (slopes[place, :] - drift)).astype(bf16)
                low[place, :] = grad_scores
                start = 2 * half * rows + rows - strip_rows - at
                strip_sum[head, :, pl.ds(start, rows)] += grad_scores.astype(f32)
                terms = (dot_nn(grad_scores, query), dot_nn(part.astype(bf16), grad))
                for which, term in enumerate(terms):
                    if head == 0:
                        halves[which, place, :] = term
                    elif half == 0:
                        own_out[to, lanes(which * inner + first)] = halves[which, place, :] + term
                    else:
                        far_out[which, to, lanes(first)] = (
                            halves[which, place, :] + term
                        ).astype(bf16)
        keys = [source[seq_rows, lanes(base + first)] for source, base in sources]
        grad_query = dot_tn(keys[0], low[pl.ds(0, rows), :]) + dot_tn(
            keys[1], low[pl.ds(rows, rows), :]
        )
        outs.append(grad_query[head * width : (head + 1) * width, :])
    projected[seq_rows, lanes(first)] = jnp.concatenate(outs, axis=0).T.astype(bf16)


def back_kernel(
    count,
    qkv_rows,
    valid_ref,
    diag_ref,
    one_hot_ref,
    gate_grad_ref,
    gains,
    stat,
    tokens_in,
    out_grad_in,
    block_in,
    after_in,
    low_in_in,
    low_mid_in,
    projected_in,
    far_in,
    mixed_in,
    qkv_in,
    proj_in,
    gate_all,
    up_all,
    down_all,
    gate_pre,
    up_pre,
    hidden_in,
    gate_values,
    tokens_out,
    mixed_sum,
    small_sum,
    gate_sum,
    up_sum,
    down_sum,
    core_land,
    one_land,
    two_land,
    last_land,
    kv_land,
    mixed_core,
    mixed_one,
    mixed_two,
    mixed_last,
    total,
    grad_ff,
    low_mid,
    weights,
    pre,
    hidden,
    slope_bufs,
    turned,
    sending,
    sums,
    kept,
    staging,
    halves,
    far,
    strip_sum,
    rowbuf,
    small,
    diag,
    gain_sums,
    send,
    recv,
    fetch,
    stage,
    row_sem,
    park,
):
    planes = count // 4
    part = planes // 2
    row_total, model = total.shape
    seqs, pairs = stat.shape[:2]
    rows = row_total // seqs
    inner = proj_in.shape[0]
    group = gate_all.shape[2]
    piece = group // (2 * part)
    block = mixed_sum.shape[0]
    turns = ((1, 2), (2, 1))
    columns = pl.ds(0, group)
    greet(count)
    copies = Copies(count, send, recv)
    dp, ctx = copies.dp, copies.ctx
    used = [0]

    def load(source, target):
        copy = pltpu.make_async_copy(source, target, fetch.at[used[0]])
        used[0] += 1
        copy.start()
        return copy

    block_load = load(block_in, total)
    grad_load = load(out_grad_in, weights.at[pl.ds(0, row_total)])
    hidden_order = [(half, at) for half in (1, 0) for at in (1, 3, 0, 2)]

    def hidden_load(step):
        half, at = hidden_order[step]
        return load(hidden_in.at[half, at], hidden.at[step % 2])

    hidden_wait = hidden_load(0)
    low_mid_load = load(low_mid_in, low_mid)
    gain_sums[...] = jnp.zeros_like(gain_sums)
    block_load.wait()
    grad_load.wait()

    @pl.loop(0, row_total // strip_rows)
    def _(at):
        place = pl.ds(pl.multiple_of(at * strip_rows, strip_rows), strip_rows)
        value = total[place, :]
        gain = gains[pl.ds(2, 1), :]
        delete = gains[pl.ds(3, 1), :]
        scale = lax.rsqrt(jnp.mean(value * value, axis=1, keepdims=True) + norm_eps)
        low_out = (value * scale * gain).astype(bf16).astype(f32)
        logit = jnp.sum(low_out * delete, axis=1, keepdims=True)
        sigmoid = 1.0 / (1.0 + jnp.exp(-logit))
        gate_values[place, :] = delete_scale * sigmoid
        grad_logit = (
            (gate_grad_ref[place, :] * delete_scale * sigmoid * (1.0 - sigmoid))
            .astype(bf16)
            .astype(f32)
        )
        slope, gain_part = norm_slope(value, gain, grad_logit * delete)
        grad = weights[place, :].astype(f32) + slope
        total[place, :] = grad
        grad_ff[place, :] = grad.astype(bf16)
        gain_sums[pl.ds(16, 8), :] += fold_rows(gain_part, jnp.sum)
        gain_sums[pl.ds(24, 8), :] += fold_rows(grad_logit * low_out, jnp.sum)

    parked = pltpu.make_async_copy(total, tokens_out, park.at[0])
    parked.start()

    outs = (down_sum, gate_sum, up_sum)
    high = ((0, 1), (0, 1), (2, 3))
    lows = ((4, 5), (6, 7), (4, 5))
    keep_at = (0, 1, 0)
    one, two, last = {}, {}, {}
    stage_slot = [0]

    def slot_rows(slot, size=group):
        return pl.ds(slot * group, size)

    def pull(source, size):
        slot = stage_slot[0] % 2
        stage_slot[0] += 1
        copy = pltpu.make_async_copy(source, staging.at[slot_rows(slot, size)], stage.at[slot])
        copy.start()
        return copy, slot * group

    def add_rows(target, base, other, other_base, size, out=None, out_base=0):
        step = 64 if size % 64 == 0 else 16
        into, into_base = (target, base) if out is None else (out, out_base)

        @pl.loop(0, size // step)
        def _(at):
            place = lambda first: pl.ds(pl.multiple_of(first + at * step, 16), step)
            into[place(into_base), :] = (
                target[place(base), :].astype(f32) + other[place(other_base), :].astype(f32)
            ).astype(bf16)

    def send_high(at, half):
        one[at, half] = copies.start(
            sums.at[slot_rows(high[at][half])], one_land.at[at, half], turns[half][0]
        )

    def after_one(at):
        waits = []
        for half in range(2):
            one[at, half].wait_recv()
            waits.append(pull(one_land.at[at, half], group))
        for half, (copy, base) in enumerate(waits):
            slot = lows[at][half]
            copy.wait()
            add_rows(sums, slot * group, staging, base, group)
            two[at, half] = copies.start(
                sums.at[pl.ds(slot * group + part * piece, part * piece)],
                two_land.at[at, half],
                turns[half][1],
            )

    def after_two(at):
        waits = []
        for half in range(2):
            two[at, half].wait_recv()
            waits.append(pull(two_land.at[at, half], part * piece))
        last[at] = []
        if at == 2:
            for copy in last[0]:
                copies.sent(copy)
        base_row = keep_at[at] * group
        for half, (copy, base) in enumerate(waits):
            copy.wait()
            add_rows(
                sums,
                lows[at][half] * group,
                staging,
                base,
                part * piece,
                kept,
                base_row + half * part * piece,
            )
            for plane in range(part):
                step = half * part + plane
                if step:
                    last[at].append(
                        copies.start(
                            kept.at[pl.ds(base_row + step * piece, piece)],
                            last_land.at[at, pl.ds((step - 1) * piece, piece)],
                            4 * step,
                        )
                    )

    def after_last(at):
        for copy in last[at]:
            copy.wait_recv()
        copy, base = pull(last_land.at[at], (planes - 1) * piece)
        copy.wait()
        result = kept[pl.ds(keep_at[at] * group, piece), :].astype(f32)
        for step in range(planes - 1):
            result = result + staging[pl.ds(base + step * piece, piece), :].astype(f32)
        outs[at][...] = result

    arrived = {}

    def send_far(at, number, slot):
        arrived[at, number] = copies.start(
            sending.at[slot_rows(slot)], core_land.at[at, number], 0
        )
        return arrived[at, number]

    def own_slot(at, number):
        return (high if number % 2 else lows)[at][number // 2]

    def add_far(at, number, pulled):
        copy, base = pulled
        copy.wait()
        slot = own_slot(at, number)
        add_rows(sums, slot * group, staging, base, group)
        if number % 2:
            send_high(at, number // 2)

    last_send = {}
    for step, (half, number) in enumerate(hidden_order):
        following = hidden_load(step + 1) if step + 1 < len(hidden_order) else None
        hidden_wait.wait()
        turned[0] = hidden[step % 2].T
        if half:
            if step % 2 in last_send:
                copies.sent(last_send[step % 2])
            sending[slot_rows(step % 2), :] = dot_nn(turned[0, columns, :], grad_ff[...]).astype(bf16)
            last_send[step % 2] = send_far(0, number, step % 2)
        else:
            arrived[0, number].wait_recv()
            pulled = pull(core_land.at[0, number], group)
            sums[slot_rows(own_slot(0, number)), :] = dot_nn(
                turned[0, columns, :], grad_ff[...]
            ).astype(bf16)
            add_far(0, number, pulled)
        hidden_wait = following

    parked.wait()
    low_mid_load.wait()
    order = hidden_order
    down_slots, gate_slot, up_slot = (0, 1), 2, 3

    def down_load(step):
        half, number = order[step]
        return load(down_all.at[half, number], weights.at[slot_rows(down_slots[step % 2])])

    def pre_load(step):
        half, number = order[step]
        return [load(gate_pre.at[half, number], pre.at[0]), load(up_pre.at[half, number], pre.at[1])]

    def pair_load(step):
        half, number = order[step]
        return [
            load(gate_all.at[half, number], weights.at[slot_rows(gate_slot)]),
            load(up_all.at[half, number], weights.at[slot_rows(up_slot)]),
        ]

    tile = rows // 2
    tiles = row_total // tile
    down_wait = down_load(0)
    pre_wait = pre_load(0)
    pair_wait = pair_load(0)
    for step, (half, number) in enumerate(order):
        following = down_load(step + 1) if step + 1 < len(order) else None
        down_wait.wait()
        for copy in pre_wait:
            copy.wait()
        down_rows = slot_rows(down_slots[step % 2])

        @pl.loop(0, tiles)
        def _(at):
            place = pl.ds(pl.multiple_of(at * tile, tile), tile)
            grad_hidden = dot_nt(grad_ff[place, :], weights[down_rows, :])
            value, slope = gelu_parts(pre[0, place, columns])
            slope_bufs[0, place, columns] = (grad_hidden * pre[1, place, columns] * slope).astype(bf16)
            slope_bufs[1, place, columns] = (grad_hidden * value).astype(bf16)

        down_wait = following
        pre_wait = pre_load(step + 1) if step + 1 < len(order) else ()
        pulled = []
        for which in range(2):
            turned[which] = slope_bufs[which].T
            at = 1 + which
            if half:
                if which in last_send:
                    copies.sent(last_send[which])
                sending[slot_rows(which), :] = dot_nn(
                    turned[which, columns, :], low_mid[...]
                ).astype(bf16)
                last_send[which] = send_far(at, number, which)
            else:
                arrived[at, number].wait_recv()
                pulled = pull(core_land.at[at, number], group)
                slot = own_slot(at, number)
                if at == 1 and number % 2:
                    copies.sent(one[0, number // 2])
                if at == 2 and number % 2 == 0:
                    copies.sent(two[0, number // 2])
                sums[slot_rows(slot), :] = dot_nn(turned[which, columns, :], low_mid[...]).astype(
                    bf16
                )
                add_far(at, number, pulled)
        for copy in pair_wait:
            copy.wait()

        @pl.loop(0, tiles)
        def _(at):
            place = pl.ds(pl.multiple_of(at * tile, tile), tile)
            term = dot_nn(slope_bufs[0, place, columns], weights[slot_rows(gate_slot), :]) + dot_nn(
                slope_bufs[1, place, columns], weights[slot_rows(up_slot), :]
            )
            total[place, :] = term if step == 0 else total[place, :] + term

        pair_wait = pair_load(step + 1) if step + 1 < len(order) else ()
        if step == 3:
            after_one(0)
        if step == 5:
            after_two(0)

    qkv_place, proj_place = pl.ds(0, 3 * inner), pl.ds(3 * inner, inner)
    projected_place = pl.ds(4 * inner, row_total)
    qkv_load = load(qkv_in, weights.at[qkv_place])
    proj_load = load(proj_in, weights.at[proj_place])
    projected = weights.at[projected_place, pl.ds(0, 3 * inner)]
    projected_load = load(projected_in, projected)
    mixed = hidden.at[0, :, pl.ds(0, inner)]
    mixed_load = load(mixed_in, mixed)
    far_load = load(far_in, far)
    tokens_load = load(tokens_in, low_mid)
    thin = rowbuf.shape[2]

    def thin_rows(at):
        return pl.ds(pl.multiple_of(at * thin, thin), thin)

    def row_copies(sources, at, slot):
        return [
            pltpu.make_async_copy(source.at[thin_rows(at)], rowbuf.at[which, slot], row_sem.at[which, slot])
            for which, source in enumerate(sources)
        ]

    def row_stream(sources, body):
        steps = row_total // thin
        for copy in row_copies(sources, 0, 0):
            copy.start()

        @pl.loop(0, steps)
        def _(at):
            slot = at % 2
            for copy in row_copies(sources, at, slot):
                copy.wait()

            @pl.when(at + 1 < steps)
            def _():
                for copy in row_copies(sources, at + 1, 1 - slot):
                    copy.start()

            body(thin_rows(at), slot)

    def middle(place, slot):
        slope, gain_part = norm_slope(rowbuf[0, slot], gains[pl.ds(1, 1), :], total[place, :])
        grad = rowbuf[1, slot] + slope
        total[place, :] = grad
        grad_ff[place, :] = grad.astype(bf16)
        gain_sums[pl.ds(8, 8), :] += fold_rows(gain_part, jnp.sum)

    row_stream((after_in, tokens_out), middle)
    parked = pltpu.make_async_copy(total, tokens_out, park.at[0])
    parked.start()
    grads = slope_bufs.at[1, :, pl.ds(0, inner)]
    proj_load.wait()
    for place in rows_of(row_total, rows):
        grads[place, :] = dot_nt(grad_ff[place, :], weights[proj_place, :]).astype(bf16)
    mixed_load.wait()
    weights[proj_place, :] = dot_tn(mixed[...], grad_ff[...]).astype(bf16)
    low_in_load = load(low_in_in, grad_ff)
    after_one(1)
    after_last(0)
    projected_load.wait()
    far_load.wait()
    parked.wait()

    probs = total.at[:, pl.ds(2 * inner, rows)]
    slopes = pre.at[0, :, pl.ds(0, rows)]
    low = slope_bufs.at[0, :, pl.ds(0, rows)]
    for pair in range(pairs):
        for head in range(2):
            for half in range(2):
                strip = strip_of(diag_ref[pl.ds(4 * pair + 2 * head + half, 1), :], 2 * rows)
                for side in range(2):
                    pre[1, pl.ds((4 * head + 2 * half + side) * strip_rows, strip_rows), pl.ds(0, rows)] = (
                        strip[:, side * rows : (side + 1) * rows]
                    )

        def window(head, half, start):
            first = (4 * head + 2 * half) * strip_rows
            found = pre[1, pl.ds(first, strip_rows), pl.ds(start, rows - start)]
            if start:
                found = jnp.concatenate(
                    [found, pre[1, pl.ds(first + strip_rows, strip_rows), pl.ds(0, start)]], axis=1
                )
            return found

        strip_sum[...] = jnp.zeros_like(strip_sum)

        @pl.loop(0, seqs)
        def _(seq):
            attend_back_pair(
                valid_ref, seq, pair, projected, far, window, stat, grads, probs, slopes, low,
                strip_sum, halves, total, hidden, rows, inner,
            )

        span = 2 * rows
        for head in range(2):
            for half in range(2):
                skew = strip_sum[head, :, pl.ds(half * span, span)]
                row = lax.broadcasted_iota(jnp.int32, skew.shape, 0)
                step = 1
                while step < strip_rows:
                    skew = jnp.where(row & step != 0, pltpu.roll(skew, span - step, 1), skew)
                    step = 2 * step
                diag[pl.ds(2 * pair + head, 1), pl.ds(half * span, span)] = jnp.sum(
                    skew, axis=0, keepdims=True
                )
        if pair == 1:
            after_two(1)
    swap = [
        copies.start(hidden.at[which, :, pl.ds(0, inner)], kv_land.at[which], 0) for which in range(2)
    ]
    after_one(2)
    for which in range(2):
        swap[which].wait_recv()
    kv_loads = [
        load(kv_land.at[which], far.at[:, pl.ds(which * inner, inner)]) for which in range(2)
    ]
    for which in range(2):
        kv_loads[which].wait()
        for place in rows_of(row_total, rows):
            to = pl.ds(which * inner, inner)
            projected[place, pl.ds((which + 1) * inner, inner)] = (
                total[place, to] + far[place, to].astype(f32)
            ).astype(bf16)

    low_in_load.wait()
    for at, half in ((1, 0), (1, 1), (2, 0), (2, 1)):
        copies.sent(one[at, half])
    out_size = inner // (2 * count)
    cut = row_total - inner
    total[pl.ds(cut, inner), :] = weights[proj_place, :].astype(f32)
    first_blocks = cut // qkv_rows
    for base, begin, end in ((0, 0, first_blocks), (3 * inner - cut, first_blocks, 2 * count)):
        for to in range(0, cut, cut // 2 // strip_rows * strip_rows):
            size = min(cut // 2 // strip_rows * strip_rows, cut - to)
            total[pl.ds(to, size), :] = dot_tn(projected[:, pl.ds(base + to, size)], grad_ff[...])
        for at in range(begin, end):
            rowbuf[0, 0, pl.ds(0, qkv_rows), :] = total[pl.ds(at * qkv_rows - base, qkv_rows), :]
            rowbuf[0, 0, pl.ds(qkv_rows, out_size), :] = total[pl.ds(cut + at * out_size, out_size), :]
            sums[pl.ds(at * block, block), :] = rowbuf[0, 0, pl.ds(0, block), :].astype(bf16)

    def piece_row(half, at, core):
        far_bit, near_bit, plane = at // (2 * part), at // part % 2, at % part
        bits = turns[half][0] * far_bit + turns[half][1] * near_bit + 4 * (half * part + plane)
        return pl.multiple_of((flip(dp, bits) * 2 + core) * block, 16)

    every = [(half, at) for half in range(2) for at in range(4 * part)]
    core_waits = [
        copies.start(
            sums.at[pl.ds(piece_row(half, at, 1 - ctx), block)],
            mixed_core.at[pl.ds(step * block, block)],
            0,
        )
        for step, (half, at) in enumerate(every)
    ]
    for at in (0, 1):
        copies.sent(last_send[at])
    for step, (half, at) in enumerate(every):
        sending[pl.ds(step * block, block), :] = sums[pl.ds(piece_row(half, at, ctx), block), :]
    for copy in core_waits:
        copy.wait_recv()
    span = 4 * part * block
    copy = pltpu.make_async_copy(mixed_core, staging.at[pl.ds(0, 2 * span)], stage.at[0])
    copy.start()
    copy.wait()
    add_rows(sending, 0, staging, 0, 2 * span)
    mixed_ones = [
        copies.start(
            sending.at[pl.ds(half * span + span // 2, span // 2)], mixed_one.at[half], turns[half][0]
        )
        for half in range(2)
    ]

    qkv_load.wait()

    @pl.loop(0, tiles)
    def _(at):
        place = pl.ds(pl.multiple_of(at * tile, tile), tile)
        total[place, :] = dot_nn(projected[place, :], weights[qkv_place, :])

    after_two(2)
    after_last(1)
    for half in range(2):
        mixed_ones[half].wait_recv()
    copies_in = [
        pltpu.make_async_copy(
            mixed_one.at[half], staging.at[pl.ds(half * span, span // 2)], stage.at[half]
        )
        for half in range(2)
    ]
    for copy in copies_in:
        copy.start()
    mixed_twos = []
    for half in range(2):
        copies_in[half].wait()
        add_rows(sending, half * span, staging, half * span, span // 2)
        mixed_twos.append(
            copies.start(
                sending.at[pl.ds(half * span + span // 4, span // 4)], mixed_two.at[half], turns[half][1]
            )
        )
    tokens_load.wait()

    def first_norm(place, slot):
        slope, gain_part = norm_slope(
            low_mid[place, :].astype(f32), gains[pl.ds(0, 1), :], total[place, :]
        )
        total[place, :] = rowbuf[0, slot] + slope
        gain_sums[pl.ds(0, 8), :] += fold_rows(gain_part, jnp.sum)

    row_stream((tokens_out,), first_norm)
    parked = pltpu.make_async_copy(total, tokens_out, park.at[0])
    parked.start()
    for half in range(2):
        mixed_twos[half].wait_recv()
    copies_in = [
        pltpu.make_async_copy(
            mixed_two.at[half], staging.at[pl.ds(half * span, span // 4)], stage.at[half]
        )
        for half in range(2)
    ]
    for copy in copies_in:
        copy.start()
    mixed_lasts = []
    for half in range(2):
        copies_in[half].wait()
        add_rows(sending, half * span, staging, half * span, span // 4)
        for plane in range(part):
            step = half * part + plane
            if step:
                mixed_lasts.append(
                    copies.start(
                        sending.at[pl.ds(half * span + plane * block, block)],
                        mixed_last.at[pl.ds((step - 1) * block, block)],
                        4 * step,
                    )
                )

    small[0] = jnp.zeros(small.shape[1:], f32)
    for at in range(4):
        small[0, pl.ds(at, 1), :] = jnp.sum(gain_sums[pl.ds(8 * at, 8), :], axis=0, keepdims=True)
    table = lax.dot_general(
        diag[...],
        one_hot_ref[...],
        (((1,), (1,)), ((), ())),
        precision=lax.Precision.HIGHEST,
        preferred_element_type=f32,
    )
    for at in range(2):
        small[0, pl.ds(4, 4), pl.ds(at * 128, 128)] = table[4 * at : 4 * at + 4, :]
    for step, bits in enumerate(butterfly(count)):
        copy = copies.start(small.at[2 * step], small.at[2 * step + 1], bits)
        copy.wait_recv()
        small[2 * step + 2] = small[2 * step] + small[2 * step + 1]
    small_sum[...] = small[2 * len(butterfly(count))]
    for copy in mixed_lasts:
        copy.wait_recv()
    copy = pltpu.make_async_copy(
        mixed_last, staging.at[pl.ds(0, (planes - 1) * block)], stage.at[0]
    )
    copy.start()
    copy.wait()
    result = sending[pl.ds(0, block), :].astype(f32)
    for step in range(planes - 1):
        result = result + staging[pl.ds(step * block, block), :].astype(f32)
    mixed_sum[...] = result
    after_last(2)
    parked.wait()
    copies.finish()


def back(
    valid, diagonal, one_hot, gate_grad, gains, stat, arrays, qkv_rows, block, sizes, count
):
    seqs, rows, heads, inner = sizes
    total, model = arrays[0].shape
    planes = count // 4
    part = planes // 2
    group = arrays[-4].shape[2]
    piece = group // (2 * part)
    wide = max(rows, group)
    rounds = len(butterfly(count))
    number = 3 * (4 + 4 + planes - 1) + 2 + 8 * part + 4 + planes - 1 + rounds
    any_space = pl.BlockSpec(memory_space=pl.ANY)
    vmem = pl.BlockSpec(memory_space=pltpu.VMEM)
    shape = jax.ShapeDtypeStruct
    landing = [
        (3, 4, group, model),
        (3, 2, group, model),
        (3, 2, part * piece, model),
        (3, (planes - 1) * piece, model),
        (2, total, inner),
        (8 * part * block, model),
        (2, 2 * part * block, model),
        (2, part * block, model),
        ((planes - 1) * block, model),
    ]
    thin = 64
    return pl.pallas_call(
        functools.partial(back_kernel, count, qkv_rows),
        in_specs=[pl.BlockSpec(memory_space=pltpu.SMEM)] + [vmem] * 5 + [any_space] * len(arrays),
        out_specs=[vmem, any_space] + [vmem] * 5 + [any_space] * len(landing),
        out_shape=[
            shape((total, 1), f32),
            shape((total, model), f32),
            shape((block, model), f32),
            shape((8, model), f32),
            shape((piece, model), f32),
            shape((piece, model), f32),
            shape((piece, model), f32),
        ]
        + [shape(at, bf16) for at in landing],
        scratch_shapes=[
            pltpu.VMEM((total, model), f32),
            pltpu.VMEM((total, model), bf16),
            pltpu.VMEM((total, model), bf16),
            pltpu.VMEM((max(4 * inner + total, 4 * group), model), bf16),
            pltpu.VMEM((2, total, wide), f32),
            pltpu.VMEM((2, total, wide), bf16),
            pltpu.VMEM((2, total, wide), bf16),
            pltpu.VMEM((2, wide, total), bf16),
            pltpu.VMEM((2 * group, model), bf16),
            pltpu.VMEM((8 * group, model), bf16),
            pltpu.VMEM((2 * group, model), bf16),
            pltpu.VMEM((2 * group, model), bf16),
            pltpu.VMEM((2, 2 * rows, strip_rows), f32),
            pltpu.VMEM((total, 2 * inner), bf16),
            pltpu.VMEM((2, strip_rows, 4 * rows), f32),
            pltpu.VMEM((2, 2, thin, model), f32),
            pltpu.VMEM((2 * rounds + 1, 8, model), f32),
            pltpu.VMEM((8, 4 * rows), f32),
            pltpu.VMEM((32, model), f32),
            pltpu.SemaphoreType.DMA((number,)),
            pltpu.SemaphoreType.DMA((number,)),
            pltpu.SemaphoreType.DMA((64,)),
            pltpu.SemaphoreType.DMA((2,)),
            pltpu.SemaphoreType.DMA((2, 2)),
            pltpu.SemaphoreType.DMA((1,)),
        ],
        compiler_params=pltpu.CompilerParams(
            collective_id=1, has_side_effects=True, vmem_limit_bytes=63 * 2**20
        ),
    )(valid, diagonal, one_hot, gate_grad, gains, stat, *arrays)[:7]


def per_device(
    tokens,
    lengths,
    qkv_weight,
    out_weight,
    gate_weight,
    up_weight,
    down_weight,
    norm_gains,
    delete_weight,
    bias_table,
    out_grad,
    gate_grad,
):
    seqs, rows, model = tokens.shape
    total = seqs * rows
    ctx = lax.axis_index("ctx")
    dp_count = lax.axis_size("dp")
    heads = bias_table.shape[1]
    buckets = bias_table.shape[0]

    qkv_rows = qkv_weight.shape[1]
    shard = model // dp_count
    qkv_rows, out_rows = qkv_weight.shape[1], out_weight.shape[0]
    inner = 2 * dp_count * out_rows
    width = inner // heads
    small = jnp.concatenate([norm_gains, delete_weight.astype(f32)[None]])
    shift = rows * (1 - 2 * ctx)
    place = jnp.arange(2 * rows, dtype=jnp.int32)
    diagonal = (rows - strip_rows) - jnp.where(place >= 2 * rows - strip_rows, place - 2 * rows, place)
    diagonal = jnp.concatenate([diagonal, diagonal + shift])
    one_hot = (bucket_of(diagonal)[:, None] == jnp.arange(buckets)[None, :]).astype(f32)
    bias = jnp.dot(bias_table.T, one_hot.T, precision=lax.Precision.HIGHEST)
    valid = jnp.stack([lengths - rows * ctx, lengths - rows * (1 - ctx)], axis=1)

    def padded(block):
        return jnp.pad(block, ((0, -block.shape[0] % 16), (0, 0)))

    mixed_shard = padded(jnp.concatenate([qkv_weight.T, out_weight]))
    (
        gate_all,
        up_all,
        down_all,
        low_in,
        projected,
        far_kv,
        mixed,
        stats,
        after_attn,
        low_mid,
        gains,
        qkv_t,
        out_full,
        gate_pre_all,
        up_pre_all,
        hidden_all,
        block_out,
    ) = front(
        valid,
        bias.reshape(2 * heads, 2 * rows),
        tokens.reshape(total, model),
        jnp.pad(small, ((0, 4), (0, -shard % 128))),
        mixed_shard,
        padded(gate_weight.T),
        padded(up_weight.T),
        padded(down_weight),
        qkv_rows,
        (seqs, rows, heads, inner),
        dp_count,
    )
    gate_values, tokens_grad, mixed_sum, small_sum, gate_sum, up_sum, down_sum = back(
        valid,
        bias.reshape(2 * heads, 2 * rows),
        jnp.pad(one_hot.T, ((0, 128 - buckets), (0, 0))),
        gate_grad.reshape(total, 1),
        gains,
        stats,
        (
            tokens.reshape(total, model),
            out_grad.reshape(total, model),
            block_out,
            after_attn,
            low_in,
            low_mid,
            projected,
            far_kv,
            mixed,
            qkv_t,
            out_full,
            gate_all,
            up_all,
            down_all,
            gate_pre_all,
            up_pre_all,
            hidden_all,
        ),
        qkv_rows,
        mixed_shard.shape[0],
        (seqs, rows, heads, inner),
        dp_count,
    )
    anchor = lax.axis_index("dp") * shard
    ff_rows = down_weight.shape[0]
    table = jnp.concatenate([small_sum[4:8, :buckets], small_sum[4:8, 128 : 128 + buckets]])
    return (
        block_out.reshape(seqs, rows, model),
        gate_values.reshape(seqs, rows),
        tokens_grad.reshape(seqs, rows, model),
        mixed_sum[:qkv_rows].T,
        mixed_sum[qkv_rows : qkv_rows + out_rows],
        gate_sum[:ff_rows].T,
        up_sum[:ff_rows].T,
        down_sum[:ff_rows],
        lax.dynamic_slice_in_dim(small_sum[:3], anchor, shard, 1),
        lax.dynamic_slice_in_dim(small_sum[3], anchor, shard, 0),
        table[:heads].T,
    )


def solution(mesh):
    wide = P("dp", "ctx", None)
    columns = P(None, ("dp", "ctx"))
    depth = P(("dp", "ctx"), None)
    return jax.shard_map(
        per_device,
        mesh=mesh,
        in_specs=(
            wide,
            P("dp"),
            columns,
            depth,
            columns,
            columns,
            depth,
            P(None, "dp"),
            P("dp"),
            P(),
            wide,
            P("dp", "ctx"),
        ),
        out_specs=(
            wide,
            P("dp", "ctx"),
            wide,
            columns,
            depth,
            columns,
            columns,
            depth,
            P(None, "dp"),
            P("dp"),
            P(),
        ),
        check_vma=False,
    )
```

```python
import functools

import jax
import jax.numpy as jnp
from jax import lax
from jax.experimental import pallas as pl
from jax.experimental.pallas import tpu as pltpu
from jax.sharding import PartitionSpec as P

norm_eps = 1e-06
masked_score = -1e30
delete_scale = -30.0
bucket_edges = (12, 16, 23, 32, 46, 64, 91)
f32 = jnp.float32
bf16 = jnp.bfloat16
strip_rows = 128
fine_rows = 128
fine_unroll = 1
row_depth = 3
ffn_unroll = 0
mid_unroll = 0
tile_cut = 1
row_thin = 64


def bucket_of(offset):
    distance = jnp.abs(offset)
    far_bucket = 8 + sum(((distance >= boundary).astype(jnp.int32) for boundary in bucket_edges))
    near_bucket = jnp.where(distance < 8, distance, jnp.minimum(far_bucket, 15))
    return near_bucket + jnp.where(offset > 0, 16, 0)


def dot_nt(left, right):
    return lax.dot_general(left, right, (((1,), (1,)), ((), ())), preferred_element_type=f32)


def dot_nn(left, right):
    return lax.dot_general(left, right, (((1,), (0,)), ((), ())), preferred_element_type=f32)


def dot_tn(left, right):
    return lax.dot_general(left, right, (((0,), (0,)), ((), ())), preferred_element_type=f32)


def swap_ctx(block):
    return lax.ppermute(block, "ctx", [(0, 1), (1, 0)])


def head_lanes(block, head, width):
    lane = lax.broadcasted_iota(jnp.int32, block.shape, 1)
    return jnp.where(lane // width == head, block, jnp.zeros_like(block))


def fold_rows(block, op):
    return op(block.reshape(block.shape[0] // 8, 8, block.shape[1]), axis=0)


def flip(at, bits):
    bit = 1
    while bit <= bits:
        if bits & bit:
            at = at + bit - 2 * bit * (at // bit % 2)
        bit = 2 * bit
    return at


class Copies:
    def __init__(self, count, send, recv):
        self.send, self.recv, self.made, self.done = send, recv, [], set()
        self.dp, self.ctx = lax.axis_index("dp"), lax.axis_index("ctx")
        self.where = {0: {"ctx": 1 - self.ctx}}
        for bits in [1, 2] + [4 * step for step in range(1, count // 4)]:
            self.where[bits] = {"dp": flip(self.dp, bits)}

    def start(self, source, target, bits):
        at = len(self.made)
        copy = pltpu.make_async_remote_copy(
            src_ref=source,
            dst_ref=target,
            send_sem=self.send.at[at],
            recv_sem=self.recv.at[at],
            device_id=self.where[bits],
            device_id_type=pl.DeviceIdType.MESH,
        )
        copy.start()
        self.made.append(copy)
        return copy

    def sent(self, copy):
        if id(copy) not in self.done:
            copy.wait_send()
            self.done.add(id(copy))

    def finish(self):
        for copy in self.made:
            self.sent(copy)


def greet(count):
    barrier = pltpu.get_barrier_semaphore()
    dp, ctx = lax.axis_index("dp"), lax.axis_index("ctx")
    bits = [1, 2] + [4 * step for step in range(1, count // 4)]
    for at in bits:
        pl.semaphore_signal(
            barrier, inc=1, device_id={"dp": flip(dp, at)}, device_id_type=pl.DeviceIdType.MESH
        )
    pl.semaphore_signal(
        barrier, inc=1, device_id={"ctx": 1 - ctx}, device_id_type=pl.DeviceIdType.MESH
    )
    pl.semaphore_wait(barrier, len(bits) + 1)


def rows_of(total, size):
    return [pl.ds(at, size) for at in range(0, total, size)]


def diagonal_buckets(rows, half):
    place = lax.broadcasted_iota(jnp.int32, (1, 2 * rows), 1)
    lane = jnp.where(place >= 2 * rows - strip_rows, place - 2 * rows, place)
    shift = rows * (1 - 2 * lax.axis_index("ctx")) if half else 0
    return bucket_of((rows - strip_rows) - lane + shift)


def valid_keys(lengths, seq, half, rows):
    ctx = lax.axis_index("ctx")
    return lengths[seq] - rows * (1 - ctx if half else ctx)


def strip_of(diagonal, span):
    wide = jnp.broadcast_to(diagonal, (strip_rows, span))
    return pltpu.roll(wide, 0, 1, stride=1, stride_axis=0)


def fill_strips(strips, diag_ref, pair, span):
    for head in range(2):
        for half in range(2):
            strips[head, :, pl.ds(half * span, span)] = strip_of(
                diag_ref[pl.ds(4 * pair + 2 * head + half, 1), :], span
            )


def score_block(valid_ref, seq, keys, query, strips, head, half, at, rows):
    start = half * strips.shape[2] // 2 + rows - strip_rows - at
    scores = dot_nt(keys, query) + strips[head, :, pl.ds(start, rows)]
    place = at + lax.broadcasted_iota(jnp.int32, scores.shape, 0)
    return jnp.where(place < valid_keys(valid_ref, seq, half, rows), scores, masked_score)


def lanes(first):
    return pl.ds(first, strip_rows)


def attend_pair(valid_ref, seq, pair, projected, far, strips, mixed_ref, stat_ref, work, probs, rows, inner):
    width = strip_rows // 2
    seq_rows = pl.ds(pl.multiple_of(seq * rows, rows), rows)
    first = strip_rows * pair
    queries = projected[seq_rows, lanes(first)]
    outs = []
    for head in range(2):
        query = head_lanes(queries, head, width)
        top = jnp.full((8, rows), masked_score, f32)
        for half, (source, base) in enumerate(((projected, inner), (far, 0))):
            for at in range(0, rows, strip_rows):
                keys = source[pl.ds(pl.multiple_of(seq * rows + at, strip_rows), strip_rows), lanes(base + first)]
                scores = score_block(
                    valid_ref, seq, keys, query, strips, head, half, at, rows
                )
                work[pl.ds(half * rows + at, strip_rows), :] = scores
                top = jnp.maximum(top, fold_rows(scores, jnp.max))
        row_max = jnp.max(top, axis=0, keepdims=True)
        total = jnp.zeros((8, rows), f32)
        for at in range(0, 2 * rows, strip_rows):
            exponent = jnp.exp(work[pl.ds(at, strip_rows), :] - row_max)
            work[pl.ds(at, strip_rows), :] = exponent
            total = total + fold_rows(exponent, jnp.sum)
        row_sum = jnp.sum(total, axis=0, keepdims=True)
        share = 1.0 / row_sum
        for at in range(0, 2 * rows, strip_rows):
            probs[pl.ds(at, strip_rows), :] = (work[pl.ds(at, strip_rows), :] * share).astype(bf16)
        stat_ref[seq, pair, pl.ds(head, 1), :] = row_max + jnp.log(row_sum)
        mixed = dot_tn(
            projected[seq_rows, lanes(2 * inner + first)], probs[pl.ds(0, rows), :]
        ) + dot_tn(far[seq_rows, lanes(inner + first)], probs[pl.ds(rows, rows), :])
        outs.append(mixed[head * width : (head + 1) * width, :])
    mixed_ref[seq_rows, lanes(first)] = jnp.concatenate(outs, axis=0).T.astype(bf16)


def gelu_parts(value):
    inner = 0.7978845608028654 * (value + 0.044715 * value * value * value)
    slope = 0.7978845608028654 * (1.0 + 3.0 * 0.044715 * value * value)
    tanh = jnp.tanh(inner)
    half = 0.5 * (1.0 + tanh)
    return value * half, half + 0.5 * value * (1.0 - tanh * tanh) * slope


def front_kernel(
    count,
    qkv_rows,
    valid_ref,
    table_ref,
    tokens_ref,
    gains_in,
    delete_in,
    qkv_in,
    proj_in,
    out_grad_in,
    gate_in,
    up_in,
    down_in,
    gate_all,
    up_all,
    down_all,
    low_in_out,
    projected_out,
    far_out,
    mixed_out,
    stat_out,
    after_out,
    low_mid_out,
    gains_out,
    qkv_out,
    proj_out,
    gate_pre_out,
    up_pre_out,
    hidden_out,
    block_out,
    diag_out,
    out_grad_out,
    tokens_out,
    small_in,
    mixed_in,
    diag_ref,
    small_all,
    mixed_all,
    low_in,
    projected,
    far,
    mixed,
    stat,
    total,
    low_mid,
    gains,
    qkv,
    proj,
    strips,
    probs,
    weights,
    gate_buf,
    up_buf,
    hidden,
    send,
    recv,
    local,
    flush,
    fetch,
    store,
    here_sem,
):
    planes = count // 4
    part = planes // 2
    piece = gate_in.shape[0]
    model = total.shape[1]
    row_total = total.shape[0]
    seqs, pairs = stat.shape[:2]
    rows = row_total // seqs
    inner = proj.shape[0]
    group = gate_all.shape[2]
    shard = model // count
    small_in[...] = jnp.zeros_like(small_in)
    small_in[pl.ds(0, 3), pl.ds(0, shard)] = gains_in[...]
    small_in[pl.ds(3, 1), pl.ds(0, shard)] = delete_in[...].astype(f32)
    out_rows = proj_in.shape[0]
    total[pl.ds(0, mixed_in.shape[0]), :] = jnp.zeros(mixed_in.shape, f32)
    total[pl.ds(0, qkv_rows), :] = qkv_in[...].astype(f32)
    total[pl.ds(qkv_rows, out_rows), :] = proj_in[...].astype(f32)
    mixed_in[...] = total[pl.ds(0, mixed_in.shape[0]), :].astype(bf16)
    greet(count)
    copies = Copies(count, send, recv)
    dp, ctx = copies.dp, copies.ctx
    z, y, x = dp // 4, dp // 2 % 2, dp % 2
    near = pl.ds(z // part * part, part)
    away = pl.ds((1 - z // part) * part, part)
    matrices = ((gate_in, gate_all), (up_in, up_all), (down_in, down_all))
    here = [
        pltpu.make_async_copy(source, target, local.at[at])
        for at, (source, target) in enumerate(
            (
                (mixed_in, mixed_all.at[z, y, x, ctx]),
                (small_in, small_all.at[z, y, x]),
            )
            + tuple((source, target.at[0, 0, pl.ds(0, piece)]) for source, target in matrices)
        )
    ]
    for copy in here:
        copy.start()
    flushed = []

    def put(source, target):
        copy = pltpu.make_async_copy(source, target, flush.at[len(flushed)])
        copy.start()
        flushed.append(copy)

    def arrive(found):
        for copy in found:
            copy.wait_recv()

    bits_down = [1 << at for at in range(planes.bit_length() - 1)][::-1]

    def plane_place(target, plane):
        return target.at[0, 2 * (plane // part), pl.ds(plane % part * piece, piece)]

    def planes_start(source, target):
        return {
            bit: copies.start(source, plane_place(target, bit), 4 * bit) for bit in bits_down
        }

    def planes_rest(target, found):
        for bit in bits_down[:-1]:
            for plane in range(bit, planes, 2 * bit):
                found[plane].wait_recv()
                found[-plane] = None
                for lower in bits_down:
                    if lower < bit:
                        place = plane_place(target, plane)
                        found[plane + lower] = copies.start(
                            place, plane_place(target, plane + lower), 4 * lower
                        )

    def planes_arrive(found, planes_wanted):
        for plane in planes_wanted:
            if plane and -plane not in found:
                found[plane].wait_recv()
                found[-plane] = None

    def first_turn(target, found):
        low, high = pl.ds(0, part * piece), pl.ds(part * piece, part * piece)
        turns = []
        for half, (at, bits) in enumerate(((0, 2), (2, 1))):
            planes_arrive(found, range(half * part, (half + 1) * part))
            turns.append(copies.start(target.at[0, at, low], target.at[0, at, high], bits))
        return turns

    def second_turn(target):
        return [
            copies.start(target.at[0, at], target.at[0, at + 1], bits)
            for at, bits in ((0, 1), (2, 2))
        ]

    def core_turn(target, late):
        return [
            copies.start(target.at[0, at + late], target.at[1, at + late], 0) for at in (0, 2)
        ]

    small_waits = [
        copies.start(small_in, small_all.at[z, y, x], 4 * step) for step in range(1, planes)
    ]
    waits = {
        bit: copies.start(mixed_in, mixed_all.at[z, y, x, ctx], 4 * bit) for bit in bits_down
    }
    for bit in bits_down[:-1]:
        for plane in range(bit, planes, 2 * bit):
            waits[plane].wait_recv()
            for lower in bits_down:
                if lower < bit:
                    place = mixed_all.at[flip(z, plane), y, x, ctx]
                    waits[plane + lower] = copies.start(place, place, 4 * lower)
    plane_waits = [planes_start(*matrices[0])]

    work = gate_buf.at[0, :, pl.ds(0, rows)]
    for half in range(2):
        bucket = diagonal_buckets(rows, half)
        for head in range(2 * pairs):
            bias = jnp.zeros(bucket.shape, f32)
            for at in range(table_ref.shape[0]):
                bias = jnp.where(bucket == at, table_ref[at, head], bias)
            diag_ref[pl.ds(2 * head + half, 1), :] = bias
    put(diag_ref, diag_out)
    for copy in here:
        copy.wait()
    arrive(small_waits)
    small_turn = [copies.start(small_all.at[:, y, x], small_all.at[:, y, x], 2)]
    for plane in range(1, planes, 2):
        waits[plane].wait_recv()
    turn = [
        copies.start(mixed_all.at[near, y, x, ctx], mixed_all.at[near, y, x, ctx], 2),
        copies.start(mixed_all.at[away, y, x, ctx], mixed_all.at[away, y, x, ctx], 1),
    ]
    arrive(small_turn)
    small_turn = [copies.start(small_all.at[:, :, x], small_all.at[:, :, x], 1)]
    arrive(turn)
    turn = [
        copies.start(mixed_all.at[near, :, x, ctx], mixed_all.at[near, :, x, ctx], 1),
        copies.start(mixed_all.at[away, y, :, ctx], mixed_all.at[away, y, :, ctx], 2),
    ]
    planes_rest(gate_all, plane_waits[0])
    plane_waits.append(planes_start(*matrices[1]))
    arrive(small_turn)
    padded = -(-model // 128) * 128
    lane = lax.broadcasted_iota(jnp.int32, (8, 128), 1)
    found = jnp.zeros((8, padded), f32)
    for at in range(count):
        block = jnp.where(lane < shard, small_all[at // 4, at // 2 % 2, at % 2], 0.0)
        block = jnp.concatenate([block, jnp.zeros((8, padded - 128), f32)], axis=1)
        found = found + (pltpu.roll(block, at * shard, 1) if at else block)
    gains[...] = found[:, :model]
    put(gains, gains_out)

    def token_rows(at, size):
        columns = pl.ds(pl.multiple_of(at % (rows // size) * size, size), size)
        return tokens_ref[at // (rows // size), :, columns].astype(f32).T

    @pl.loop(0, row_total // strip_rows)
    def _(at):
        place = pl.ds(pl.multiple_of(at * strip_rows, strip_rows), strip_rows)
        value = token_rows(at, strip_rows)
        scale = lax.rsqrt(jnp.mean(value * value, axis=1, keepdims=True) + norm_eps)
        low_in[place, :] = (value * scale * gains[pl.ds(0, 1), :]).astype(bf16)

    low_in_put = len(flushed)
    put(low_in, low_in_out)
    first = first_turn(gate_all, plane_waits[0])
    arrive(turn)
    turn = [copies.start(mixed_all.at[:, :, :, ctx], mixed_all.at[:, :, :, ctx], 0)]
    planes_rest(up_all, plane_waits[1])
    plane_waits.append(planes_start(*matrices[2]))
    arrive(turn)
    block_rows = mixed_in.shape[0]
    for target, begin, size in ((qkv, 0, qkv_rows), (proj, qkv_rows, inner // (2 * count))):
        batch = min(2 * count, row_total // size // 16 * 16)
        for base in range(0, 2 * count, batch):
            for at in range(base, min(base + batch, 2 * count)):
                block = mixed_all[at // 8, at // 4 % 2, at // 2 % 2, at % 2].astype(f32)
                total[pl.ds((at - base) * size, size), :] = block[begin : begin + size, :]
            number = min(batch, 2 * count - base) * size
            target[pl.ds(base * size, number), :] = total[pl.ds(0, number), :].astype(bf16)
    put(qkv, qkv_out)
    put(proj, proj_out)
    for place in rows_of(row_total, rows):
        for to in rows_of(3 * inner, inner):
            projected[place, to] = dot_nt(low_in[place, :], qkv[to, :]).astype(bf16)
    put(projected, projected_out)
    swap = [copies.start(projected.at[:, pl.ds(inner, 2 * inner)], far, 0)]
    arrive(first)
    cores = core_turn(gate_all, 0)
    second = second_turn(gate_all)
    arrive(swap)
    put(far, far_out)
    stat[...] = jnp.zeros_like(stat)
    for pair in range(pairs):
        fill_strips(strips, diag_ref, pair, 2 * rows)

        @pl.loop(0, seqs)
        def _(seq):
            attend_pair(
                valid_ref, seq, pair, projected, far, strips, mixed, stat, work, probs, rows, inner
            )

        if pair == 0:
            first = first_turn(up_all, plane_waits[1])
            planes_rest(down_all, plane_waits[2])
    put(mixed, mixed_out)
    put(stat, stat_out)

    flushed[low_in_put].wait()
    for at, place in enumerate(rows_of(row_total, rows // 2)):
        value = token_rows(at, rows // 2)
        low_in[place, :] = value.astype(bf16)
        value = value + dot_nn(mixed[place, :], proj[...])
        total[place, :] = value
        scale = lax.rsqrt(jnp.mean(value * value, axis=1, keepdims=True) + norm_eps)
        low_mid[place, :] = (value * scale * gains[pl.ds(1, 1), :]).astype(bf16)
    put(total, after_out)
    put(low_mid, low_mid_out)

    tokens_put = len(flushed)
    put(low_in, tokens_out)
    flushed[tokens_put].wait()
    cut = min(row_total, model)
    for seq in range(seqs):
        for begin in range(0, model, cut):
            size = min(cut, model - begin)
            copy = pltpu.make_async_copy(
                out_grad_in.at[seq, pl.ds(begin, size)],
                hidden.at[seq, begin // cut, pl.ds(0, size), pl.ds(0, rows)],
                here_sem.at[seq, begin // cut],
            )
            copy.start()
            copy.wait()
            for lane in rows_of(rows, strip_rows):
                low_in[pl.ds(seq * rows + lane.start, strip_rows), pl.ds(begin, size)] = (
                    hidden[seq, begin // cut, pl.ds(0, size), lane].T
                )
    put(low_in, out_grad_out)

    columns = pl.ds(0, group)

    def stream(order, target, body, extra=None):
        def get(at, slot):
            half, number = order[at]
            found = [
                pltpu.make_async_copy(target.at[half, number], weights.at[slot], fetch.at[0, slot])
            ]
            if extra is not None:
                found.append(
                    pltpu.make_async_copy(
                        extra.at[half, number], gate_buf.at[slot], fetch.at[1, slot]
                    )
                )
            for copy in found:
                copy.start()
            return found

        waiting = get(0, 0)
        for at, (half, number) in enumerate(order):
            following = get(at + 1, (at + 1) % 2) if at + 1 < len(order) else None
            for copy in waiting:
                copy.wait()
            body(at, half, number, at % 2)
            waiting = following

    pending = {}

    def settle(slot):
        for copy in pending.pop(slot, ()):
            copy.wait()

    def gate_body(at, half, number, slot):
        settle(slot)
        for place in rows_of(row_total, rows):
            gate_buf[slot, place, columns] = dot_nt(low_mid[place, :], weights[slot])
        copy = pltpu.make_async_copy(
            gate_buf.at[slot], gate_pre_out.at[half, number], store.at[slot]
        )
        copy.start()
        pending[slot] = [copy]

    def up_body(at, half, number, slot):
        settle(slot)
        for place in rows_of(row_total, rows // 2):
            value = dot_nt(low_mid[place, :], weights[slot])
            up_buf[slot, place, columns] = value
            hidden[half, number, place, columns] = (
                gelu_parts(gate_buf[slot, place, columns])[0] * value
            ).astype(bf16)
        copy = pltpu.make_async_copy(
            up_buf.at[slot], up_pre_out.at[half, number], store.at[slot]
        )
        copy.start()
        pending[slot] = [copy]

    def down_body(at, half, number, slot):
        for place in rows_of(row_total, rows // 2):
            total[place, :] += dot_nn(hidden[half, number, place, columns], weights[slot])

    every = [(half, number) for half in range(2) for number in range(4)]
    cores_held = cores
    arrive(second)
    cores_held = cores_held + core_turn(gate_all, 1)
    stream(every[:4], gate_all, gate_body)
    arrive(first)
    up_cores = core_turn(up_all, 0)
    up_second = second_turn(up_all)
    arrive(cores_held)
    stream(every[4:], gate_all, gate_body)
    down_first = first_turn(down_all, plane_waits[2])
    settle(0)
    settle(1)
    arrive(up_second)
    up_cores = up_cores + core_turn(up_all, 1)
    stream(every[:4], up_all, up_body, gate_pre_out)
    arrive(down_first)
    down_cores = core_turn(down_all, 0)
    down_second = second_turn(down_all)
    arrive(up_cores)
    stream(every[4:], up_all, up_body, gate_pre_out)
    settle(0)
    settle(1)
    put(hidden, hidden_out)
    for at, copy in enumerate(flushed):
        if at not in (low_in_put, tokens_put) and copy is not flushed[-1]:
            copy.wait()
    arrive(down_cores)
    stream([(0, 0), (0, 2), (1, 0), (1, 2)], down_all, down_body)
    arrive(down_second)
    down_cores = core_turn(down_all, 1)
    stream([(0, 1), (0, 3)], down_all, down_body)
    arrive(down_cores)
    stream([(1, 1), (1, 3)], down_all, down_body)
    flushed[-1].wait()

    put(total, block_out)
    flushed[-1].wait()
    copies.finish()


def front(lengths, table, tokens, gains, delete, qkv, proj, out_grad, gate_t, up_t, down, block, sizes, count):
    seqs, rows, heads, inner = sizes
    total, model = seqs * rows, tokens.shape[1]
    small = jax.ShapeDtypeStruct((8, -(-gains.shape[1] // 128) * 128), f32)
    mixed = jax.ShapeDtypeStruct((block, model), bf16)
    planes = count // 4
    group = count // 4 * gate_t.shape[0]
    number = 5 * (planes - 1) + 8 + 3 * 8
    any_space = pl.BlockSpec(memory_space=pl.ANY)
    vmem = pl.BlockSpec(memory_space=pltpu.VMEM)
    shape = jax.ShapeDtypeStruct
    kept = [
        ((total, model), bf16),
        ((total, 3 * inner), bf16),
        ((total, 2 * inner), bf16),
        ((total, inner), bf16),
        ((seqs, heads // 2, 8, rows), f32),
        ((total, model), f32),
        ((total, model), bf16),
        ((8, model), f32),
        ((3 * inner, model), bf16),
        ((inner, model), bf16),
    ]
    return pl.pallas_call(
        functools.partial(front_kernel, count, qkv.shape[0]),
        in_specs=[pl.BlockSpec(memory_space=pltpu.SMEM)] * 2
        + [vmem] * 5
        + [any_space]
        + [vmem] * 3,
        out_specs=[any_space] * 20,
        out_shape=[shape((2, 4, group, model), bf16)] * 3
        + [shape(*at) for at in kept]
        + [shape((2, 4, total, max(rows, group)), f32)] * 2
        + [shape((2, 4, total, max(rows, group)), bf16), shape((total, model), f32)]
        + [shape((2 * heads, 2 * rows), f32)]
        + [shape((total, model), bf16)] * 2,
        scratch_shapes=[
            pltpu.VMEM(small.shape, f32),
            pltpu.VMEM(mixed.shape, bf16),
            pltpu.VMEM((2 * heads, 2 * rows), f32),
            pltpu.VMEM((planes, 2, 2) + small.shape, f32),
            pltpu.VMEM((planes, 2, 2, 2) + mixed.shape, bf16),
        ]
        + [pltpu.VMEM(*at) for at in kept]
        + [
            pltpu.VMEM((2, strip_rows, 4 * rows), f32),
            pltpu.VMEM((2 * rows, rows), bf16),
            pltpu.VMEM((2, group, model), bf16),
            pltpu.VMEM((2, total, max(rows, group)), f32),
            pltpu.VMEM((2, total, max(rows, group)), f32),
            pltpu.VMEM((2, 4, total, max(rows, group)), bf16),
            pltpu.SemaphoreType.DMA((number,)),
            pltpu.SemaphoreType.DMA((number,)),
            pltpu.SemaphoreType.DMA((5,)),
            pltpu.SemaphoreType.DMA((19,)),
            pltpu.SemaphoreType.DMA((2, 2)),
            pltpu.SemaphoreType.DMA((2,)),
            pltpu.SemaphoreType.DMA((seqs, 2)),
        ],
        compiler_params=pltpu.CompilerParams(
            collective_id=0, has_side_effects=True, vmem_limit_bytes=61 * 2**20
        ),
    )(lengths, table, tokens, gains, delete, qkv, proj, out_grad, gate_t, up_t, down)


def butterfly(count):
    return [0] + [1 << at for at in range(count.bit_length() - 1)]


def norm_slope(value, gain, grad):
    scale = lax.rsqrt(jnp.mean(value * value, axis=1, keepdims=True) + norm_eps)
    scaled = grad * gain
    drift = jnp.mean(value * scaled, axis=1, keepdims=True)
    return scale * scaled - value * (scale * scale * scale * drift), grad * value * scale


def attend_back_pair(
    valid_ref, seq, pair, projected, far, window, stat, grads, probs, slopes, low, strip_sum, halves,
    own_out, far_out, rows, inner,
):
    width = strip_rows // 2
    seq_rows = pl.ds(pl.multiple_of(seq * rows, rows), rows)
    first = strip_rows * pair
    queries = projected[seq_rows, lanes(first)]
    grad_rows = grads[seq_rows, lanes(first)]
    sources = ((projected, inner), (far, 0))
    outs = []
    for head in range(2):
        query = head_lanes(queries, head, width)
        grad = head_lanes(grad_rows, head, width)
        log_total = stat[seq, pair, pl.ds(head, 1), :]
        drift = jnp.zeros((8, rows), f32)
        for half, (source, base) in enumerate(sources):
            for at in range(0, rows, strip_rows):
                place = pl.ds(half * rows + at, strip_rows)
                to = pl.ds(pl.multiple_of(seq * rows + at, strip_rows), strip_rows)
                start = rows - strip_rows - at
                scores = dot_nt(source[to, lanes(base + first)], query) + window(head, half, start)
                row = at + lax.broadcasted_iota(jnp.int32, scores.shape, 0)
                scores = jnp.where(row < valid_keys(valid_ref, seq, half, rows), scores, masked_score)
                part = jnp.exp(scores - log_total)
                slope = dot_nt(source[to, lanes(base + inner + first)], grad)
                probs[place, :] = part
                slopes[place, :] = slope
                drift = drift + fold_rows(part * slope, jnp.sum)
        drift = jnp.sum(drift, axis=0, keepdims=True)
        for half in range(2):
            for at in range(0, rows, strip_rows):
                place = pl.ds(half * rows + at, strip_rows)
                to = pl.ds(pl.multiple_of(seq * rows + at, strip_rows), strip_rows)
                part = probs[place, :]
                grad_scores = (part * (slopes[place, :] - drift)).astype(bf16)
                low[place, :] = grad_scores
                start = 2 * half * rows + rows - strip_rows - at
                strip_sum[head, :, pl.ds(start, rows)] += grad_scores.astype(f32)
                terms = (dot_nn(grad_scores, query), dot_nn(part.astype(bf16), grad))
                for which, term in enumerate(terms):
                    if head == 0:
                        halves[which, place, :] = term
                    elif half == 0:
                        own_out[to, lanes(which * inner + first)] = halves[which, place, :] + term
                    else:
                        far_out[which, to, lanes(first)] = (
                            halves[which, place, :] + term
                        ).astype(bf16)
        keys = [source[seq_rows, lanes(base + first)] for source, base in sources]
        grad_query = dot_tn(keys[0], low[pl.ds(0, rows), :]) + dot_tn(
            keys[1], low[pl.ds(rows, rows), :]
        )
        outs.append(grad_query[head * width : (head + 1) * width, :])
    projected[seq_rows, lanes(first)] = jnp.concatenate(outs, axis=0).T.astype(bf16)


def back_kernel(
    count,
    qkv_rows,
    valid_ref,
    diag_ref,
    gate_grad_in,
    gains,
    stat,
    tokens_in,
    out_grad_in,
    block_in,
    after_in,
    low_in_in,
    low_mid_in,
    projected_in,
    far_in,
    mixed_in,
    qkv_in,
    proj_in,
    gate_all,
    up_all,
    down_all,
    gate_pre,
    up_pre,
    hidden_in,
    gate_values,
    tokens_out,
    mixed_sum,
    small_sum,
    gate_sum,
    up_sum,
    down_sum,
    core_land,
    one_land,
    two_land,
    last_land,
    kv_land,
    mixed_core,
    mixed_one,
    mixed_two,
    mixed_last,
    total,
    grad_ff,
    low_mid,
    weights,
    pre,
    hidden,
    slope_bufs,
    turned,
    sending,
    sums,
    kept,
    staging,
    halves,
    far,
    strip_sum,
    rowbuf,
    small,
    diag,
    gain_sums,
    gate_column,
    send,
    recv,
    fetch,
    stage,
    row_sem,
    park,
):
    planes = count // 4
    part = planes // 2
    row_total, model = total.shape
    seqs, pairs = stat.shape[:2]
    rows = row_total // seqs
    inner = proj_in.shape[0]
    group = gate_all.shape[2]
    piece = group // (2 * part)
    block = mixed_sum.shape[0]
    turns = ((1, 2), (2, 1))
    columns = pl.ds(0, group)
    greet(count)
    copies = Copies(count, send, recv)
    dp, ctx = copies.dp, copies.ctx
    used = [0]

    def load(source, target):
        copy = pltpu.make_async_copy(source, target, fetch.at[used[0]])
        used[0] += 1
        copy.start()
        return copy

    chunks = rows_of(row_total, rows // 2)
    block_loads = [load(block_in.at[chunk], total.at[chunk]) for chunk in chunks]
    grad_loads = [load(out_grad_in.at[chunk], weights.at[chunk]) for chunk in chunks]
    hidden_order = [(half, at) for pair in ((1, 3), (0, 2)) for half in (1, 0) for at in pair]

    def hidden_load(step):
        half, at = hidden_order[step]
        return load(hidden_in.at[half, at], hidden.at[step % 2])

    hidden_wait = hidden_load(0)
    low_mid_load = load(low_mid_in, low_mid)
    gain_sums[...] = jnp.zeros_like(gain_sums)
    for seq in range(seqs):
        wide = jnp.broadcast_to(gate_grad_in[pl.ds(seq, 1), :], (strip_rows, rows))
        gate_column[pl.ds(seq * rows, rows), :] = wide.T[:, :1]

    def out_norm(first):
        place = pl.ds(pl.multiple_of(first, fine_rows), fine_rows)
        value = total[place, :]
        gain = gains[pl.ds(2, 1), :]
        delete = gains[pl.ds(3, 1), :]
        scale = lax.rsqrt(jnp.mean(value * value, axis=1, keepdims=True) + norm_eps)
        low_out = (value * scale * gain).astype(bf16).astype(f32)
        logit = jnp.sum(low_out * delete, axis=1, keepdims=True)
        sigmoid = 1.0 / (1.0 + jnp.exp(-logit))
        grad_logit = (
            (gate_column[place, :] * delete_scale * sigmoid * (1.0 - sigmoid))
            .astype(bf16)
            .astype(f32)
        )
        gate_column[place, :] = delete_scale * sigmoid
        gain_sums[pl.ds(24, 8), :] += fold_rows(grad_logit * low_out, jnp.sum)
        slope, gain_part = norm_slope(value, gain, grad_logit * delete)
        grad = weights[place, :].astype(f32) + slope
        total[place, :] = grad
        grad_ff[place, :] = grad.astype(bf16)
        gain_sums[pl.ds(16, 8), :] += fold_rows(gain_part, jnp.sum)

    for at in range(len(chunks)):
        block_loads[at].wait()
        grad_loads[at].wait()

        @pl.loop(0, rows // 2 // fine_rows, unroll=fine_unroll)
        def _(step):
            out_norm(at * (rows // 2) + step * fine_rows)

    parked = pltpu.make_async_copy(total, tokens_out, park.at[0])
    parked.start()

    outs = (down_sum, gate_sum, up_sum)
    high = ((0, 1), (0, 1), (2, 3))
    lows = ((4, 5), (6, 7), (4, 5))
    keep_at = (0, 1, 0)
    one, two, last = {}, {}, {}
    stage_slot = [0]

    def slot_rows(slot, size=group):
        return pl.ds(slot * group, size)

    def pull(source, size):
        slot = stage_slot[0] % 2
        stage_slot[0] += 1
        copy = pltpu.make_async_copy(source, staging.at[slot_rows(slot, size)], stage.at[slot])
        copy.start()
        return copy, slot * group

    def add_rows(target, base, other, other_base, size, out=None, out_base=0):
        step = 64 if size % 64 == 0 else 16
        into, into_base = (target, base) if out is None else (out, out_base)

        @pl.loop(0, size // step)
        def _(at):
            place = lambda first: pl.ds(pl.multiple_of(first + at * step, 16), step)
            into[place(into_base), :] = (
                target[place(base), :].astype(f32) + other[place(other_base), :].astype(f32)
            ).astype(bf16)

    def send_high(at, half):
        one[at, half] = copies.start(
            sums.at[slot_rows(high[at][half])], one_land.at[at, half], turns[half][0]
        )

    def after_one(at, halves=(0, 1)):
        waits = []
        for half in halves:
            one[at, half].wait_recv()
            waits.append((half,) + pull(one_land.at[at, half], group))
        for half, copy, base in waits:
            slot = lows[at][half]
            copy.wait()
            add_rows(sums, slot * group, staging, base, group)
            two[at, half] = copies.start(
                sums.at[pl.ds(slot * group + part * piece, part * piece)],
                two_land.at[at, half],
                turns[half][1],
            )

    def send_planes(source, base, size, target, bit, found):
        for plane in range(bit, planes, 2 * bit):
            found[plane] = copies.start(
                source.at[pl.ds(base + plane * size, size)],
                target.at[pl.ds((plane - 1) * size, size)],
                4 * bit,
            )

    def after_two(at):
        waits = []
        for half in range(2):
            two[at, half].wait_recv()
            waits.append(pull(two_land.at[at, half], part * piece))
        last[at] = {}
        if at == 2:
            for copy in last[0].values():
                copies.sent(copy)
        base_row = keep_at[at] * group
        for half, (copy, base) in enumerate(waits):
            copy.wait()
            add_rows(
                sums,
                lows[at][half] * group,
                staging,
                base,
                part * piece,
                kept,
                base_row + half * part * piece,
            )
        send_planes(kept, base_row, piece, last_land.at[at], 1, last[at])

    def after_planes(at):
        base_row = keep_at[at] * group
        bit = 1
        while 2 * bit < planes:
            for plane in range(bit, planes, 2 * bit):
                last[at][plane].wait_recv()
                copy, base = pull(last_land.at[at, pl.ds((plane - 1) * piece, piece)], piece)
                copy.wait()
                add_rows(kept, base_row + (plane - bit) * piece, staging, base, piece)
            bit = 2 * bit
            send_planes(kept, base_row, piece, last_land.at[at], bit, last[at])

    def after_last(at):
        plane = planes // 2
        last[at][plane].wait_recv()
        copy, base = pull(last_land.at[at, pl.ds((plane - 1) * piece, piece)], piece)
        copy.wait()
        outs[at][...] = kept[pl.ds(keep_at[at] * group, piece), :].astype(f32) + staging[
            pl.ds(base, piece), :
        ].astype(f32)

    arrived = {}

    def send_far(at, number, slot):
        arrived[at, number] = copies.start(
            sending.at[slot_rows(slot)], core_land.at[at, number], 0
        )
        return arrived[at, number]

    def own_slot(at, number):
        return (high if number % 2 else lows)[at][number // 2]

    def add_far(at, number, pulled, product):
        copy, base = pulled
        slot = own_slot(at, number)
        sums[slot_rows(slot), :] = product.astype(bf16)
        copy.wait()
        add_rows(sums, slot * group, staging, base, group)
        if number % 2:
            send_high(at, number // 2)

    thin = rowbuf.shape[2]

    def thin_rows(at):
        return pl.ds(pl.multiple_of(at * thin, thin), thin)

    def row_copies(sources, at, slot):
        return [
            pltpu.make_async_copy(source.at[thin_rows(at)], rowbuf.at[which, slot], row_sem.at[which, slot])
            for which, source in enumerate(sources)
        ]

    depth = rowbuf.shape[1]

    def row_ahead(sources):
        for at in range(depth - 1):
            for copy in row_copies(sources, at, at):
                copy.start()

    def row_stream(sources, body):
        steps = row_total // thin

        @pl.loop(0, steps)
        def _(at):
            slot = at % depth
            for copy in row_copies(sources, at, slot):
                copy.wait()

            @pl.when(at + depth - 1 < steps)
            def _():
                for copy in row_copies(sources, at + depth - 1, (at + depth - 1) % depth):
                    copy.start()

            body(thin_rows(at), slot, pl.ds(0, thin))

    last_send = {}
    for step, (half, number) in enumerate(hidden_order):
        following = hidden_load(step + 1) if step + 1 < len(hidden_order) else None
        hidden_wait.wait()
        turned[0] = hidden[step % 2].T
        if half:
            if step % 2 in last_send:
                copies.sent(last_send[step % 2])
            sending[slot_rows(step % 2), :] = dot_nn(turned[0, columns, :], grad_ff[...]).astype(bf16)
            last_send[step % 2] = send_far(0, number, step % 2)
        else:
            arrived[0, number].wait_recv()
            pulled = pull(core_land.at[0, number], group)
            add_far(0, number, pulled, dot_nn(turned[0, columns, :], grad_ff[...]))
        hidden_wait = following

    parked.wait()
    low_mid_load.wait()
    order = hidden_order
    down_slots, gate_slot, up_slot = (0, 1), 2, 3

    def down_load(step):
        half, number = order[step]
        return load(down_all.at[half, number], weights.at[slot_rows(down_slots[step % 2])])

    def pre_load(step):
        half, number = order[step]
        return [load(gate_pre.at[half, number], pre.at[0]), load(up_pre.at[half, number], pre.at[1])]

    def pair_load(step):
        half, number = order[step]
        return [
            load(gate_all.at[half, number], weights.at[slot_rows(gate_slot)]),
            load(up_all.at[half, number], weights.at[slot_rows(up_slot)]),
        ]

    tile = rows // tile_cut
    tiles = row_total // tile
    down_wait = down_load(0)
    pre_wait = pre_load(0)
    pair_wait = pair_load(0)
    for step, (half, number) in enumerate(order):
        following = down_load(step + 1) if step + 1 < len(order) else None
        down_wait.wait()
        for copy in pre_wait:
            copy.wait()
        down_rows = slot_rows(down_slots[step % 2])

        def hidden_tile(at):
            place = pl.ds(at * tile, tile) if isinstance(at, int) else pl.ds(pl.multiple_of(at * tile, tile), tile)
            grad_hidden = dot_nt(grad_ff[place, :], weights[down_rows, :])
            value, slope = gelu_parts(pre[0, place, columns])
            slope_bufs[0, place, columns] = (grad_hidden * pre[1, place, columns] * slope).astype(bf16)
            slope_bufs[1, place, columns] = (grad_hidden * value).astype(bf16)

        if ffn_unroll:
            for at in range(tiles):
                hidden_tile(at)
        else:
            pl.loop(0, tiles)(hidden_tile)

        if step == 2:
            after_one(0)
        if step == 4:
            after_two(0)
        down_wait = following
        pre_wait = pre_load(step + 1) if step + 1 < len(order) else ()
        pulled = []
        if not half:
            for at in (1, 2):
                arrived[at, number].wait_recv()
                pulled.append(pull(core_land.at[at, number], group))
        for which in range(2):
            turned[which] = slope_bufs[which].T
            at = 1 + which
            if half:
                if which in last_send:
                    copies.sent(last_send[which])
                sending[slot_rows(which), :] = dot_nn(
                    turned[which, columns, :], low_mid[...]
                ).astype(bf16)
                last_send[which] = send_far(at, number, which)
            else:
                if at == 1 and number % 2:
                    copies.sent(one[0, number // 2])
                if at == 2 and number % 2 == 0:
                    copies.sent(two[0, number // 2])
                add_far(at, number, pulled[which], dot_nn(turned[which, columns, :], low_mid[...]))
        for copy in pair_wait:
            copy.wait()

        def mid_tile(at):
            place = pl.ds(at * tile, tile) if isinstance(at, int) else pl.ds(pl.multiple_of(at * tile, tile), tile)
            term = dot_nn(slope_bufs[0, place, columns], weights[slot_rows(gate_slot), :]) + dot_nn(
                slope_bufs[1, place, columns], weights[slot_rows(up_slot), :]
            )
            total[place, :] = term if step == 0 else total[place, :] + term

        if mid_unroll:
            for at in range(tiles):
                mid_tile(at)
        else:
            pl.loop(0, tiles)(mid_tile)

        pair_wait = pair_load(step + 1) if step + 1 < len(order) else ()
        if step == 6:
            after_one(1, (0,))
        if step == 7:
            after_one(1, (1,))
            after_planes(0)

    row_ahead((after_in, tokens_out))

    qkv_place, proj_place = pl.ds(0, 3 * inner), pl.ds(3 * inner, inner)
    projected_place = pl.ds(4 * inner, row_total)
    qkv_load = load(qkv_in, weights.at[qkv_place])
    proj_load = load(proj_in, weights.at[proj_place])
    projected = weights.at[projected_place, pl.ds(0, 3 * inner)]
    projected_load = load(projected_in, projected)
    mixed = hidden.at[0, :, pl.ds(0, inner)]
    mixed_load = load(mixed_in, mixed)
    far_load = load(far_in, far)
    tokens_load = load(tokens_in, low_mid)
    def middle(place, slot, part):
        slope, gain_part = norm_slope(rowbuf[0, slot, part], gains[pl.ds(1, 1), :], total[place, :])
        grad = rowbuf[1, slot, part] + slope
        total[place, :] = grad
        grad_ff[place, :] = grad.astype(bf16)
        gain_sums[pl.ds(8, 8), :] += fold_rows(gain_part, jnp.sum)

    row_stream((after_in, tokens_out), middle)
    after_one(2)
    parked = pltpu.make_async_copy(total, tokens_out, park.at[0])
    parked.start()
    grads = slope_bufs.at[1, :, pl.ds(0, inner)]
    proj_load.wait()
    for place in rows_of(row_total, rows):
        grads[place, :] = dot_nt(grad_ff[place, :], weights[proj_place, :]).astype(bf16)
    mixed_load.wait()
    weights[proj_place, :] = dot_tn(mixed[...], grad_ff[...]).astype(bf16)
    low_in_load = load(low_in_in, grad_ff)
    after_last(0)
    projected_load.wait()
    far_load.wait()
    parked.wait()

    probs = total.at[:, pl.ds(2 * inner, rows)]
    slopes = pre.at[0, :, pl.ds(0, rows)]
    low = slope_bufs.at[0, :, pl.ds(0, rows)]
    for pair in range(pairs):
        for head in range(2):
            for half in range(2):
                strip = strip_of(diag_ref[pl.ds(4 * pair + 2 * head + half, 1), :], 2 * rows)
                for side in range(2):
                    pre[1, pl.ds((4 * head + 2 * half + side) * strip_rows, strip_rows), pl.ds(0, rows)] = (
                        strip[:, side * rows : (side + 1) * rows]
                    )

        def window(head, half, start):
            first = (4 * head + 2 * half) * strip_rows
            found = pre[1, pl.ds(first, strip_rows), pl.ds(start, rows - start)]
            if start:
                found = jnp.concatenate(
                    [found, pre[1, pl.ds(first + strip_rows, strip_rows), pl.ds(0, start)]], axis=1
                )
            return found

        strip_sum[...] = jnp.zeros_like(strip_sum)

        @pl.loop(0, seqs)
        def _(seq):
            attend_back_pair(
                valid_ref, seq, pair, projected, far, window, stat, grads, probs, slopes, low,
                strip_sum, halves, total, hidden, rows, inner,
            )

        span = 2 * rows
        for head in range(2):
            for half in range(2):
                skew = strip_sum[head, :, pl.ds(half * span, span)]
                row = lax.broadcasted_iota(jnp.int32, skew.shape, 0)
                step = 1
                while step < strip_rows:
                    skew = jnp.where(row & step != 0, pltpu.roll(skew, span - step, 1), skew)
                    step = 2 * step
                diag[pl.ds(2 * pair + head, 1), pl.ds(half * span, span)] = jnp.sum(
                    skew, axis=0, keepdims=True
                )
        if pair == 0:
            after_two(1)
        if pair == 1:
            after_two(2)
    after_planes(1)
    swap = [
        copies.start(hidden.at[which, :, pl.ds(0, inner)], kv_land.at[which], 0) for which in range(2)
    ]
    for which in range(2):
        swap[which].wait_recv()
    kv_loads = [
        load(kv_land.at[which], far.at[:, pl.ds(which * inner, inner)]) for which in range(2)
    ]
    for which in range(2):
        kv_loads[which].wait()
        for place in rows_of(row_total, rows):
            to = pl.ds(which * inner, inner)
            projected[place, pl.ds((which + 1) * inner, inner)] = (
                total[place, to] + far[place, to].astype(f32)
            ).astype(bf16)

    after_planes(2)

    low_in_load.wait()
    for at, half in ((1, 0), (1, 1), (2, 0), (2, 1)):
        copies.sent(one[at, half])
    out_size = inner // (2 * count)
    cut = row_total - inner
    total[pl.ds(cut, inner), :] = weights[proj_place, :].astype(f32)
    first_blocks = cut // qkv_rows
    for base, begin, end in ((0, 0, first_blocks), (3 * inner - cut, first_blocks, 2 * count)):
        for to in range(0, cut, cut // 2 // strip_rows * strip_rows):
            size = min(cut // 2 // strip_rows * strip_rows, cut - to)
            total[pl.ds(to, size), :] = dot_tn(projected[:, pl.ds(base + to, size)], grad_ff[...])
        for at in range(begin, end):
            rowbuf[0, 0, pl.ds(0, qkv_rows), :] = total[pl.ds(at * qkv_rows - base, qkv_rows), :]
            rowbuf[0, 0, pl.ds(qkv_rows, out_size), :] = total[pl.ds(cut + at * out_size, out_size), :]
            sums[pl.ds(at * block, block), :] = rowbuf[0, 0, pl.ds(0, block), :].astype(bf16)

    def piece_row(half, at, core):
        far_bit, near_bit, plane = at // (2 * part), at // part % 2, at % part
        bits = turns[half][0] * far_bit + turns[half][1] * near_bit + 4 * (half * part + plane)
        return pl.multiple_of((flip(dp, bits) * 2 + core) * block, 16)

    every = [(half, at) for half in range(2) for at in range(4 * part)]
    core_waits = [
        copies.start(
            sums.at[pl.ds(piece_row(half, at, 1 - ctx), block)],
            mixed_core.at[pl.ds(step * block, block)],
            0,
        )
        for step, (half, at) in enumerate(every)
    ]
    for at in (0, 1):
        copies.sent(last_send[at])
    for step, (half, at) in enumerate(every):
        sending[pl.ds(step * block, block), :] = sums[pl.ds(piece_row(half, at, ctx), block), :]
    for copy in core_waits:
        copy.wait_recv()
    span = 4 * part * block
    copy = pltpu.make_async_copy(mixed_core, staging.at[pl.ds(0, 2 * span)], stage.at[0])
    copy.start()
    copy.wait()
    add_rows(sending, 0, staging, 0, 2 * span)
    mixed_ones = [
        copies.start(
            sending.at[pl.ds(half * span + span // 2, span // 2)], mixed_one.at[half], turns[half][0]
        )
        for half in range(2)
    ]

    qkv_load.wait()

    @pl.loop(0, tiles)
    def _(at):
        place = pl.ds(pl.multiple_of(at * tile, tile), tile)
        total[place, :] = dot_nn(projected[place, :], weights[qkv_place, :])

    after_last(1)
    for half in range(2):
        mixed_ones[half].wait_recv()
    copies_in = [
        pltpu.make_async_copy(
            mixed_one.at[half], staging.at[pl.ds(half * span, span // 2)], stage.at[half]
        )
        for half in range(2)
    ]
    for copy in copies_in:
        copy.start()
    mixed_twos = []
    for half in range(2):
        copies_in[half].wait()
        add_rows(sending, half * span, staging, half * span, span // 2)
        mixed_twos.append(
            copies.start(
                sending.at[pl.ds(half * span + span // 4, span // 4)], mixed_two.at[half], turns[half][1]
            )
        )
    tokens_load.wait()

    def first_norm(place, slot, part):
        slope, gain_part = norm_slope(
            low_mid[place, :].astype(f32), gains[pl.ds(0, 1), :], total[place, :]
        )
        total[place, :] = rowbuf[0, slot, part] + slope
        gain_sums[pl.ds(0, 8), :] += fold_rows(gain_part, jnp.sum)

    row_ahead((tokens_out,))
    row_stream((tokens_out,), first_norm)
    parked = pltpu.make_async_copy(total, tokens_out, park.at[0])
    parked.start()
    for half in range(2):
        mixed_twos[half].wait_recv()
    copies_in = [
        pltpu.make_async_copy(
            mixed_two.at[half], staging.at[pl.ds(half * span, span // 4)], stage.at[half]
        )
        for half in range(2)
    ]
    for copy in copies_in:
        copy.start()
    for half in range(2):
        copies_in[half].wait()
        add_rows(sending, half * span, staging, half * span, span // 4)
    copies.sent(mixed_twos[0])
    quarter = span // 4
    for at in range(0, quarter, 16):
        sending[pl.ds(quarter + at, 16), :] = sending[pl.ds(span + at, 16), :]
    mixed_lasts = {}
    send_planes(sending, 0, block, mixed_last, 1, mixed_lasts)
    after_last(2)

    for seq in range(seqs):
        wide = jnp.broadcast_to(gate_column[pl.ds(seq * rows, rows), :], (rows, strip_rows))
        gate_values[pl.ds(seq, 1), :] = wide.T[:1, :]

    small[0] = jnp.zeros(small.shape[1:], f32)
    for at in range(4):
        small[0, pl.ds(at, 1), :] = jnp.sum(gain_sums[pl.ds(8 * at, 8), :], axis=0, keepdims=True)
    bucket = jnp.concatenate([diagonal_buckets(rows, half) for half in range(2)], axis=1)
    number = lax.broadcasted_iota(jnp.int32, (strip_rows, 4 * rows), 0)
    table = lax.dot_general(
        diag[...],
        (jnp.broadcast_to(bucket, number.shape) == number).astype(f32),
        (((1,), (1,)), ((), ())),
        precision=lax.Precision.HIGHEST,
        preferred_element_type=f32,
    )
    for at in range(2):
        small[0, pl.ds(4, 4), pl.ds(at * 128, 128)] = table[4 * at : 4 * at + 4, :]
    def small_round(step, bits):
        copy = copies.start(small.at[2 * step], small.at[2 * step + 1], bits)
        copy.wait_recv()
        small[2 * step + 2] = small[2 * step] + small[2 * step + 1]

    rounds = butterfly(count)
    for step in range(3):
        small_round(step, rounds[step])
    bit = 1
    while 2 * bit < planes:
        for plane in range(bit, planes, 2 * bit):
            mixed_lasts[plane].wait_recv()
            copy = pltpu.make_async_copy(
                mixed_last.at[pl.ds((plane - 1) * block, block)],
                staging.at[pl.ds(0, block)],
                stage.at[0],
            )
            copy.start()
            copy.wait()
            add_rows(sending, (plane - bit) * block, staging, 0, block)
        bit = 2 * bit
        send_planes(sending, 0, block, mixed_last, bit, mixed_lasts)
    for step in range(3, len(rounds)):
        small_round(step, rounds[step])
    small_sum[...] = small[2 * len(butterfly(count))]
    plane = planes // 2
    mixed_lasts[plane].wait_recv()
    copy = pltpu.make_async_copy(
        mixed_last.at[pl.ds((plane - 1) * block, block)], staging.at[pl.ds(0, block)], stage.at[0]
    )
    copy.start()
    copy.wait()
    mixed_sum[...] = sending[pl.ds(0, block), :].astype(f32) + staging[pl.ds(0, block), :].astype(f32)
    parked.wait()
    copies.finish()


def back(
    lengths, diagonal, gate_grad, gains, stat, arrays, qkv_rows, block, sizes, count
):
    seqs, rows, heads, inner = sizes
    total, model = arrays[1].shape
    planes = count // 4
    part = planes // 2
    group = arrays[-4].shape[2]
    piece = group // (2 * part)
    wide = max(rows, group)
    rounds = len(butterfly(count))
    number = 3 * (4 + 4 + planes - 1) + 2 + 8 * part + 4 + planes - 1 + rounds
    any_space = pl.BlockSpec(memory_space=pl.ANY)
    vmem = pl.BlockSpec(memory_space=pltpu.VMEM)
    shape = jax.ShapeDtypeStruct
    landing = [
        (3, 4, group, model),
        (3, 2, group, model),
        (3, 2, part * piece, model),
        (3, (planes - 1) * piece, model),
        (2, total, inner),
        (8 * part * block, model),
        (2, 2 * part * block, model),
        (2, part * block, model),
        ((planes - 1) * block, model),
    ]
    thin = row_thin
    return pl.pallas_call(
        functools.partial(back_kernel, count, qkv_rows),
        in_specs=[pl.BlockSpec(memory_space=pltpu.SMEM)] + [vmem] * 4 + [any_space] * len(arrays),
        out_specs=[vmem, any_space] + [vmem] * 5 + [any_space] * len(landing),
        out_shape=[
            shape((seqs, rows), f32),
            shape((total, model), f32),
            shape((block, model), f32),
            shape((8, model), f32),
            shape((piece, model), f32),
            shape((piece, model), f32),
            shape((piece, model), f32),
        ]
        + [shape(at, bf16) for at in landing],
        scratch_shapes=[
            pltpu.VMEM((total, model), f32),
            pltpu.VMEM((total, model), bf16),
            pltpu.VMEM((total, model), bf16),
            pltpu.VMEM((max(4 * inner + total, 4 * group), model), bf16),
            pltpu.VMEM((2, total, wide), f32),
            pltpu.VMEM((2, total, wide), bf16),
            pltpu.VMEM((2, total, wide), bf16),
            pltpu.VMEM((2, wide, total), bf16),
            pltpu.VMEM((2 * group, model), bf16),
            pltpu.VMEM((8 * group, model), bf16),
            pltpu.VMEM((2 * group, model), bf16),
            pltpu.VMEM((2 * group, model), bf16),
            pltpu.VMEM((2, 2 * rows, strip_rows), f32),
            pltpu.VMEM((total, 2 * inner), bf16),
            pltpu.VMEM((2, strip_rows, 4 * rows), f32),
            pltpu.VMEM((2, row_depth, thin, model), f32),
            pltpu.VMEM((2 * rounds + 1, 8, model), f32),
            pltpu.VMEM((8, 4 * rows), f32),
            pltpu.VMEM((32, model), f32),
            pltpu.VMEM((total, 1), f32),
            pltpu.SemaphoreType.DMA((number,)),
            pltpu.SemaphoreType.DMA((number,)),
            pltpu.SemaphoreType.DMA((80,)),
            pltpu.SemaphoreType.DMA((2,)),
            pltpu.SemaphoreType.DMA((2, row_depth)),
            pltpu.SemaphoreType.DMA((1,)),
        ],
        compiler_params=pltpu.CompilerParams(
            collective_id=1, has_side_effects=True, vmem_limit_bytes=63 * 2**20
        ),
    )(lengths, diagonal, gate_grad, gains, stat, *arrays)[:7]


def turn_kernel(first_in, second_in, first_out, second_out):
    first_out[0] = first_in[...].T
    second_out[0] = second_in[...].T


def turn(first, second, seqs):
    total, model = first.shape
    steps = total // seqs // strip_rows
    by_rows = pl.BlockSpec((strip_rows, model), lambda seq, at: (seq * steps + at, 0))
    by_lanes = pl.BlockSpec((1, model, strip_rows), lambda seq, at: (seq, 0, at))
    return pl.pallas_call(
        turn_kernel,
        grid=(seqs, steps),
        in_specs=[by_rows] * 2,
        out_specs=[by_lanes] * 2,
        out_shape=[jax.ShapeDtypeStruct((seqs, model, total // seqs), f32)] * 2,
        compiler_params=pltpu.CompilerParams(vmem_limit_bytes=60 * 2**20),
    )(first, second)


def per_device(
    tokens,
    lengths,
    qkv_weight,
    out_weight,
    gate_weight,
    up_weight,
    down_weight,
    norm_gains,
    delete_weight,
    bias_table,
    out_grad,
    gate_grad,
):
    seqs, rows, model = tokens.shape
    dp_count = lax.axis_size("dp")
    buckets, heads = bias_table.shape
    shard = model // dp_count
    qkv_rows, out_rows = qkv_weight.shape[1], out_weight.shape[0]
    inner = 2 * dp_count * out_rows
    block = -(-(qkv_rows + out_rows) // 16) * 16
    sizes = (seqs, rows, heads, inner)

    def padded(matrix):
        return jnp.pad(matrix, ((0, -matrix.shape[0] % 16), (0, 0)))

    (
        gate_all,
        up_all,
        down_all,
        low_in,
        projected,
        far_kv,
        mixed,
        stats,
        after_attn,
        low_mid,
        gains,
        qkv_t,
        out_full,
        gate_pre_all,
        up_pre_all,
        hidden_all,
        block_out,
        diagonal,
        out_grad_rows,
        token_rows,
    ) = front(
        lengths,
        bias_table,
        tokens.transpose(0, 2, 1),
        norm_gains,
        delete_weight.reshape(1, shard),
        qkv_weight.T,
        out_weight,
        out_grad.transpose(0, 2, 1),
        padded(gate_weight.T),
        padded(up_weight.T),
        padded(down_weight),
        block,
        sizes,
        dp_count,
    )
    gate_values, tokens_grad, mixed_sum, small_sum, gate_sum, up_sum, down_sum = back(
        lengths,
        diagonal,
        gate_grad,
        gains,
        stats,
        (
            token_rows,
            out_grad_rows,
            block_out,
            after_attn,
            low_in,
            low_mid,
            projected,
            far_kv,
            mixed,
            qkv_t,
            out_full,
            gate_all,
            up_all,
            down_all,
            gate_pre_all,
            up_pre_all,
            hidden_all,
        ),
        qkv_rows,
        block,
        sizes,
        dp_count,
    )
    anchor = lax.axis_index("dp") * shard
    ff_rows = down_weight.shape[0]
    table = jnp.concatenate([small_sum[4:8, :buckets], small_sum[4:8, 128 : 128 + buckets]])
    block_turned, tokens_turned = turn(block_out, tokens_grad, seqs)
    return (
        block_turned.transpose(0, 2, 1),
        gate_values,
        tokens_turned.transpose(0, 2, 1),
        mixed_sum[:qkv_rows].T,
        mixed_sum[qkv_rows : qkv_rows + out_rows],
        gate_sum[:ff_rows].T,
        up_sum[:ff_rows].T,
        down_sum[:ff_rows],
        lax.dynamic_slice_in_dim(small_sum[:3], anchor, shard, 1),
        lax.dynamic_slice_in_dim(small_sum[3], anchor, shard, 0),
        table[:heads].T,
    )


def solution(mesh):
    wide = P("dp", "ctx", None)
    columns = P(None, ("dp", "ctx"))
    depth = P(("dp", "ctx"), None)
    return jax.shard_map(
        per_device,
        mesh=mesh,
        in_specs=(
            wide,
            P("dp"),
            columns,
            depth,
            columns,
            columns,
            depth,
            P(None, "dp"),
            P("dp"),
            P(),
            wide,
            P("dp", "ctx"),
        ),
        out_specs=(
            wide,
            P("dp", "ctx"),
            wide,
            columns,
            depth,
            columns,
            columns,
            depth,
            P(None, "dp"),
            P("dp"),
            P(),
        ),
        check_vma=False,
    )
```

```python
import functools

import jax
import jax.numpy as jnp
from jax import lax
from jax.experimental import pallas as pl
from jax.experimental.pallas import tpu as pltpu
from jax.sharding import PartitionSpec as P

norm_eps = 1e-06
masked_score = -1e30
delete_scale = -30.0
bucket_edges = (12, 16, 23, 32, 46, 64, 91)
f32 = jnp.float32
bf16 = jnp.bfloat16
strip_rows = 128
fine_rows = 128
fine_unroll = 1
row_depth = 3
ffn_unroll = 0
mid_unroll = 0
tile_cut = 1
row_thin = 64


def bucket_of(offset):
    distance = jnp.abs(offset)
    far_bucket = 8 + sum(((distance >= boundary).astype(jnp.int32) for boundary in bucket_edges))
    near_bucket = jnp.where(distance < 8, distance, jnp.minimum(far_bucket, 15))
    return near_bucket + jnp.where(offset > 0, 16, 0)


def dot_nt(left, right):
    return lax.dot_general(left, right, (((1,), (1,)), ((), ())), preferred_element_type=f32)


def dot_nn(left, right):
    return lax.dot_general(left, right, (((1,), (0,)), ((), ())), preferred_element_type=f32)


def dot_tn(left, right):
    return lax.dot_general(left, right, (((0,), (0,)), ((), ())), preferred_element_type=f32)


def swap_ctx(block):
    return lax.ppermute(block, "ctx", [(0, 1), (1, 0)])


def head_lanes(block, head, width):
    lane = lax.broadcasted_iota(jnp.int32, block.shape, 1)
    return jnp.where(lane // width == head, block, jnp.zeros_like(block))


def fold_rows(block, op):
    return op(block.reshape(block.shape[0] // 8, 8, block.shape[1]), axis=0)


def flip(at, bits):
    bit = 1
    while bit <= bits:
        if bits & bit:
            at = at + bit - 2 * bit * (at // bit % 2)
        bit = 2 * bit
    return at


class Copies:
    def __init__(self, count, send, recv):
        self.send, self.recv, self.made, self.done = send, recv, [], set()
        self.dp, self.ctx = lax.axis_index("dp"), lax.axis_index("ctx")
        self.where = {0: {"ctx": 1 - self.ctx}}
        for bits in [1, 2] + [4 * step for step in range(1, count // 4)]:
            self.where[bits] = {"dp": flip(self.dp, bits)}

    def start(self, source, target, bits):
        at = len(self.made)
        copy = pltpu.make_async_remote_copy(
            src_ref=source,
            dst_ref=target,
            send_sem=self.send.at[at],
            recv_sem=self.recv.at[at],
            device_id=self.where[bits],
            device_id_type=pl.DeviceIdType.MESH,
        )
        copy.start()
        self.made.append(copy)
        return copy

    def sent(self, copy):
        if id(copy) not in self.done:
            copy.wait_send()
            self.done.add(id(copy))

    def finish(self):
        for copy in self.made:
            self.sent(copy)


def greet(count):
    barrier = pltpu.get_barrier_semaphore()
    dp, ctx = lax.axis_index("dp"), lax.axis_index("ctx")
    bits = [1, 2] + [4 * step for step in range(1, count // 4)]
    for at in bits:
        pl.semaphore_signal(
            barrier, inc=1, device_id={"dp": flip(dp, at)}, device_id_type=pl.DeviceIdType.MESH
        )
    pl.semaphore_signal(
        barrier, inc=1, device_id={"ctx": 1 - ctx}, device_id_type=pl.DeviceIdType.MESH
    )


def meet(count):
    pl.semaphore_wait(pltpu.get_barrier_semaphore(), 2 + count // 4)


def rows_of(total, size):
    return [pl.ds(at, size) for at in range(0, total, size)]


def diagonal_buckets(rows, half):
    place = lax.broadcasted_iota(jnp.int32, (1, 2 * rows), 1)
    lane = jnp.where(place >= 2 * rows - strip_rows, place - 2 * rows, place)
    shift = rows * (1 - 2 * lax.axis_index("ctx")) if half else 0
    return bucket_of((rows - strip_rows) - lane + shift)


def valid_keys(lengths, seq, half, rows):
    ctx = lax.axis_index("ctx")
    return lengths[seq] - rows * (1 - ctx if half else ctx)


def strip_of(diagonal, span):
    wide = jnp.broadcast_to(diagonal, (strip_rows, span))
    return pltpu.roll(wide, 0, 1, stride=1, stride_axis=0)


def fill_strips(strips, diag_ref, pair, span):
    for head in range(2):
        for half in range(2):
            strips[head, :, pl.ds(half * span, span)] = strip_of(
                diag_ref[pl.ds(4 * pair + 2 * head + half, 1), :], span
            )


def score_block(valid_ref, seq, keys, query, strips, head, half, at, rows):
    start = half * strips.shape[2] // 2 + rows - strip_rows - at
    scores = dot_nt(keys, query) + strips[head, :, pl.ds(start, rows)]
    place = at + lax.broadcasted_iota(jnp.int32, scores.shape, 0)
    return jnp.where(place < valid_keys(valid_ref, seq, half, rows), scores, masked_score)


def lanes(first):
    return pl.ds(first, strip_rows)


def attend_pair(valid_ref, seq, pair, projected, far, strips, mixed_ref, stat_ref, work, probs, rows, inner):
    width = strip_rows // 2
    seq_rows = pl.ds(pl.multiple_of(seq * rows, rows), rows)
    first = strip_rows * pair
    queries = projected[seq_rows, lanes(first)]
    outs = []
    for head in range(2):
        query = head_lanes(queries, head, width)
        top = jnp.full((8, rows), masked_score, f32)
        for half, (source, base) in enumerate(((projected, inner), (far, 0))):
            for at in range(0, rows, strip_rows):
                keys = source[pl.ds(pl.multiple_of(seq * rows + at, strip_rows), strip_rows), lanes(base + first)]
                scores = score_block(
                    valid_ref, seq, keys, query, strips, head, half, at, rows
                )
                work[pl.ds(half * rows + at, strip_rows), :] = scores
                top = jnp.maximum(top, fold_rows(scores, jnp.max))
        row_max = jnp.max(top, axis=0, keepdims=True)
        total = jnp.zeros((8, rows), f32)
        for at in range(0, 2 * rows, strip_rows):
            exponent = jnp.exp(work[pl.ds(at, strip_rows), :] - row_max)
            work[pl.ds(at, strip_rows), :] = exponent
            total = total + fold_rows(exponent, jnp.sum)
        row_sum = jnp.sum(total, axis=0, keepdims=True)
        share = 1.0 / row_sum
        for at in range(0, 2 * rows, strip_rows):
            probs[pl.ds(at, strip_rows), :] = (work[pl.ds(at, strip_rows), :] * share).astype(bf16)
        stat_ref[seq, pair, pl.ds(head, 1), :] = row_max + jnp.log(row_sum)
        mixed = dot_tn(
            projected[seq_rows, lanes(2 * inner + first)], probs[pl.ds(0, rows), :]
        ) + dot_tn(far[seq_rows, lanes(inner + first)], probs[pl.ds(rows, rows), :])
        outs.append(mixed[head * width : (head + 1) * width, :])
    mixed_ref[seq_rows, lanes(first)] = jnp.concatenate(outs, axis=0).T.astype(bf16)


def gelu_parts(value):
    inner = 0.7978845608028654 * (value + 0.044715 * value * value * value)
    slope = 0.7978845608028654 * (1.0 + 3.0 * 0.044715 * value * value)
    tanh = jnp.tanh(inner)
    half = 0.5 * (1.0 + tanh)
    return value * half, half + 0.5 * value * (1.0 - tanh * tanh) * slope


def front_kernel(
    count,
    qkv_rows,
    valid_ref,
    table_ref,
    tokens_ref,
    gains_in,
    delete_in,
    qkv_in,
    proj_in,
    out_grad_in,
    gate_in,
    up_in,
    down_in,
    gate_all,
    up_all,
    down_all,
    low_in_out,
    projected_out,
    far_out,
    mixed_out,
    stat_out,
    after_out,
    low_mid_out,
    gains_out,
    qkv_out,
    proj_out,
    gate_pre_out,
    up_pre_out,
    hidden_out,
    block_out,
    diag_out,
    out_grad_out,
    tokens_out,
    small_in,
    mixed_in,
    diag_ref,
    small_all,
    mixed_all,
    low_in,
    projected,
    far,
    mixed,
    stat,
    total,
    low_mid,
    gains,
    qkv,
    proj,
    strips,
    probs,
    weights,
    gate_buf,
    up_buf,
    hidden,
    send,
    recv,
    local,
    flush,
    fetch,
    store,
    here_sem,
):
    planes = count // 4
    part = planes // 2
    piece = gate_in.shape[0]
    model = total.shape[1]
    row_total = total.shape[0]
    seqs, pairs = stat.shape[:2]
    rows = row_total // seqs
    inner = proj.shape[0]
    group = gate_all.shape[2]
    shard = model // count
    greet(count)
    small_in[...] = jnp.zeros_like(small_in)
    small_in[pl.ds(0, 3), pl.ds(0, shard)] = gains_in[...]
    small_in[pl.ds(3, 1), pl.ds(0, shard)] = delete_in[...].astype(f32)
    out_rows = proj_in.shape[0]
    total[pl.ds(0, mixed_in.shape[0]), :] = jnp.zeros(mixed_in.shape, f32)
    total[pl.ds(0, qkv_rows), :] = qkv_in[...].astype(f32)
    total[pl.ds(qkv_rows, out_rows), :] = proj_in[...].astype(f32)
    mixed_in[...] = total[pl.ds(0, mixed_in.shape[0]), :].astype(bf16)
    meet(count)
    copies = Copies(count, send, recv)
    dp, ctx = copies.dp, copies.ctx
    z, y, x = dp // 4, dp // 2 % 2, dp % 2
    near = pl.ds(z // part * part, part)
    away = pl.ds((1 - z // part) * part, part)
    matrices = ((gate_in, gate_all), (up_in, up_all), (down_in, down_all))
    here = [
        pltpu.make_async_copy(source, target, local.at[at])
        for at, (source, target) in enumerate(
            (
                (mixed_in, mixed_all.at[z, y, x, ctx]),
                (small_in, small_all.at[z, y, x]),
            )
            + tuple((source, target.at[0, 0, pl.ds(0, piece)]) for source, target in matrices)
        )
    ]
    for copy in here:
        copy.start()
    flushed = []

    def put(source, target):
        copy = pltpu.make_async_copy(source, target, flush.at[len(flushed)])
        copy.start()
        flushed.append(copy)

    def arrive(found):
        for copy in found:
            copy.wait_recv()

    bits_down = [1 << at for at in range(planes.bit_length() - 1)][::-1]

    def plane_place(target, plane):
        return target.at[0, 2 * (plane // part), pl.ds(plane % part * piece, piece)]

    def planes_start(source, target):
        return {
            bit: copies.start(source, plane_place(target, bit), 4 * bit) for bit in bits_down
        }

    def planes_rest(target, found):
        for bit in bits_down[:-1]:
            for plane in range(bit, planes, 2 * bit):
                found[plane].wait_recv()
                found[-plane] = None
                for lower in bits_down:
                    if lower < bit:
                        place = plane_place(target, plane)
                        found[plane + lower] = copies.start(
                            place, plane_place(target, plane + lower), 4 * lower
                        )

    def planes_arrive(found, planes_wanted):
        for plane in planes_wanted:
            if plane and -plane not in found:
                found[plane].wait_recv()
                found[-plane] = None

    def first_turn(target, found):
        low, high = pl.ds(0, part * piece), pl.ds(part * piece, part * piece)
        turns = []
        for half, (at, bits) in enumerate(((0, 2), (2, 1))):
            planes_arrive(found, range(half * part, (half + 1) * part))
            turns.append(copies.start(target.at[0, at, low], target.at[0, at, high], bits))
        return turns

    def second_turn(target):
        return [
            copies.start(target.at[0, at], target.at[0, at + 1], bits)
            for at, bits in ((0, 1), (2, 2))
        ]

    def core_turn(target, late):
        return [
            copies.start(target.at[0, at + late], target.at[1, at + late], 0) for at in (0, 2)
        ]

    small_waits = [
        copies.start(small_in, small_all.at[z, y, x], 4 * step) for step in range(1, planes)
    ]
    waits = {
        bit: copies.start(mixed_in, mixed_all.at[z, y, x, ctx], 4 * bit) for bit in bits_down
    }
    for bit in bits_down[:-1]:
        for plane in range(bit, planes, 2 * bit):
            waits[plane].wait_recv()
            for lower in bits_down:
                if lower < bit:
                    place = mixed_all.at[flip(z, plane), y, x, ctx]
                    waits[plane + lower] = copies.start(place, place, 4 * lower)
    plane_waits = [planes_start(*matrices[0])]

    work = gate_buf.at[0, :, pl.ds(0, rows)]
    for half in range(2):
        bucket = diagonal_buckets(rows, half)
        for head in range(2 * pairs):
            bias = jnp.zeros(bucket.shape, f32)
            for at in range(table_ref.shape[0]):
                bias = jnp.where(bucket == at, table_ref[at, head], bias)
            diag_ref[pl.ds(2 * head + half, 1), :] = bias
    put(diag_ref, diag_out)
    for copy in here:
        copy.wait()
    arrive(small_waits)
    small_turn = [copies.start(small_all.at[:, y, x], small_all.at[:, y, x], 2)]
    for plane in range(1, planes, 2):
        waits[plane].wait_recv()
    turn = [
        copies.start(mixed_all.at[near, y, x, ctx], mixed_all.at[near, y, x, ctx], 2),
        copies.start(mixed_all.at[away, y, x, ctx], mixed_all.at[away, y, x, ctx], 1),
    ]
    arrive(small_turn)
    small_turn = [copies.start(small_all.at[:, :, x], small_all.at[:, :, x], 1)]
    arrive(turn)
    turn = [
        copies.start(mixed_all.at[near, :, x, ctx], mixed_all.at[near, :, x, ctx], 1),
        copies.start(mixed_all.at[away, y, :, ctx], mixed_all.at[away, y, :, ctx], 2),
    ]
    planes_rest(gate_all, plane_waits[0])
    plane_waits.append(planes_start(*matrices[1]))
    arrive(small_turn)
    padded = -(-model // 128) * 128
    lane = lax.broadcasted_iota(jnp.int32, (8, 128), 1)
    found = jnp.zeros((8, padded), f32)
    for at in range(count):
        block = jnp.where(lane < shard, small_all[at // 4, at // 2 % 2, at % 2], 0.0)
        block = jnp.concatenate([block, jnp.zeros((8, padded - 128), f32)], axis=1)
        found = found + (pltpu.roll(block, at * shard, 1) if at else block)
    gains[...] = found[:, :model]
    put(gains, gains_out)

    def token_rows(at, size):
        columns = pl.ds(pl.multiple_of(at % (rows // size) * size, size), size)
        return tokens_ref[at // (rows // size), :, columns].astype(f32).T

    @pl.loop(0, row_total // strip_rows)
    def _(at):
        place = pl.ds(pl.multiple_of(at * strip_rows, strip_rows), strip_rows)
        value = token_rows(at, strip_rows)
        scale = lax.rsqrt(jnp.mean(value * value, axis=1, keepdims=True) + norm_eps)
        low_in[place, :] = (value * scale * gains[pl.ds(0, 1), :]).astype(bf16)

    low_in_put = len(flushed)
    put(low_in, low_in_out)
    first = first_turn(gate_all, plane_waits[0])
    arrive(turn)
    turn = [copies.start(mixed_all.at[:, :, :, ctx], mixed_all.at[:, :, :, ctx], 0)]
    planes_rest(up_all, plane_waits[1])
    plane_waits.append(planes_start(*matrices[2]))
    arrive(turn)
    block_rows = mixed_in.shape[0]
    for target, begin, size in ((qkv, 0, qkv_rows), (proj, qkv_rows, inner // (2 * count))):
        batch = min(2 * count, row_total // size // 16 * 16)
        for base in range(0, 2 * count, batch):
            for at in range(base, min(base + batch, 2 * count)):
                block = mixed_all[at // 8, at // 4 % 2, at // 2 % 2, at % 2].astype(f32)
                total[pl.ds((at - base) * size, size), :] = block[begin : begin + size, :]
            number = min(batch, 2 * count - base) * size
            target[pl.ds(base * size, number), :] = total[pl.ds(0, number), :].astype(bf16)
    put(qkv, qkv_out)
    put(proj, proj_out)
    for place in rows_of(row_total, rows):
        for to in rows_of(3 * inner, inner):
            projected[place, to] = dot_nt(low_in[place, :], qkv[to, :]).astype(bf16)
    put(projected, projected_out)
    swap = [copies.start(projected.at[:, pl.ds(inner, 2 * inner)], far, 0)]
    arrive(first)
    cores = core_turn(gate_all, 0)
    second = second_turn(gate_all)
    arrive(swap)
    put(far, far_out)
    stat[...] = jnp.zeros_like(stat)
    for pair in range(pairs):
        fill_strips(strips, diag_ref, pair, 2 * rows)

        @pl.loop(0, seqs)
        def _(seq):
            attend_pair(
                valid_ref, seq, pair, projected, far, strips, mixed, stat, work, probs, rows, inner
            )

        if pair == 0:
            first = first_turn(up_all, plane_waits[1])
            planes_rest(down_all, plane_waits[2])
    put(mixed, mixed_out)
    put(stat, stat_out)

    flushed[low_in_put].wait()
    for at, place in enumerate(rows_of(row_total, rows // 2)):
        value = token_rows(at, rows // 2)
        low_in[place, :] = value.astype(bf16)
        value = value + dot_nn(mixed[place, :], proj[...])
        total[place, :] = value
        scale = lax.rsqrt(jnp.mean(value * value, axis=1, keepdims=True) + norm_eps)
        low_mid[place, :] = (value * scale * gains[pl.ds(1, 1), :]).astype(bf16)
    put(total, after_out)
    put(low_mid, low_mid_out)

    tokens_put = len(flushed)
    put(low_in, tokens_out)
    flushed[tokens_put].wait()
    cut = min(row_total, model)
    for seq in range(seqs):
        for begin in range(0, model, cut):
            size = min(cut, model - begin)
            copy = pltpu.make_async_copy(
                out_grad_in.at[seq, pl.ds(begin, size)],
                hidden.at[seq, begin // cut, pl.ds(0, size), pl.ds(0, rows)],
                here_sem.at[seq, begin // cut],
            )
            copy.start()
            copy.wait()
            for lane in rows_of(rows, strip_rows):
                low_in[pl.ds(seq * rows + lane.start, strip_rows), pl.ds(begin, size)] = (
                    hidden[seq, begin // cut, pl.ds(0, size), lane].T
                )
    put(low_in, out_grad_out)

    columns = pl.ds(0, group)

    def stream(order, target, body, extra=None):
        def get(at, slot):
            half, number = order[at]
            found = [
                pltpu.make_async_copy(target.at[half, number], weights.at[slot], fetch.at[0, slot])
            ]
            if extra is not None:
                found.append(
                    pltpu.make_async_copy(
                        extra.at[half, number], gate_buf.at[slot], fetch.at[1, slot]
                    )
                )
            for copy in found:
                copy.start()
            return found

        waiting = get(0, 0)
        for at, (half, number) in enumerate(order):
            following = get(at + 1, (at + 1) % 2) if at + 1 < len(order) else None
            for copy in waiting:
                copy.wait()
            body(at, half, number, at % 2)
            waiting = following

    pending = {}

    def settle(slot):
        for copy in pending.pop(slot, ()):
            copy.wait()

    def gate_body(at, half, number, slot):
        settle(slot)
        for place in rows_of(row_total, rows):
            gate_buf[slot, place, columns] = dot_nt(low_mid[place, :], weights[slot])
        copy = pltpu.make_async_copy(
            gate_buf.at[slot], gate_pre_out.at[half, number], store.at[slot]
        )
        copy.start()
        pending[slot] = [copy]

    def up_body(at, half, number, slot):
        settle(slot)
        for place in rows_of(row_total, rows // 2):
            value = dot_nt(low_mid[place, :], weights[slot])
            up_buf[slot, place, columns] = value
            hidden[half, number, place, columns] = (
                gelu_parts(gate_buf[slot, place, columns])[0] * value
            ).astype(bf16)
        copy = pltpu.make_async_copy(
            up_buf.at[slot], up_pre_out.at[half, number], store.at[slot]
        )
        copy.start()
        pending[slot] = [copy]

    def down_body(at, half, number, slot):
        for place in rows_of(row_total, rows // 2):
            total[place, :] += dot_nn(hidden[half, number, place, columns], weights[slot])

    every = [(half, number) for half in range(2) for number in range(4)]
    cores_held = cores
    arrive(second)
    cores_held = cores_held + core_turn(gate_all, 1)
    stream(every[:4], gate_all, gate_body)
    arrive(first)
    up_cores = core_turn(up_all, 0)
    up_second = second_turn(up_all)
    arrive(cores_held)
    stream(every[4:], gate_all, gate_body)
    down_first = first_turn(down_all, plane_waits[2])
    settle(0)
    settle(1)
    arrive(up_second)
    up_cores = up_cores + core_turn(up_all, 1)
    stream(every[:4], up_all, up_body, gate_pre_out)
    arrive(down_first)
    down_cores = core_turn(down_all, 0)
    down_second = second_turn(down_all)
    arrive(up_cores)
    stream(every[4:], up_all, up_body, gate_pre_out)
    settle(0)
    settle(1)
    put(hidden, hidden_out)
    for at, copy in enumerate(flushed):
        if at not in (low_in_put, tokens_put) and copy is not flushed[-1]:
            copy.wait()
    arrive(down_cores)
    stream([(0, 0), (0, 2), (1, 0), (1, 2)], down_all, down_body)
    arrive(down_second)
    down_cores = core_turn(down_all, 1)
    stream([(0, 1), (0, 3)], down_all, down_body)
    arrive(down_cores)
    stream([(1, 1), (1, 3)], down_all, down_body)
    flushed[-1].wait()

    put(total, block_out)
    flushed[-1].wait()
    copies.finish()


def front(lengths, table, tokens, gains, delete, qkv, proj, out_grad, gate_t, up_t, down, block, sizes, count):
    seqs, rows, heads, inner = sizes
    total, model = seqs * rows, tokens.shape[1]
    small = jax.ShapeDtypeStruct((8, -(-gains.shape[1] // 128) * 128), f32)
    mixed = jax.ShapeDtypeStruct((block, model), bf16)
    planes = count // 4
    group = count // 4 * gate_t.shape[0]
    number = 5 * (planes - 1) + 8 + 3 * 8
    any_space = pl.BlockSpec(memory_space=pl.ANY)
    vmem = pl.BlockSpec(memory_space=pltpu.VMEM)
    shape = jax.ShapeDtypeStruct
    kept = [
        ((total, model), bf16),
        ((total, 3 * inner), bf16),
        ((total, 2 * inner), bf16),
        ((total, inner), bf16),
        ((seqs, heads // 2, 8, rows), f32),
        ((total, model), f32),
        ((total, model), bf16),
        ((8, model), f32),
        ((3 * inner, model), bf16),
        ((inner, model), bf16),
    ]
    return pl.pallas_call(
        functools.partial(front_kernel, count, qkv.shape[0]),
        in_specs=[pl.BlockSpec(memory_space=pltpu.SMEM)] * 2
        + [vmem] * 5
        + [any_space]
        + [vmem] * 3,
        out_specs=[any_space] * 20,
        out_shape=[shape((2, 4, group, model), bf16)] * 3
        + [shape(*at) for at in kept]
        + [shape((2, 4, total, max(rows, group)), f32)] * 2
        + [shape((2, 4, total, max(rows, group)), bf16), shape((total, model), f32)]
        + [shape((2 * heads, 2 * rows), f32)]
        + [shape((total, model), bf16)] * 2,
        scratch_shapes=[
            pltpu.VMEM(small.shape, f32),
            pltpu.VMEM(mixed.shape, bf16),
            pltpu.VMEM((2 * heads, 2 * rows), f32),
            pltpu.VMEM((planes, 2, 2) + small.shape, f32),
            pltpu.VMEM((planes, 2, 2, 2) + mixed.shape, bf16),
        ]
        + [pltpu.VMEM(*at) for at in kept]
        + [
            pltpu.VMEM((2, strip_rows, 4 * rows), f32),
            pltpu.VMEM((2 * rows, rows), bf16),
            pltpu.VMEM((2, group, model), bf16),
            pltpu.VMEM((2, total, max(rows, group)), f32),
            pltpu.VMEM((2, total, max(rows, group)), f32),
            pltpu.VMEM((2, 4, total, max(rows, group)), bf16),
            pltpu.SemaphoreType.DMA((number,)),
            pltpu.SemaphoreType.DMA((number,)),
            pltpu.SemaphoreType.DMA((5,)),
            pltpu.SemaphoreType.DMA((19,)),
            pltpu.SemaphoreType.DMA((2, 2)),
            pltpu.SemaphoreType.DMA((2,)),
            pltpu.SemaphoreType.DMA((seqs, 2)),
        ],
        compiler_params=pltpu.CompilerParams(
            collective_id=0, has_side_effects=True, vmem_limit_bytes=61 * 2**20
        ),
    )(lengths, table, tokens, gains, delete, qkv, proj, out_grad, gate_t, up_t, down)


def butterfly(count):
    return [0] + [1 << at for at in range(count.bit_length() - 1)]


def norm_slope(value, gain, grad):
    scale = lax.rsqrt(jnp.mean(value * value, axis=1, keepdims=True) + norm_eps)
    scaled = grad * gain
    drift = jnp.mean(value * scaled, axis=1, keepdims=True)
    return scale * scaled - value * (scale * scale * scale * drift), grad * value * scale


def attend_back_pair(
    valid_ref, seq, pair, projected, far, window, stat, grads, probs, slopes, low, strip_sum, halves,
    own_out, far_out, rows, inner,
):
    width = strip_rows // 2
    seq_rows = pl.ds(pl.multiple_of(seq * rows, rows), rows)
    first = strip_rows * pair
    queries = projected[seq_rows, lanes(first)]
    grad_rows = grads[seq_rows, lanes(first)]
    sources = ((projected, inner), (far, 0))
    outs = []
    for head in range(2):
        query = head_lanes(queries, head, width)
        grad = head_lanes(grad_rows, head, width)
        log_total = stat[seq, pair, pl.ds(head, 1), :]
        drift = jnp.zeros((8, rows), f32)
        for half, (source, base) in enumerate(sources):
            for at in range(0, rows, strip_rows):
                place = pl.ds(half * rows + at, strip_rows)
                to = pl.ds(pl.multiple_of(seq * rows + at, strip_rows), strip_rows)
                start = rows - strip_rows - at
                scores = dot_nt(source[to, lanes(base + first)], query) + window(head, half, start)
                row = at + lax.broadcasted_iota(jnp.int32, scores.shape, 0)
                scores = jnp.where(row < valid_keys(valid_ref, seq, half, rows), scores, masked_score)
                part = jnp.exp(scores - log_total)
                slope = dot_nt(source[to, lanes(base + inner + first)], grad)
                probs[place, :] = part
                slopes[place, :] = slope
                drift = drift + fold_rows(part * slope, jnp.sum)
        drift = jnp.sum(drift, axis=0, keepdims=True)
        for half in range(2):
            for at in range(0, rows, strip_rows):
                place = pl.ds(half * rows + at, strip_rows)
                to = pl.ds(pl.multiple_of(seq * rows + at, strip_rows), strip_rows)
                part = probs[place, :]
                grad_scores = (part * (slopes[place, :] - drift)).astype(bf16)
                low[place, :] = grad_scores
                start = 2 * half * rows + rows - strip_rows - at
                strip_sum[head, :, pl.ds(start, rows)] += grad_scores.astype(f32)
                terms = (dot_nn(grad_scores, query), dot_nn(part.astype(bf16), grad))
                for which, term in enumerate(terms):
                    if head == 0:
                        halves[which, place, :] = term
                    elif half == 0:
                        own_out[to, lanes(which * inner + first)] = halves[which, place, :] + term
                    else:
                        far_out[which, to, lanes(first)] = (
                            halves[which, place, :] + term
                        ).astype(bf16)
        keys = [source[seq_rows, lanes(base + first)] for source, base in sources]
        grad_query = dot_tn(keys[0], low[pl.ds(0, rows), :]) + dot_tn(
            keys[1], low[pl.ds(rows, rows), :]
        )
        outs.append(grad_query[head * width : (head + 1) * width, :])
    projected[seq_rows, lanes(first)] = jnp.concatenate(outs, axis=0).T.astype(bf16)


def back_kernel(
    count,
    qkv_rows,
    valid_ref,
    diag_ref,
    gate_grad_in,
    gains,
    stat,
    tokens_in,
    out_grad_in,
    block_in,
    after_in,
    low_in_in,
    low_mid_in,
    projected_in,
    far_in,
    mixed_in,
    qkv_in,
    proj_in,
    gate_all,
    up_all,
    down_all,
    gate_pre,
    up_pre,
    hidden_in,
    gate_values,
    tokens_out,
    mixed_sum,
    small_sum,
    gate_sum,
    up_sum,
    down_sum,
    core_land,
    one_land,
    two_land,
    last_land,
    kv_land,
    mixed_core,
    mixed_one,
    mixed_two,
    mixed_last,
    total,
    grad_ff,
    low_mid,
    weights,
    pre,
    hidden,
    slope_bufs,
    turned,
    sending,
    sums,
    kept,
    staging,
    halves,
    far,
    strip_sum,
    rowbuf,
    small,
    diag,
    gain_sums,
    gate_column,
    send,
    recv,
    fetch,
    stage,
    row_sem,
    park,
):
    planes = count // 4
    part = planes // 2
    row_total, model = total.shape
    seqs, pairs = stat.shape[:2]
    rows = row_total // seqs
    inner = proj_in.shape[0]
    group = gate_all.shape[2]
    piece = group // (2 * part)
    block = mixed_sum.shape[0]
    turns = ((1, 2), (2, 1))
    columns = pl.ds(0, group)
    greet(count)
    copies = Copies(count, send, recv)
    dp, ctx = copies.dp, copies.ctx
    used = [0]

    def load(source, target):
        copy = pltpu.make_async_copy(source, target, fetch.at[used[0]])
        used[0] += 1
        copy.start()
        return copy

    chunks = rows_of(row_total, rows // 2)
    block_loads = [load(block_in.at[chunk], total.at[chunk]) for chunk in chunks]
    grad_loads = [load(out_grad_in.at[chunk], weights.at[chunk]) for chunk in chunks]
    hidden_order = [(half, at) for pair in ((1, 3), (0, 2)) for half in (1, 0) for at in pair]

    def hidden_load(step):
        half, at = hidden_order[step]
        return load(hidden_in.at[half, at], hidden.at[step % 2])

    hidden_wait = hidden_load(0)
    low_mid_load = load(low_mid_in, low_mid)
    gain_sums[...] = jnp.zeros_like(gain_sums)
    for seq in range(seqs):
        wide = jnp.broadcast_to(gate_grad_in[pl.ds(seq, 1), :], (strip_rows, rows))
        gate_column[pl.ds(seq * rows, rows), :] = wide.T[:, :1]

    def out_norm(first):
        place = pl.ds(pl.multiple_of(first, fine_rows), fine_rows)
        value = total[place, :]
        gain = gains[pl.ds(2, 1), :]
        delete = gains[pl.ds(3, 1), :]
        scale = lax.rsqrt(jnp.mean(value * value, axis=1, keepdims=True) + norm_eps)
        low_out = (value * scale * gain).astype(bf16).astype(f32)
        logit = jnp.sum(low_out * delete, axis=1, keepdims=True)
        sigmoid = 1.0 / (1.0 + jnp.exp(-logit))
        grad_logit = (
            (gate_column[place, :] * delete_scale * sigmoid * (1.0 - sigmoid))
            .astype(bf16)
            .astype(f32)
        )
        gate_column[place, :] = delete_scale * sigmoid
        gain_sums[pl.ds(24, 8), :] += fold_rows(grad_logit * low_out, jnp.sum)
        slope, gain_part = norm_slope(value, gain, grad_logit * delete)
        grad = weights[place, :].astype(f32) + slope
        total[place, :] = grad
        grad_ff[place, :] = grad.astype(bf16)
        gain_sums[pl.ds(16, 8), :] += fold_rows(gain_part, jnp.sum)

    for at in range(len(chunks)):
        block_loads[at].wait()
        grad_loads[at].wait()

        @pl.loop(0, rows // 2 // fine_rows, unroll=fine_unroll)
        def _(step):
            out_norm(at * (rows // 2) + step * fine_rows)

    parked = pltpu.make_async_copy(total, tokens_out, park.at[0])
    parked.start()

    meet(count)

    outs = (down_sum, gate_sum, up_sum)
    high = ((0, 1), (0, 1), (2, 3))
    lows = ((4, 5), (6, 7), (4, 5))
    keep_at = (0, 1, 0)
    one, two, last = {}, {}, {}
    stage_slot = [0]

    def slot_rows(slot, size=group):
        return pl.ds(slot * group, size)

    def pull(source, size):
        slot = stage_slot[0] % 2
        stage_slot[0] += 1
        copy = pltpu.make_async_copy(source, staging.at[slot_rows(slot, size)], stage.at[slot])
        copy.start()
        return copy, slot * group

    def add_rows(target, base, other, other_base, size, out=None, out_base=0):
        step = 64 if size % 64 == 0 else 16
        into, into_base = (target, base) if out is None else (out, out_base)

        @pl.loop(0, size // step)
        def _(at):
            place = lambda first: pl.ds(pl.multiple_of(first + at * step, 16), step)
            into[place(into_base), :] = (
                target[place(base), :].astype(f32) + other[place(other_base), :].astype(f32)
            ).astype(bf16)

    def send_high(at, half):
        one[at, half] = copies.start(
            sums.at[slot_rows(high[at][half])], one_land.at[at, half], turns[half][0]
        )

    def after_one(at, halves=(0, 1)):
        waits = []
        for half in halves:
            one[at, half].wait_recv()
            waits.append((half,) + pull(one_land.at[at, half], group))
        for half, copy, base in waits:
            slot = lows[at][half]
            copy.wait()
            add_rows(sums, slot * group, staging, base, group)
            two[at, half] = copies.start(
                sums.at[pl.ds(slot * group + part * piece, part * piece)],
                two_land.at[at, half],
                turns[half][1],
            )

    def send_planes(source, base, size, target, bit, found):
        for plane in range(bit, planes, 2 * bit):
            found[plane] = copies.start(
                source.at[pl.ds(base + plane * size, size)],
                target.at[pl.ds((plane - 1) * size, size)],
                4 * bit,
            )

    def after_two(at):
        waits = []
        for half in range(2):
            two[at, half].wait_recv()
            waits.append(pull(two_land.at[at, half], part * piece))
        last[at] = {}
        if at == 2:
            for copy in last[0].values():
                copies.sent(copy)
        base_row = keep_at[at] * group
        for half, (copy, base) in enumerate(waits):
            copy.wait()
            add_rows(
                sums,
                lows[at][half] * group,
                staging,
                base,
                part * piece,
                kept,
                base_row + half * part * piece,
            )
        send_planes(kept, base_row, piece, last_land.at[at], 1, last[at])

    def after_planes(at):
        base_row = keep_at[at] * group
        bit = 1
        while 2 * bit < planes:
            for plane in range(bit, planes, 2 * bit):
                last[at][plane].wait_recv()
                copy, base = pull(last_land.at[at, pl.ds((plane - 1) * piece, piece)], piece)
                copy.wait()
                add_rows(kept, base_row + (plane - bit) * piece, staging, base, piece)
            bit = 2 * bit
            send_planes(kept, base_row, piece, last_land.at[at], bit, last[at])

    def after_last(at):
        plane = planes // 2
        last[at][plane].wait_recv()
        copy, base = pull(last_land.at[at, pl.ds((plane - 1) * piece, piece)], piece)
        copy.wait()
        outs[at][...] = kept[pl.ds(keep_at[at] * group, piece), :].astype(f32) + staging[
            pl.ds(base, piece), :
        ].astype(f32)

    arrived = {}

    def send_far(at, number, slot):
        arrived[at, number] = copies.start(
            sending.at[slot_rows(slot)], core_land.at[at, number], 0
        )
        return arrived[at, number]

    def own_slot(at, number):
        return (high if number % 2 else lows)[at][number // 2]

    def add_far(at, number, pulled, product):
        copy, base = pulled
        slot = own_slot(at, number)
        sums[slot_rows(slot), :] = product.astype(bf16)
        copy.wait()
        add_rows(sums, slot * group, staging, base, group)
        if number % 2:
            send_high(at, number // 2)

    thin = rowbuf.shape[2]

    def thin_rows(at):
        return pl.ds(pl.multiple_of(at * thin, thin), thin)

    def row_copies(sources, at, slot):
        return [
            pltpu.make_async_copy(source.at[thin_rows(at)], rowbuf.at[which, slot], row_sem.at[which, slot])
            for which, source in enumerate(sources)
        ]

    depth = rowbuf.shape[1]

    def row_ahead(sources):
        for at in range(depth - 1):
            for copy in row_copies(sources, at, at):
                copy.start()

    def row_stream(sources, body):
        steps = row_total // thin

        @pl.loop(0, steps)
        def _(at):
            slot = at % depth
            for copy in row_copies(sources, at, slot):
                copy.wait()

            @pl.when(at + depth - 1 < steps)
            def _():
                for copy in row_copies(sources, at + depth - 1, (at + depth - 1) % depth):
                    copy.start()

            body(thin_rows(at), slot, pl.ds(0, thin))

    last_send = {}
    for step, (half, number) in enumerate(hidden_order):
        following = hidden_load(step + 1) if step + 1 < len(hidden_order) else None
        hidden_wait.wait()
        turned[0] = hidden[step % 2].T
        if half:
            if step % 2 in last_send:
                copies.sent(last_send[step % 2])
            sending[slot_rows(step % 2), :] = dot_nn(turned[0, columns, :], grad_ff[...]).astype(bf16)
            last_send[step % 2] = send_far(0, number, step % 2)
        else:
            arrived[0, number].wait_recv()
            pulled = pull(core_land.at[0, number], group)
            add_far(0, number, pulled, dot_nn(turned[0, columns, :], grad_ff[...]))
        hidden_wait = following

    parked.wait()
    low_mid_load.wait()
    order = hidden_order
    down_slots, gate_slot, up_slot = (0, 1), 2, 3

    def down_load(step):
        half, number = order[step]
        return load(down_all.at[half, number], weights.at[slot_rows(down_slots[step % 2])])

    def pre_load(step):
        half, number = order[step]
        return [load(gate_pre.at[half, number], pre.at[0]), load(up_pre.at[half, number], pre.at[1])]

    def pair_load(step):
        half, number = order[step]
        return [
            load(gate_all.at[half, number], weights.at[slot_rows(gate_slot)]),
            load(up_all.at[half, number], weights.at[slot_rows(up_slot)]),
        ]

    tile = rows // tile_cut
    tiles = row_total // tile
    down_wait = down_load(0)
    pre_wait = pre_load(0)
    pair_wait = pair_load(0)
    for step, (half, number) in enumerate(order):
        following = down_load(step + 1) if step + 1 < len(order) else None
        down_wait.wait()
        for copy in pre_wait:
            copy.wait()
        down_rows = slot_rows(down_slots[step % 2])

        def hidden_tile(at):
            place = pl.ds(at * tile, tile) if isinstance(at, int) else pl.ds(pl.multiple_of(at * tile, tile), tile)
            grad_hidden = dot_nt(grad_ff[place, :], weights[down_rows, :])
            value, slope = gelu_parts(pre[0, place, columns])
            slope_bufs[0, place, columns] = (grad_hidden * pre[1, place, columns] * slope).astype(bf16)
            slope_bufs[1, place, columns] = (grad_hidden * value).astype(bf16)

        if ffn_unroll:
            for at in range(tiles):
                hidden_tile(at)
        else:
            pl.loop(0, tiles)(hidden_tile)

        if step == 2:
            after_one(0)
        if step == 4:
            after_two(0)
        down_wait = following
        pre_wait = pre_load(step + 1) if step + 1 < len(order) else ()
        pulled = []
        if not half:
            for at in (1, 2):
                arrived[at, number].wait_recv()
                pulled.append(pull(core_land.at[at, number], group))
        for which in range(2):
            turned[which] = slope_bufs[which].T
            at = 1 + which
            if half:
                if which in last_send:
                    copies.sent(last_send[which])
                sending[slot_rows(which), :] = dot_nn(
                    turned[which, columns, :], low_mid[...]
                ).astype(bf16)
                last_send[which] = send_far(at, number, which)
            else:
                if at == 1 and number % 2:
                    copies.sent(one[0, number // 2])
                if at == 2 and number % 2 == 0:
                    copies.sent(two[0, number // 2])
                add_far(at, number, pulled[which], dot_nn(turned[which, columns, :], low_mid[...]))
        for copy in pair_wait:
            copy.wait()

        def mid_tile(at):
            place = pl.ds(at * tile, tile) if isinstance(at, int) else pl.ds(pl.multiple_of(at * tile, tile), tile)
            term = dot_nn(slope_bufs[0, place, columns], weights[slot_rows(gate_slot), :]) + dot_nn(
                slope_bufs[1, place, columns], weights[slot_rows(up_slot), :]
            )
            total[place, :] = term if step == 0 else total[place, :] + term

        if mid_unroll:
            for at in range(tiles):
                mid_tile(at)
        else:
            pl.loop(0, tiles)(mid_tile)

        pair_wait = pair_load(step + 1) if step + 1 < len(order) else ()
        if step == 6:
            after_one(1, (0,))
        if step == 7:
            after_one(1, (1,))
            after_planes(0)

    row_ahead((after_in, tokens_out))

    qkv_place, proj_place = pl.ds(0, 3 * inner), pl.ds(3 * inner, inner)
    projected_place = pl.ds(4 * inner, row_total)
    qkv_load = load(qkv_in, weights.at[qkv_place])
    proj_load = load(proj_in, weights.at[proj_place])
    projected = weights.at[projected_place, pl.ds(0, 3 * inner)]
    projected_load = load(projected_in, projected)
    mixed = hidden.at[0, :, pl.ds(0, inner)]
    mixed_load = load(mixed_in, mixed)
    far_load = load(far_in, far)
    tokens_load = load(tokens_in, low_mid)
    def middle(place, slot, part):
        slope, gain_part = norm_slope(rowbuf[0, slot, part], gains[pl.ds(1, 1), :], total[place, :])
        grad = rowbuf[1, slot, part] + slope
        total[place, :] = grad
        grad_ff[place, :] = grad.astype(bf16)
        gain_sums[pl.ds(8, 8), :] += fold_rows(gain_part, jnp.sum)

    row_stream((after_in, tokens_out), middle)
    after_one(2)
    parked = pltpu.make_async_copy(total, tokens_out, park.at[0])
    parked.start()
    grads = slope_bufs.at[1, :, pl.ds(0, inner)]
    proj_load.wait()
    for place in rows_of(row_total, rows):
        grads[place, :] = dot_nt(grad_ff[place, :], weights[proj_place, :]).astype(bf16)
    mixed_load.wait()
    weights[proj_place, :] = dot_tn(mixed[...], grad_ff[...]).astype(bf16)
    low_in_load = load(low_in_in, grad_ff)
    after_last(0)
    projected_load.wait()
    far_load.wait()
    parked.wait()

    probs = total.at[:, pl.ds(2 * inner, rows)]
    slopes = pre.at[0, :, pl.ds(0, rows)]
    low = slope_bufs.at[0, :, pl.ds(0, rows)]
    for pair in range(pairs):
        for head in range(2):
            for half in range(2):
                strip = strip_of(diag_ref[pl.ds(4 * pair + 2 * head + half, 1), :], 2 * rows)
                for side in range(2):
                    pre[1, pl.ds((4 * head + 2 * half + side) * strip_rows, strip_rows), pl.ds(0, rows)] = (
                        strip[:, side * rows : (side + 1) * rows]
                    )

        def window(head, half, start):
            first = (4 * head + 2 * half) * strip_rows
            found = pre[1, pl.ds(first, strip_rows), pl.ds(start, rows - start)]
            if start:
                found = jnp.concatenate(
                    [found, pre[1, pl.ds(first + strip_rows, strip_rows), pl.ds(0, start)]], axis=1
                )
            return found

        strip_sum[...] = jnp.zeros_like(strip_sum)

        @pl.loop(0, seqs)
        def _(seq):
            attend_back_pair(
                valid_ref, seq, pair, projected, far, window, stat, grads, probs, slopes, low,
                strip_sum, halves, total, hidden, rows, inner,
            )

        span = 2 * rows
        for head in range(2):
            for half in range(2):
                skew = strip_sum[head, :, pl.ds(half * span, span)]
                row = lax.broadcasted_iota(jnp.int32, skew.shape, 0)
                step = 1
                while step < strip_rows:
                    skew = jnp.where(row & step != 0, pltpu.roll(skew, span - step, 1), skew)
                    step = 2 * step
                diag[pl.ds(2 * pair + head, 1), pl.ds(half * span, span)] = jnp.sum(
                    skew, axis=0, keepdims=True
                )
        if pair == 0:
            after_two(1)
        if pair == 1:
            after_two(2)
    after_planes(1)
    swap = [
        copies.start(hidden.at[which, :, pl.ds(0, inner)], kv_land.at[which], 0) for which in range(2)
    ]
    for which in range(2):
        swap[which].wait_recv()
    kv_loads = [
        load(kv_land.at[which], far.at[:, pl.ds(which * inner, inner)]) for which in range(2)
    ]
    for which in range(2):
        kv_loads[which].wait()
        for place in rows_of(row_total, rows):
            to = pl.ds(which * inner, inner)
            projected[place, pl.ds((which + 1) * inner, inner)] = (
                total[place, to] + far[place, to].astype(f32)
            ).astype(bf16)

    after_planes(2)

    low_in_load.wait()
    for at, half in ((1, 0), (1, 1), (2, 0), (2, 1)):
        copies.sent(one[at, half])
    out_size = inner // (2 * count)
    cut = row_total - inner
    total[pl.ds(cut, inner), :] = weights[proj_place, :].astype(f32)
    first_blocks = cut // qkv_rows
    for base, begin, end in ((0, 0, first_blocks), (3 * inner - cut, first_blocks, 2 * count)):
        for to in range(0, cut, cut // 2 // strip_rows * strip_rows):
            size = min(cut // 2 // strip_rows * strip_rows, cut - to)
            total[pl.ds(to, size), :] = dot_tn(projected[:, pl.ds(base + to, size)], grad_ff[...])
        for at in range(begin, end):
            rowbuf[0, 0, pl.ds(0, qkv_rows), :] = total[pl.ds(at * qkv_rows - base, qkv_rows), :]
            rowbuf[0, 0, pl.ds(qkv_rows, out_size), :] = total[pl.ds(cut + at * out_size, out_size), :]
            sums[pl.ds(at * block, block), :] = rowbuf[0, 0, pl.ds(0, block), :].astype(bf16)

    def piece_row(half, at, core):
        far_bit, near_bit, plane = at // (2 * part), at // part % 2, at % part
        bits = turns[half][0] * far_bit + turns[half][1] * near_bit + 4 * (half * part + plane)
        return pl.multiple_of((flip(dp, bits) * 2 + core) * block, 16)

    every = [(half, at) for half in range(2) for at in range(4 * part)]
    core_waits = [
        copies.start(
            sums.at[pl.ds(piece_row(half, at, 1 - ctx), block)],
            mixed_core.at[pl.ds(step * block, block)],
            0,
        )
        for step, (half, at) in enumerate(every)
    ]
    for at in (0, 1):
        copies.sent(last_send[at])
    for step, (half, at) in enumerate(every):
        sending[pl.ds(step * block, block), :] = sums[pl.ds(piece_row(half, at, ctx), block), :]
    for copy in core_waits:
        copy.wait_recv()
    span = 4 * part * block
    copy = pltpu.make_async_copy(mixed_core, staging.at[pl.ds(0, 2 * span)], stage.at[0])
    copy.start()
    copy.wait()
    add_rows(sending, 0, staging, 0, 2 * span)
    mixed_ones = [
        copies.start(
            sending.at[pl.ds(half * span + span // 2, span // 2)], mixed_one.at[half], turns[half][0]
        )
        for half in range(2)
    ]

    qkv_load.wait()

    @pl.loop(0, tiles)
    def _(at):
        place = pl.ds(pl.multiple_of(at * tile, tile), tile)
        total[place, :] = dot_nn(projected[place, :], weights[qkv_place, :])

    after_last(1)
    for half in range(2):
        mixed_ones[half].wait_recv()
    copies_in = [
        pltpu.make_async_copy(
            mixed_one.at[half], staging.at[pl.ds(half * span, span // 2)], stage.at[half]
        )
        for half in range(2)
    ]
    for copy in copies_in:
        copy.start()
    mixed_twos = []
    for half in range(2):
        copies_in[half].wait()
        add_rows(sending, half * span, staging, half * span, span // 2)
        mixed_twos.append(
            copies.start(
                sending.at[pl.ds(half * span + span // 4, span // 4)], mixed_two.at[half], turns[half][1]
            )
        )
    tokens_load.wait()

    def first_norm(place, slot, part):
        slope, gain_part = norm_slope(
            low_mid[place, :].astype(f32), gains[pl.ds(0, 1), :], total[place, :]
        )
        total[place, :] = rowbuf[0, slot, part] + slope
        gain_sums[pl.ds(0, 8), :] += fold_rows(gain_part, jnp.sum)

    row_ahead((tokens_out,))
    row_stream((tokens_out,), first_norm)
    parked = pltpu.make_async_copy(total, tokens_out, park.at[0])
    parked.start()
    for half in range(2):
        mixed_twos[half].wait_recv()
    copies_in = [
        pltpu.make_async_copy(
            mixed_two.at[half], staging.at[pl.ds(half * span, span // 4)], stage.at[half]
        )
        for half in range(2)
    ]
    for copy in copies_in:
        copy.start()
    for half in range(2):
        copies_in[half].wait()
        add_rows(sending, half * span, staging, half * span, span // 4)
    copies.sent(mixed_twos[0])
    quarter = span // 4
    for at in range(0, quarter, 16):
        sending[pl.ds(quarter + at, 16), :] = sending[pl.ds(span + at, 16), :]
    mixed_lasts = {}
    send_planes(sending, 0, block, mixed_last, 1, mixed_lasts)
    after_last(2)

    for seq in range(seqs):
        wide = jnp.broadcast_to(gate_column[pl.ds(seq * rows, rows), :], (rows, strip_rows))
        gate_values[pl.ds(seq, 1), :] = wide.T[:1, :]

    small[0] = jnp.zeros(small.shape[1:], f32)
    for at in range(4):
        small[0, pl.ds(at, 1), :] = jnp.sum(gain_sums[pl.ds(8 * at, 8), :], axis=0, keepdims=True)
    bucket = jnp.concatenate([diagonal_buckets(rows, half) for half in range(2)], axis=1)
    number = lax.broadcasted_iota(jnp.int32, (strip_rows, 4 * rows), 0)
    table = lax.dot_general(
        diag[...],
        (jnp.broadcast_to(bucket, number.shape) == number).astype(f32),
        (((1,), (1,)), ((), ())),
        precision=lax.Precision.HIGHEST,
        preferred_element_type=f32,
    )
    for at in range(2):
        small[0, pl.ds(4, 4), pl.ds(at * 128, 128)] = table[4 * at : 4 * at + 4, :]
    def small_round(step, bits):
        copy = copies.start(small.at[2 * step], small.at[2 * step + 1], bits)
        copy.wait_recv()
        small[2 * step + 2] = small[2 * step] + small[2 * step + 1]

    rounds = butterfly(count)
    for step in range(3):
        small_round(step, rounds[step])
    bit = 1
    while 2 * bit < planes:
        for plane in range(bit, planes, 2 * bit):
            mixed_lasts[plane].wait_recv()
            copy = pltpu.make_async_copy(
                mixed_last.at[pl.ds((plane - 1) * block, block)],
                staging.at[pl.ds(0, block)],
                stage.at[0],
            )
            copy.start()
            copy.wait()
            add_rows(sending, (plane - bit) * block, staging, 0, block)
        bit = 2 * bit
        send_planes(sending, 0, block, mixed_last, bit, mixed_lasts)
    for step in range(3, len(rounds)):
        small_round(step, rounds[step])
    small_sum[...] = small[2 * len(butterfly(count))]
    plane = planes // 2
    mixed_lasts[plane].wait_recv()
    copy = pltpu.make_async_copy(
        mixed_last.at[pl.ds((plane - 1) * block, block)], staging.at[pl.ds(0, block)], stage.at[0]
    )
    copy.start()
    copy.wait()
    mixed_sum[...] = sending[pl.ds(0, block), :].astype(f32) + staging[pl.ds(0, block), :].astype(f32)
    parked.wait()
    copies.finish()


def back(
    lengths, diagonal, gate_grad, gains, stat, arrays, qkv_rows, block, sizes, count
):
    seqs, rows, heads, inner = sizes
    total, model = arrays[1].shape
    planes = count // 4
    part = planes // 2
    group = arrays[-4].shape[2]
    piece = group // (2 * part)
    wide = max(rows, group)
    rounds = len(butterfly(count))
    number = 3 * (4 + 4 + planes - 1) + 2 + 8 * part + 4 + planes - 1 + rounds
    any_space = pl.BlockSpec(memory_space=pl.ANY)
    vmem = pl.BlockSpec(memory_space=pltpu.VMEM)
    shape = jax.ShapeDtypeStruct
    landing = [
        (3, 4, group, model),
        (3, 2, group, model),
        (3, 2, part * piece, model),
        (3, (planes - 1) * piece, model),
        (2, total, inner),
        (8 * part * block, model),
        (2, 2 * part * block, model),
        (2, part * block, model),
        ((planes - 1) * block, model),
    ]
    thin = row_thin
    return pl.pallas_call(
        functools.partial(back_kernel, count, qkv_rows),
        in_specs=[pl.BlockSpec(memory_space=pltpu.SMEM)] + [vmem] * 4 + [any_space] * len(arrays),
        out_specs=[vmem, any_space] + [vmem] * 5 + [any_space] * len(landing),
        out_shape=[
            shape((seqs, rows), f32),
            shape((total, model), f32),
            shape((block, model), f32),
            shape((8, model), f32),
            shape((piece, model), f32),
            shape((piece, model), f32),
            shape((piece, model), f32),
        ]
        + [shape(at, bf16) for at in landing],
        scratch_shapes=[
            pltpu.VMEM((total, model), f32),
            pltpu.VMEM((total, model), bf16),
            pltpu.VMEM((total, model), bf16),
            pltpu.VMEM((max(4 * inner + total, 4 * group), model), bf16),
            pltpu.VMEM((2, total, wide), f32),
            pltpu.VMEM((2, total, wide), bf16),
            pltpu.VMEM((2, total, wide), bf16),
            pltpu.VMEM((2, wide, total), bf16),
            pltpu.VMEM((2 * group, model), bf16),
            pltpu.VMEM((8 * group, model), bf16),
            pltpu.VMEM((2 * group, model), bf16),
            pltpu.VMEM((2 * group, model), bf16),
            pltpu.VMEM((2, 2 * rows, strip_rows), f32),
            pltpu.VMEM((total, 2 * inner), bf16),
            pltpu.VMEM((2, strip_rows, 4 * rows), f32),
            pltpu.VMEM((2, row_depth, thin, model), f32),
            pltpu.VMEM((2 * rounds + 1, 8, model), f32),
            pltpu.VMEM((8, 4 * rows), f32),
            pltpu.VMEM((32, model), f32),
            pltpu.VMEM((total, 1), f32),
            pltpu.SemaphoreType.DMA((number,)),
            pltpu.SemaphoreType.DMA((number,)),
            pltpu.SemaphoreType.DMA((80,)),
            pltpu.SemaphoreType.DMA((2,)),
            pltpu.SemaphoreType.DMA((2, row_depth)),
            pltpu.SemaphoreType.DMA((1,)),
        ],
        compiler_params=pltpu.CompilerParams(
            collective_id=1, has_side_effects=True, vmem_limit_bytes=63 * 2**20
        ),
    )(lengths, diagonal, gate_grad, gains, stat, *arrays)[:7]


def turn_kernel(first_in, second_in, first_out, second_out):
    first_out[0] = first_in[...].T
    second_out[0] = second_in[...].T


def turn(first, second, seqs):
    total, model = first.shape
    steps = total // seqs // strip_rows
    by_rows = pl.BlockSpec((strip_rows, model), lambda seq, at: (seq * steps + at, 0))
    by_lanes = pl.BlockSpec((1, model, strip_rows), lambda seq, at: (seq, 0, at))
    return pl.pallas_call(
        turn_kernel,
        grid=(seqs, steps),
        in_specs=[by_rows] * 2,
        out_specs=[by_lanes] * 2,
        out_shape=[jax.ShapeDtypeStruct((seqs, model, total // seqs), f32)] * 2,
        compiler_params=pltpu.CompilerParams(vmem_limit_bytes=60 * 2**20),
    )(first, second)


def per_device(
    tokens,
    lengths,
    qkv_weight,
    out_weight,
    gate_weight,
    up_weight,
    down_weight,
    norm_gains,
    delete_weight,
    bias_table,
    out_grad,
    gate_grad,
):
    seqs, rows, model = tokens.shape
    dp_count = lax.axis_size("dp")
    buckets, heads = bias_table.shape
    shard = model // dp_count
    qkv_rows, out_rows = qkv_weight.shape[1], out_weight.shape[0]
    inner = 2 * dp_count * out_rows
    block = -(-(qkv_rows + out_rows) // 16) * 16
    sizes = (seqs, rows, heads, inner)

    def padded(matrix):
        return jnp.pad(matrix, ((0, -matrix.shape[0] % 16), (0, 0)))

    (
        gate_all,
        up_all,
        down_all,
        low_in,
        projected,
        far_kv,
        mixed,
        stats,
        after_attn,
        low_mid,
        gains,
        qkv_t,
        out_full,
        gate_pre_all,
        up_pre_all,
        hidden_all,
        block_out,
        diagonal,
        out_grad_rows,
        token_rows,
    ) = front(
        lengths,
        bias_table,
        tokens.transpose(0, 2, 1),
        norm_gains,
        delete_weight.reshape(1, shard),
        qkv_weight.T,
        out_weight,
        out_grad.transpose(0, 2, 1),
        padded(gate_weight.T),
        padded(up_weight.T),
        padded(down_weight),
        block,
        sizes,
        dp_count,
    )
    gate_values, tokens_grad, mixed_sum, small_sum, gate_sum, up_sum, down_sum = back(
        lengths,
        diagonal,
        gate_grad,
        gains,
        stats,
        (
            token_rows,
            out_grad_rows,
            block_out,
            after_attn,
            low_in,
            low_mid,
            projected,
            far_kv,
            mixed,
            qkv_t,
            out_full,
            gate_all,
            up_all,
            down_all,
            gate_pre_all,
            up_pre_all,
            hidden_all,
        ),
        qkv_rows,
        block,
        sizes,
        dp_count,
    )
    anchor = lax.axis_index("dp") * shard
    ff_rows = down_weight.shape[0]
    table = jnp.concatenate([small_sum[4:8, :buckets], small_sum[4:8, 128 : 128 + buckets]])
    block_turned, tokens_turned = turn(block_out, tokens_grad, seqs)
    return (
        block_turned.transpose(0, 2, 1),
        gate_values,
        tokens_turned.transpose(0, 2, 1),
        mixed_sum[:qkv_rows].T,
        mixed_sum[qkv_rows : qkv_rows + out_rows],
        gate_sum[:ff_rows].T,
        up_sum[:ff_rows].T,
        down_sum[:ff_rows],
        lax.dynamic_slice_in_dim(small_sum[:3], anchor, shard, 1),
        lax.dynamic_slice_in_dim(small_sum[3], anchor, shard, 0),
        table[:heads].T,
    )


def solution(mesh):
    wide = P("dp", "ctx", None)
    columns = P(None, ("dp", "ctx"))
    depth = P(("dp", "ctx"), None)
    return jax.shard_map(
        per_device,
        mesh=mesh,
        in_specs=(
            wide,
            P("dp"),
            columns,
            depth,
            columns,
            columns,
            depth,
            P(None, "dp"),
            P("dp"),
            P(),
            wide,
            P("dp", "ctx"),
        ),
        out_specs=(
            wide,
            P("dp", "ctx"),
            wide,
            columns,
            depth,
            columns,
            columns,
            depth,
            P(None, "dp"),
            P("dp"),
            P(),
        ),
        check_vma=False,
    )
```
